512 devices in a mesh: group: 16 (over y, x), curve: 32 (over z, core).
Axes of the slice: x: 4, y: 4, z: 16, core: 2. Of those that a mesh axis runs over, the one named last changes fastest.
Arguments:
- rhs_old: float32 [3584, 24, 576], P(('group', 'curve')), may hold values from -3.1 to 3.1
- coef_old: float32 [3584, 24, 576], P(('group', 'curve')), may hold values from 0.03 to 10
- old_owner: int32 [16, 128], P('group'), may hold values from 0 to 31, as said below
- new_owner: int32 [16, 128], P('group'), may hold values from 0 to 31, as said below
- neighbours: int32 [16, 128, 4], P('group'), may hold values from -1 to 2047, as said below
- coarse_map: int32 [16, 128], P('group'), may hold values from 0 to 31, never falling along the last dimension, each value on 1 to 8 neighbouring positions
Outputs:
- pressure: float32 [2560, 24, 576], P(('group', 'curve'))
The draws below stay inside these ranges and needn't reach their ends.
Inputs may be any that keep to these rules, and one draw needn't show every extreme that they name: `new_owner`: never falls along the blocks; every device of a segment holds 3 to 5 blocks, and some device holds 5. `old_owner`: never falls along the blocks; every device held at least one block and at most 7, and some device held 7; each block's new owner differs from its old owner by at most one. `neighbours`: the relation is symmetric, low-x with high-x and low-y with high-y; a neighbour is at most 3 places from its block in the global block order. `coarse_map`: never falls along the blocks; every coarse cell holds 1 to 8 consecutive blocks.
All inputs are finite; a program needn't handle non-finite values.
Results may differ from the reference program's by a relative error of at most 0.0003.
Values sent between devices are 32-bit elements; how exact they have to be, the bound alone decides.
No kernel may reach another device: no remote copies, remote signals or barrier semaphores. Data moves between devices by JAX's collectives and lax.ppermute only.
A program may use at most 64 MiB of HBM per device.

```python
import math
import jax
import jax.numpy as jnp
import numpy as np
from jax import lax

BS = 24
MEAN_BLK = 4
SWEEPS = 2
SEG_MOST = 8
CAP_OLD = 7
CAP_NEW = 5
NBG = 128
NBLK = 2048
NCOARSE = 32
N_GROUP = 16
N_CURVE = 32


def owner_tables(key):
    base = jax.random.fold_in(key, 11)
    keys = jax.random.split(base, 4)
    pair_total = N_CURVE // 2
    swing = jax.random.randint(keys[0], (N_GROUP, pair_total), -1, 2)
    chosen = jax.random.randint(keys[1], (N_GROUP, 1), 1, pair_total)
    second = (chosen + jax.random.randint(keys[2], (N_GROUP, 1), 1, pair_total)) % pair_total
    pair_ids = jnp.arange(pair_total)[None, :]
    swing = jnp.where(pair_ids == chosen, 1, jnp.where(pair_ids == second, -1, swing))
    new_counts = jnp.stack([MEAN_BLK + swing, MEAN_BLK - swing], axis=2).reshape(N_GROUP, N_CURVE)
    new_starts = jnp.cumsum(new_counts, axis=1) - new_counts
    device_ids = jnp.arange(N_CURVE)[None, :]
    moved = jax.random.randint(keys[3], (N_GROUP, N_CURVE), -1, 2)
    heavy = 2 * chosen
    moved = jnp.where(device_ids == heavy, -1, jnp.where(device_ids == heavy + 1, 1, moved))
    moved = jnp.where(device_ids == 0, 0, moved)
    old_starts = new_starts + moved
    block_ids = jnp.arange(NBG)[None, None, :]
    new_table = jnp.sum(block_ids >= new_starts[:, :, None], axis=1) - 1
    old_table = jnp.sum(block_ids >= old_starts[:, :, None], axis=1) - 1
    return (new_table.astype(jnp.int32), old_table.astype(jnp.int32))


def draw_new_owner(key, part):
    return owner_tables(key)[0]


def draw_old_owner(key, part):
    return owner_tables(key)[1]


def draw_neighbours(key, part):
    column_total = NBLK // 2
    direction = jax.random.randint(jax.random.fold_in(key, 23), (column_total,), 0, 2)
    block_ids = jnp.arange(NBLK)
    column = block_ids // 2
    inner_pos = block_ids % 2
    height = jnp.where(direction[column] == 0, inner_pos, 1 - inner_pos)

    def block_at(column_at, height_at):
        clipped = jnp.clip(column_at, 0, column_total - 1)
        return 2 * clipped + jnp.where(direction[clipped] == 0, height_at, 1 - height_at)
    lower_x = jnp.where(column > 0, block_at(column - 1, height), -1)
    upper_x = jnp.where(column < column_total - 1, block_at(column + 1, height), -1)
    partner = 2 * column + 1 - inner_pos
    lower_y = jnp.where(height == 1, partner, -1)
    upper_y = jnp.where(height == 0, partner, -1)
    table = jnp.stack([lower_x, upper_x, lower_y, upper_y], axis=1)
    return table.reshape(N_GROUP, NBG, 4).astype(jnp.int32)


def spread_between(key, shape, lower, upper):
    return jnp.exp(jax.random.uniform(key, shape, jnp.float32, math.log(lower), math.log(upper)))


def draw_rhs_old(key, part):
    key = jax.random.fold_in(key, 31)
    keys = jax.random.split(key, 2)
    slot_total = N_GROUP * N_CURVE * CAP_OLD
    shape = (slot_total, BS, BS * BS)
    rough = jnp.clip(0.5 * jax.random.normal(keys[0], shape, jnp.float32), -3.0, 3.0)
    level = 0.012
    phase = jax.random.uniform(keys[1], (N_GROUP,), jnp.float32, 0.0, 2.0 * math.pi)
    slot_ids = jnp.arange(slot_total)
    segment_slots = N_CURVE * CAP_OLD
    position = (slot_ids % segment_slots).astype(jnp.float32) / segment_slots
    offset = level * (1.2 + jnp.sin(2.0 * math.pi * position + phase[slot_ids // segment_slots]))
    return rough + offset[:, None, None]


def draw_coef_old(key, part):
    key = jax.random.fold_in(key, 37)
    keys = jax.random.split(key, 2)
    shape = (N_GROUP * N_CURVE * CAP_OLD, BS, BS * BS)
    high = spread_between(keys[0], shape, 4.0, 10.0)
    low = spread_between(keys[1], shape, 0.03, 0.08)
    plane = jnp.arange(BS * BS)
    depth = plane % BS
    across = plane // BS
    rim = (depth < 2) | (depth >= BS - 2) | (across < 2) | (across >= BS - 2)
    return jnp.where(rim[None, None, :], low, high)


def split_up(number_of, total, most, skew):
    weights = [(1 << 20) // math.isqrt(standing ** skew) + 1 for standing in range(2, number_of + 1)]
    spare, counts = total - most - (number_of - 1), [1] * (number_of - 1)
    while spare > 0:
        candidates = [i for i in range(number_of - 1) if counts[i] < most]
        mass, budget = sum([weights[i] for i in candidates]), spare
        for i in candidates:
            extra = min(most - counts[i], max(1, budget * weights[i] // mass), spare)
            counts[i] = counts[i] + extra
            spare = spare - extra
    return np.array([most] + counts)


def uneven(rng, count, total, limit, slope):
    if count == 2:
        one = jax.random.randint(rng, (), max(1, total - limit), min(limit, total - 1) + 1)
        return jnp.stack([one, total - one])
    lengths = jnp.asarray(split_up(count, total, limit, slope), jnp.int32)
    twos = (count - 1) // 2
    giver, taker = lengths[1:1 + 2 * twos:2], lengths[2:2 + 2 * twos:2]
    slack = jnp.minimum(giver - 1, limit - taker)
    passed = jax.random.randint(jax.random.fold_in(rng, 1), (twos,), 0, 1 << 20) % (slack + 1)
    lengths = lengths.at[1:1 + 2 * twos:2].set(giver - passed).at[2:2 + 2 * twos:2].set(taker + passed)
    return lengths[jax.random.permutation(jax.random.fold_in(rng, 2), count)]


def setup_inputs(seed: int = 0) -> dict:
    key_list = jax.random.split(jax.random.key(seed), 7)
    rhs_old = draw_rhs_old(jax.random.fold_in(key_list[6], 71), 0)
    coef_old = draw_coef_old(jax.random.fold_in(key_list[6], 71), 0)
    old_owner = draw_old_owner(jax.random.fold_in(key_list[6], 71), 0)
    new_owner = draw_new_owner(jax.random.fold_in(key_list[6], 71), 0)
    neighbours = draw_neighbours(jax.random.fold_in(key_list[6], 71), 0)
    coarse_map = jax.vmap(lambda own: jnp.searchsorted(jnp.cumsum(uneven(own, NCOARSE, NBG, SEG_MOST, 1)), jnp.arange(NBG), side="right"))(jax.random.split(key_list[5], N_GROUP)).reshape((N_GROUP, NBG)).astype(jnp.int32)
    return {"rhs_old": rhs_old, "coef_old": coef_old, "old_owner": old_owner, "new_owner": new_owner, "neighbours": neighbours, "coarse_map": coarse_map}


OMEGA = 0.8
OPPOSITE = (1, 0, 3, 2)

def harmonic(left_side, right_side):
    return 2.0 * left_side * right_side / (left_side + right_side)

def block_faces(cell_field):
    block_count, side_cells, plane_cells = cell_field.shape
    lower_y = cell_field[:, :, :side_cells].reshape(block_count, plane_cells)
    upper_y = cell_field[:, :, plane_cells - side_cells:].reshape(block_count, plane_cells)
    return jnp.stack([cell_field[:, 0, :], cell_field[:, side_cells - 1, :], lower_y, upper_y], axis=1)

def depth_index(side_cells, plane_cells):
    return lax.broadcasted_iota(jnp.int32, (1, 1, plane_cells), 2) % side_cells

def conduct(coefficient, ghost_cells, factor):
    block_count, side_cells, plane_cells = coefficient.shape
    rows_padded = jnp.concatenate([ghost_cells[:, 0][:, None], coefficient, ghost_cells[:, 1][:, None]], axis=1)
    cond_rows = harmonic(rows_padded[:, :-1], rows_padded[:, 1:]) * factor
    cols_padded = jnp.concatenate([ghost_cells[:, 2].reshape(block_count, side_cells, side_cells), coefficient, ghost_cells[:, 3].reshape(block_count, side_cells, side_cells)], axis=2)
    cond_cols = harmonic(cols_padded[:, :, :-side_cells], cols_padded[:, :, side_cells:]) * factor
    depth_pos = depth_index(side_cells, plane_cells)
    below_cells = jnp.concatenate([coefficient[:, :, :1], coefficient[:, :, :-1]], axis=2)
    above_cells = jnp.concatenate([coefficient[:, :, 1:], coefficient[:, :, -1:]], axis=2)
    cond_below = harmonic(jnp.where(depth_pos == 0, coefficient, below_cells), coefficient) * factor
    cond_above = harmonic(coefficient, jnp.where(depth_pos == side_cells - 1, coefficient, above_cells)) * factor
    diagonal = cond_rows[:, :-1] + cond_rows[:, 1:] + cond_cols[:, :, :-side_cells] + cond_cols[:, :, side_cells:] + cond_below + cond_above
    return (cond_rows, cond_cols, cond_below, cond_above, diagonal)

def operate(cell_field, ghost_cells, cond):
    cond_rows, cond_cols, cond_below, cond_above, diagonal = cond
    block_count, side_cells, plane_cells = cell_field.shape
    rows_padded = jnp.concatenate([ghost_cells[:, 0][:, None], cell_field, ghost_cells[:, 1][:, None]], axis=1)
    flux_rows = cond_rows * (rows_padded[:, 1:] - rows_padded[:, :-1])
    cols_padded = jnp.concatenate([ghost_cells[:, 2].reshape(block_count, side_cells, side_cells), cell_field, ghost_cells[:, 3].reshape(block_count, side_cells, side_cells)], axis=2)
    flux_cols = cond_cols * (cols_padded[:, :, side_cells:] - cols_padded[:, :, :-side_cells])
    depth_pos = depth_index(side_cells, plane_cells)
    zero_column = jnp.zeros((block_count, side_cells, 1), jnp.float32)
    below_cells = jnp.where(depth_pos == 0, 0.0, jnp.concatenate([zero_column, cell_field[:, :, :-1]], axis=2))
    above_cells = jnp.where(depth_pos == side_cells - 1, 0.0, jnp.concatenate([cell_field[:, :, 1:], zero_column], axis=2))
    return flux_rows[:, :-1] - flux_rows[:, 1:] + (flux_cols[:, :, :-side_cells] - flux_cols[:, :, side_cells:]) + cond_below * (cell_field - below_cells) + cond_above * (cell_field - above_cells)

def coarsen(cell_field):
    block_count, side_cells, plane_cells = cell_field.shape
    half_cells = side_cells // 2
    grouped = cell_field.reshape(block_count, half_cells, 2, half_cells, 2, half_cells, 2)
    return grouped.mean(axis=(2, 4, 6)).reshape(block_count, half_cells, half_cells * half_cells)

def refine(cell_field):
    block_count, half_cells, plane_cells = cell_field.shape
    spread = jnp.broadcast_to(cell_field.reshape(block_count, half_cells, 1, half_cells, 1, half_cells, 1), (block_count, half_cells, 2, half_cells, 2, half_cells, 2))
    return spread.reshape(block_count, 2 * half_cells, 4 * half_cells * half_cells)

def block_totals(cond):
    cond_rows, cond_cols, cond_below, cond_above, diagonal = cond
    block_count, side_cells, plane_cells = cond_below.shape
    depth_pos = depth_index(side_cells, plane_cells)
    low_rows = jnp.sum(cond_rows[:, 0], axis=1)
    high_rows = jnp.sum(cond_rows[:, side_cells], axis=1)
    low_cols = jnp.sum(cond_cols[:, :, :side_cells], axis=(1, 2))
    high_cols = jnp.sum(cond_cols[:, :, plane_cells:], axis=(1, 2))
    outer_depth = jnp.sum(jnp.where(depth_pos == 0, cond_below, 0.0) + jnp.where(depth_pos == side_cells - 1, cond_above, 0.0), axis=(1, 2))
    surface_total = low_rows + high_rows + low_cols + high_cols + outer_depth
    return (surface_total, jnp.stack([low_rows, high_rows, low_cols, high_cols], axis=1))

def coarse_solve(surface_total, face_totals, residual_sums, inside, local_ids, cell_map, coarse_cells):
    block_count = surface_total.shape[0]
    slot_ids = jnp.arange(block_count, dtype=jnp.int32)
    link_table = (local_ids[:, :, None] == slot_ids[None, None, :]) & inside[:, :, None]
    matrix = jnp.diag(surface_total) - jnp.sum(jnp.where(link_table, face_totals[:, :, None], 0.0), axis=1)
    member = (cell_map[:, None] == jnp.arange(coarse_cells, dtype=jnp.int32)[None, :]).astype(jnp.float32)
    coarse = jnp.dot(member.T, jnp.dot(matrix, member, precision=lax.Precision.HIGHEST), precision=lax.Precision.HIGHEST)
    target = jnp.dot(member.T, residual_sums[:, None], precision=lax.Precision.HIGHEST)
    lower_factor = jnp.linalg.cholesky(coarse)
    middle = lax.linalg.triangular_solve(lower_factor, target, left_side=True, lower=True)
    solved = lax.linalg.triangular_solve(lower_factor, middle, left_side=True, lower=True, transpose_a=True)
    return solved[:, 0]

def ghost_faces(cell_field, neighbour_ids, own_fill):
    surface = block_faces(cell_field)
    clipped = jnp.maximum(neighbour_ids, 0)
    picked_faces = surface[clipped, jnp.array(OPPOSITE, dtype=jnp.int32)[None, :]]
    default = surface if own_fill else jnp.zeros_like(surface)
    return jnp.where((neighbour_ids >= 0)[:, :, None], picked_faces, default)

def jacobi_sweep(cell_field, target, cond, neighbour_ids):
    ghost_cells = ghost_faces(cell_field, neighbour_ids, False)
    return cell_field + OMEGA * (target - operate(cell_field, ghost_cells, cond)) / cond[4]

def reference(rhs_old, coef_old, old_owner, new_owner, neighbours, coarse_map):
    group_ids = jnp.arange(N_GROUP, dtype=jnp.int32)[:, None]
    block_ids = jnp.arange(NBG, dtype=jnp.int32)[None, :]
    old_start = jnp.sum(old_owner[:, None, :] < old_owner[:, :, None], axis=2).astype(jnp.int32)
    old_rows = ((group_ids * N_CURVE + old_owner) * CAP_OLD + block_ids - old_start).reshape(NBLK)
    source = rhs_old[old_rows]
    coefficient = coef_old[old_rows]
    neighbour_ids = neighbours.reshape(NBLK, 4)
    cond_fine = conduct(coefficient, ghost_faces(coefficient, neighbour_ids, True), 1.0)
    pressure = jnp.zeros_like(source)
    for repeat in range(SWEEPS):
        pressure = jacobi_sweep(pressure, source, cond_fine, neighbour_ids)
    residual = source - operate(pressure, ghost_faces(pressure, neighbour_ids, False), cond_fine)
    target = coarsen(residual)
    coef_level = coarsen(coefficient)
    cond_level = conduct(coef_level, ghost_faces(coef_level, neighbour_ids, True), 0.25)
    correction = jnp.zeros_like(target)
    for repeat in range(SWEEPS):
        correction = jacobi_sweep(correction, target, cond_level, neighbour_ids)
    residual_level = target - operate(correction, ghost_faces(correction, neighbour_ids, False), cond_level)
    surface_total, face_totals = block_totals(cond_level)
    residual_sums = jnp.sum(residual_level, axis=(1, 2))
    local_ids = neighbours - group_ids[:, :, None] * NBG
    inside = (neighbours >= 0) & (local_ids >= 0) & (local_ids < NBG)
    solver = jax.vmap(lambda total_row, face_row, sum_row, inside_row, local_row, map_row: coarse_solve(total_row, face_row, sum_row, inside_row, local_row, map_row, NCOARSE))
    answer = solver(surface_total.reshape(N_GROUP, NBG), face_totals.reshape(N_GROUP, NBG, 4), residual_sums.reshape(N_GROUP, NBG), inside, local_ids, coarse_map)
    per_block = jnp.take_along_axis(answer, coarse_map, axis=1).reshape(NBLK)
    correction = correction + per_block[:, None, None]
    for repeat in range(SWEEPS):
        correction = jacobi_sweep(correction, target, cond_level, neighbour_ids)
    pressure = pressure + refine(correction)
    for repeat in range(SWEEPS):
        pressure = jacobi_sweep(pressure, source, cond_fine, neighbour_ids)
    new_start = jnp.sum(new_owner[:, None, :] < new_owner[:, :, None], axis=2).astype(jnp.int32)
    new_rows = ((group_ids * N_CURVE + new_owner) * CAP_NEW + block_ids - new_start).reshape(NBLK)
    output = jnp.zeros((N_GROUP * N_CURVE * CAP_NEW, BS, BS * BS), jnp.float32)
    return output.at[new_rows].set(pressure)
```

```python
import jax
import jax.numpy as jnp
from jax import lax
from jax.experimental import pallas as pl
from jax.experimental.pallas import tpu as pltpu
from jax.sharding import PartitionSpec as P

OMEGA = 0.8
KEEP = 1.0 - OMEGA
CAP_OLD = 7
CAP_NEW = 5
REACH = 3
NBG = 128
NCOARSE = 32
AXES = ("group", "curve")
F32 = jnp.float32
I32 = jnp.int32

HELD, PICK, TABLE, CELL, BAND = 0, 1, 8, 32, 40
ABSENT = 2 * REACH + CAP_NEW


class Level:
    def __init__(self, side, rows, width, high_at, x_low, x_high, face_rows, factor):
        self.side, self.rows, self.width = side, rows, width
        self.last = side * side - side - (width - 128)
        self.high_at = high_at
        self.x_low, self.x_high, self.face_rows = x_low, x_high, face_rows
        self.tiles = width // 128
        self.factor = factor


FINE = Level(24, 24, 640, 40, 24, 32, 40, 1.0)
COARSE = Level(12, 16, 256, 68, 16, 20, 24, 0.25)
BOTH_ROWS = FINE.face_rows + COARSE.face_rows


def iota(shape, axis):
    return lax.broadcasted_iota(I32, shape, axis)


def over(value, side):
    return (value * 43691) >> (20 if side == 24 else 19)


def pack_faces(lev, field, faces, k, base):
    lane = iota((lev.rows, 128), 1)
    tail = field[:, lev.width - 128 :]
    move = lev.high_at - lev.last
    if move:
        tail = pltpu.roll(tail, move, 1)
    faces[k, base : base + lev.rows, :] = jnp.where(lane < lev.side, field[:, :128], tail)
    for j in range(lev.tiles):
        part = slice(128 * j, 128 * j + 128)
        low, high = base + lev.x_low + j, base + lev.x_high + j
        faces[k, low : low + 1, :] = field[0:1, part]
        faces[k, high : high + 1, :] = field[lev.side - 1 : lev.side, part]


def send_faces(info, faces, ahead, back):
    first = jnp.maximum(info[HELD] - REACH, 0)
    for j in range(REACH):
        ahead[j] = faces[first + j]
        back[j] = faces[j]


def fill_table(table, before, faces, after):
    table[0:REACH] = before[...]
    table[REACH : REACH + CAP_NEW] = faces[...]
    table[REACH + CAP_NEW : ABSENT] = after[...]
    table[ABSENT] = jnp.zeros(table.shape[1:], F32)


def ghosts_of(lev, info, table, k, base):
    row = [info[TABLE + 4 * k + f] for f in range(4)]
    x_low = jnp.concatenate(
        [table[row[0], pl.ds(base + lev.x_high + j, 1), :] for j in range(lev.tiles)], axis=1
    )
    x_high = jnp.concatenate(
        [table[row[1], pl.ds(base + lev.x_low + j, 1), :] for j in range(lev.tiles)], axis=1
    )
    y_low = pltpu.roll(table[row[2], pl.ds(base, lev.rows), :], 128 - lev.high_at, 1)
    y_high = pltpu.roll(table[row[3], pl.ds(base, lev.rows), :], lev.last, 1)
    return row, x_low, x_high, y_low, y_high


def neighbour_sum(lev, field, g, ghosts):
    _, x_low, x_high, y_low, y_high = ghosts
    rows, width, side = lev.rows, lev.width, lev.side
    row = iota((rows, width), 0)
    lane = iota((rows, 128), 1)
    total = g[0] * pltpu.roll(field, 1, 1) + g[1] * pltpu.roll(field, width - 1, 1)
    total += g[2] * pltpu.roll(field, side, 1) + g[3] * pltpu.roll(field, width - side, 1)
    total += g[4] * jnp.where(row == 0, x_low, pltpu.roll(field, 1, 0))
    total += g[5] * jnp.where(row == side - 1, x_high, pltpu.roll(field, rows - 1, 0))
    low = jnp.where(lane < side, g[2][:, :128] * y_low, 0.0)
    on_high = (lane >= lev.last) & (lane < lev.last + side)
    high = jnp.where(on_high, g[3][:, width - 128 :] * y_high, 0.0)
    parts = [low, high]
    if width > 256:
        parts = [low, jnp.zeros((rows, width - 256), F32), high]
    return total + jnp.concatenate(parts, axis=1)


def conductances(lev, cell, ghosts):
    present, x_low, x_high, y_low, y_high = ghosts
    present = [p != ABSENT for p in present]
    rows, width, side = lev.rows, lev.width, lev.side
    row, lane = iota((rows, width), 0), iota((rows, width), 1)
    depth = lane - side * over(lane, side)
    last = side - 1
    end = side * side
    x_low = jnp.where(present[0], x_low, cell[0:1, :])
    x_high = jnp.where(present[1], x_high, cell[last : last + 1, :])
    y_low = jnp.where(present[2], y_low, cell[:, :128])
    y_high = jnp.where(present[3], y_high, cell[:, width - 128 :])
    spare = jnp.ones((rows, width - 128), F32)
    y_low = jnp.concatenate([y_low, spare], axis=1)
    y_high = jnp.concatenate([spare, y_high], axis=1)
    high_y = (lane >= end - side) & (lane < end)
    across = [
        jnp.where(depth == 0, cell, pltpu.roll(cell, 1, 1)),
        jnp.where(depth == last, cell, pltpu.roll(cell, width - 1, 1)),
        jnp.where(lane < side, y_low, pltpu.roll(cell, side, 1)),
        jnp.where(high_y, y_high, pltpu.roll(cell, width - side, 1)),
        jnp.where(row == 0, x_low, pltpu.roll(cell, 1, 0)),
        jnp.where(row == last, x_high, pltpu.roll(cell, rows - 1, 0)),
    ]
    q = [2.0 * cell * other / (cell + other) * lev.factor for other in across]
    diagonal = q[0] + q[1] + q[2] + q[3] + q[4] + q[5]
    inside = (lane < end) & (row < side)
    weight = jnp.where(inside, OMEGA / diagonal, 0.0)
    g = [weight * one for one in q]
    g[0] = jnp.where(depth == 0, 0.0, g[0])
    g[1] = jnp.where(depth == last, 0.0, g[1])
    masks = (row, lane, depth, inside, high_y)
    return q, g, weight, diagonal, masks


def both_totals(values):
    return jnp.sum(jnp.sum(values, axis=0, keepdims=True), axis=1, keepdims=True)


def spread_matrix():
    lane = iota((1, FINE.width), 1)
    y = over(lane, 24)
    group = 12 * (y >> 1) + ((lane - 24 * y) >> 1)
    group = jnp.where(lane < 576, group, -1)
    return (iota((COARSE.width, FINE.width), 0) == group).astype(F32).astype(jnp.bfloat16)


def split_three(values):
    high = values.astype(jnp.bfloat16)
    rest = values - high.astype(F32)
    mid = rest.astype(jnp.bfloat16)
    low = (rest - mid.astype(F32)).astype(jnp.bfloat16)
    return high, mid, low


def coarsen_blocks(fine, scratch):
    spread = spread_matrix()
    total = None
    for part in split_three(fine):
        one = lax.dot_general(
            part, spread, (((1,), (1,)), ((), ())), preferred_element_type=F32
        )
        total = one if total is None else total + one
    scratch[0] = total[:, :128]
    scratch[1] = total[:, 128:]


def coarse_rows(scratch, k):
    even, odd = pl.ds(24 * k, 12, stride=2), pl.ds(24 * k + 1, 12, stride=2)
    halves = [scratch[t, even, :] + scratch[t, odd, :] for t in range(2)]
    return 0.125 * jnp.concatenate(halves, axis=1)


def first_kernel(new_ref, old_ref, near_ref, map_ref, rhs_ref, coef_ref, ahead, back, info):
    curve = lax.axis_index("curve")
    group = lax.axis_index("group")
    new, old = new_ref[...], old_ref[...]

    def count(mask):
        return jnp.sum(jnp.where(mask, 1.0, 0.0)).astype(I32)

    new_first, held = count(new < curve), count(new == curve)
    old_first, old_count = count(old < curve), count(old == curve)
    last = jnp.clip(old_count - 1, 0, CAP_OLD - 1)
    ahead[0] = rhs_ref[last]
    ahead[1] = coef_ref[last]
    back[0] = rhs_ref[0]
    back[1] = coef_ref[0]
    info[HELD] = held
    first_id = group * NBG + new_first
    finish = first_id + held
    for k in range(CAP_NEW):
        block = new_first + k
        pick = jnp.where(block >= old_first + old_count, CAP_OLD + 1, 1 + block - old_first)
        pick = jnp.where(block < old_first, 0, pick)
        info[PICK + k] = jnp.clip(pick, 0, CAP_OLD + 1)
        occupied = k < held
        safe = jnp.clip(block, 0, NBG - 1)
        cell = map_ref[0, safe]
        info[CELL + k] = jnp.where(occupied, cell, -1)
        for f in range(4):
            near = near_ref[f, safe]
            present = occupied & (near >= 0)
            slot = jnp.where(near >= finish, REACH + CAP_NEW - finish, REACH - first_id) + near
            slot = jnp.clip(slot, 0, ABSENT - 1)
            info[TABLE + 4 * k + f] = jnp.where(present, slot, ABSENT)
            local = near - group * NBG
            inside = present & (local >= 0) & (local < NBG)
            other = map_ref[0, jnp.clip(local, 0, NBG - 1)]
            info[BAND + 4 * k + f] = jnp.where(inside, 8 * k + 3 + other - cell, -1)


def gather_kernel(
    info, rhs_ref, coef_ref, before, after, source, coef, faces, ahead, back, level, scratch
):
    source[...] = jnp.zeros(source.shape, F32)
    coef[...] = jnp.ones(coef.shape, F32)
    for k in range(CAP_NEW):
        pick = info[PICK + k]
        slot = jnp.clip(pick - 1, 0, CAP_OLD - 1)
        occupied = k < info[HELD]
        for i, (table, out, rest) in enumerate(((rhs_ref, source, 0.0), (coef_ref, coef, 1.0))):
            block = jnp.where(pick == 0, before[i], table[slot])
            block = jnp.where(pick == CAP_OLD + 1, after[i], block)
            out[k, :, 0:576] = jnp.where(occupied, block, rest)
    coarsen_blocks(coef[...].reshape(CAP_NEW * 24, FINE.width), scratch)
    row, lane = iota((16, 256), 0), iota((16, 256), 1)
    for k in range(CAP_NEW):
        pack_faces(FINE, coef[k], faces, k, 0)
        level[k] = jnp.ones((16, 256), F32)
        level[k, 0:12, :] = coarse_rows(scratch, k)
        level[k] = jnp.where((row < 12) & (lane < 144), level[k], 1.0)
        pack_faces(COARSE, level[k], faces, k, FINE.face_rows)
    send_faces(info, faces, ahead, back)


def conduct_kernel(
    info, source, coef, level, faces_in, before, after,
    fine_g, fine_s, fine_d, coarse_g, coarse_w, coarse_d, row_out, u, faces, ahead, back, table,
):
    fill_table(table, before, faces_in, after)
    lane_row = iota((1, 128), 1)
    band = jnp.zeros((1, 128), F32)
    for k in range(CAP_NEW):
        ghosts = ghosts_of(FINE, info, table, k, 0)
        _, g, weight, diagonal, _ = conductances(FINE, coef[k], ghosts)
        for i in range(6):
            fine_g[k, i] = g[i]
        fine_d[k] = (1.0 / OMEGA) * diagonal
        start = weight * source[k]
        fine_s[k] = start
        u[k] = start
        pack_faces(FINE, start, faces, k, 0)

        ghosts = ghosts_of(COARSE, info, table, k, FINE.face_rows)
        q, g, weight, diagonal, masks = conductances(COARSE, level[k], ghosts)
        row, lane, depth, inside, high_y = masks
        for i in range(6):
            coarse_g[k, i] = g[i]
        coarse_w[k] = weight
        coarse_d[k] = (1.0 / OMEGA) * diagonal
        face = [
            both_totals(jnp.where(inside & (row == 0), q[4], 0.0)),
            both_totals(jnp.where(inside & (row == 11), q[5], 0.0)),
            both_totals(jnp.where(inside & (lane < 12), q[2], 0.0)),
            both_totals(jnp.where(inside & high_y, q[3], 0.0)),
        ]
        ends = jnp.where(inside & (depth == 0), q[0], 0.0)
        ends += jnp.where(inside & (depth == 11), q[1], 0.0)
        surface = face[0] + face[1] + face[2] + face[3] + both_totals(ends)
        occupied = k < info[HELD]
        band += jnp.where((lane_row == 8 * k + 3) & occupied, surface, 0.0)
        for f in range(4):
            band -= jnp.where(lane_row == info[BAND + 4 * k + f], face[f], 0.0)
        band += jnp.where(lane_row == 64 + k, info[CELL + k].astype(F32), 0.0)
    row_out[...] = band
    send_faces(info, faces, ahead, back)


def sweep_kernel(lev, info, u_in, g, start, faces_in, before, after, u, faces, ahead, back, table):
    fill_table(table, before, faces_in, after)
    for k in range(CAP_NEW):
        field = u_in[k]
        ghosts = ghosts_of(lev, info, table, k, 0)
        new = KEEP * field + (start[k] + neighbour_sum(lev, field, g.at[k], ghosts))
        u[k] = new
        pack_faces(lev, new, faces, k, 0)
    send_faces(info, faces, ahead, back)


def residual_kernel(
    info, u_in, g, start, diagonal, weight, faces_in, before, after,
    coarse_s, faces, ahead, back, table, rest, scratch,
):
    fill_table(table, before, faces_in, after)
    for k in range(CAP_NEW):
        field = u_in[k]
        ghosts = ghosts_of(FINE, info, table, k, 0)
        inner = start[k] + neighbour_sum(FINE, field, g.at[k], ghosts)
        rest[k] = diagonal[k] * (inner - OMEGA * field)
    coarsen_blocks(rest[...].reshape(CAP_NEW * 24, FINE.width), scratch)
    for k in range(CAP_NEW):
        coarse_s[k] = jnp.zeros((16, 256), F32)
        coarse_s[k, 0:12, :] = weight[k, 0:12, :] * coarse_rows(scratch, k)
        pack_faces(COARSE, coarse_s[k], faces, k, 0)
    send_faces(info, faces, ahead, back)


def total_kernel(info, u_in, g, start, diagonal, row_in, faces_in, before, after, rows_out, table):
    fill_table(table, before, faces_in, after)
    lane_row = iota((1, 128), 1)
    row, lane = iota((16, 256), 0), iota((16, 256), 1)
    inside = (row < 12) & (lane < 144)
    band = row_in[...]
    for k in range(CAP_NEW):
        field = u_in[k]
        ghosts = ghosts_of(COARSE, info, table, k, 0)
        inner = start[k] + neighbour_sum(COARSE, field, g.at[k], ghosts)
        rest = jnp.where(inside, diagonal[k] * (inner - OMEGA * field), 0.0)
        occupied = k < info[HELD]
        band += jnp.where((lane_row == 8 * k + 7) & occupied, both_totals(rest), 0.0)
    rows_out[...] = jnp.broadcast_to(band, rows_out.shape)


def solve_kernel(info, rows_in, u_in, u, faces, ahead, back):
    rows = rows_in[...]
    shape = (NCOARSE, 128)
    row, lane = iota(shape, 0), iota(shape, 1)
    cells = iota((NCOARSE, NCOARSE), 1).astype(F32)
    band = jnp.zeros(shape, F32)
    for k in range(CAP_NEW):
        member = (rows[:, 64 + k : 65 + k] == cells).astype(F32)
        part = rows if k == 0 else pltpu.roll(rows, 128 - 8 * k, 1)
        part = jnp.where(lane < 8, part, 0.0)
        band += lax.dot_general(
            member, part, (((0,), (0,)), ((), ())),
            precision=lax.Precision.HIGHEST, preferred_element_type=F32,
        )
    matrix = jnp.where(lane == 64, band[:, 7:8], 0.0)
    for o in range(7):
        matrix += jnp.where(lane == row + (o - REACH), band[:, o : o + 1], 0.0)

    def drop(current, j):
        pivot = current[j : j + 1, :]
        share = current[:, j : j + 1] / pivot[:, j : j + 1]
        return jnp.where(iota((NCOARSE, 1), 0) == j, 0.0, share) * pivot

    apart = (NCOARSE - REACH - 1) // 2
    for j in range(apart):
        matrix = matrix - (drop(matrix, j) + drop(matrix, NCOARSE - 1 - j))
    for j in range(apart, NCOARSE - apart):
        matrix = matrix - drop(matrix, j)
    pivots = jnp.sum(jnp.where(lane == row, matrix, 0.0), axis=1, keepdims=True)
    answer = matrix[:, 64:65] / pivots
    at = iota((NCOARSE, 1), 0)
    row, lane = iota((16, 256), 0), iota((16, 256), 1)
    inside = (row < 12) & (lane < 144)
    for k in range(CAP_NEW):
        lift = jnp.sum(jnp.where(at == info[CELL + k], answer, 0.0), axis=0, keepdims=True)
        new = u_in[k] + jnp.where(inside, lift, 0.0)
        u[k] = new
        pack_faces(COARSE, new, faces, k, 0)
    send_faces(info, faces, ahead, back)


def refine_kernel(
    info, e_in, g, start, faces_in, before, after, u_in, u, faces, ahead, back, table, coarse, rest
):
    fill_table(table, before, faces_in, after)
    for k in range(CAP_NEW):
        field = e_in[k]
        ghosts = ghosts_of(COARSE, info, table, k, 0)
        coarse[k] = KEEP * field + (start[k] + neighbour_sum(COARSE, field, g.at[k], ghosts))
    spread = spread_matrix()
    total = None
    for part in split_three(coarse[...].reshape(CAP_NEW * 16, 256)):
        one = jnp.dot(part, spread, preferred_element_type=F32)
        total = one if total is None else total + one
    for k in range(CAP_NEW):
        twelve = total[16 * k : 16 * k + 12, :]
        for t in range(FINE.tiles):
            part = slice(128 * t, 128 * t + 128)
            rest[t, pl.ds(0, 12, stride=2), :] = twelve[:, part]
            rest[t, pl.ds(1, 12, stride=2), :] = twelve[:, part]
        new = u_in[k] + jnp.concatenate([rest[t] for t in range(FINE.tiles)], axis=1)
        u[k] = new
        pack_faces(FINE, new, faces, k, 0)
    send_faces(info, faces, ahead, back)


def last_kernel(info, u_in, g, start, faces_in, before, after, out, table):
    fill_table(table, before, faces_in, after)
    for k in range(CAP_NEW):
        field = u_in[k]
        ghosts = ghosts_of(FINE, info, table, k, 0)
        new = KEEP * field + (start[k] + neighbour_sum(FINE, field, g.at[k], ghosts))
        out[k] = jnp.where(k < info[HELD], new[:, 0:576], 0.0)


def sds(*shape):
    return jax.ShapeDtypeStruct(shape, F32)


SMEM = pl.BlockSpec(memory_space=pltpu.SMEM)
VMEM = pl.BlockSpec(memory_space=pltpu.VMEM)


def call(kernel, name, outs, scratch, args, in_specs=None, out_specs=None):
    many = len(outs) > 1
    return pl.pallas_call(
        kernel,
        out_shape=outs if many else outs[0],
        in_specs=in_specs or [SMEM] + [VMEM] * (len(args) - 1),
        out_specs=out_specs or ([VMEM] * len(outs) if many else VMEM),
        scratch_shapes=[pltpu.VMEM(s, F32) for s in scratch],
        compiler_params=pltpu.CompilerParams(vmem_limit_bytes=24 * 1024 * 1024),
        name=name,
    )(*args)


def shifted(block, axis, distance):
    devices = range(lax.axis_size(axis))
    route = [(i - distance, i) for i in devices if i - distance in devices]
    return lax.ppermute(block, axis, route)


def exchange(ahead, back):
    return shifted(ahead, AXES, 1), shifted(back, AXES, -1)


def face_outs(rows):
    return [sds(CAP_NEW, rows, 128), sds(REACH, rows, 128), sds(REACH, rows, 128)]


def body(rhs_old, coef_old, old_owner, new_owner, neighbours, coarse_map):
    near = jnp.transpose(neighbours[0])
    pair = sds(2, 24, 576)
    ahead, back, info = call(
        first_kernel, "owners",
        [pair, pair, jax.ShapeDtypeStruct((128,), I32)], [],
        (new_owner, old_owner, near, coarse_map, rhs_old, coef_old),
        [VMEM, VMEM, SMEM, SMEM, VMEM, VMEM], [VMEM, VMEM, SMEM],
    )
    before, after = shifted(ahead, "curve", 1), shifted(back, "curve", -1)

    fine = sds(CAP_NEW, 24, FINE.width)
    coarse = sds(CAP_NEW, 16, 256)
    fine_table = [(ABSENT + 1, FINE.face_rows, 128)]
    coarse_table = [(ABSENT + 1, COARSE.face_rows, 128)]
    fine_faces, coarse_faces = face_outs(FINE.face_rows), face_outs(COARSE.face_rows)
    sums = (2, CAP_NEW * 24, 128)

    source, coef, faces, ahead, back, level = call(
        gather_kernel, "collect", [fine, fine] + face_outs(BOTH_ROWS) + [coarse], [sums],
        (info, rhs_old, coef_old, before, after),
    )
    before, after = exchange(ahead, back)
    fine_g, fine_s, fine_d, coarse_g, coarse_w, coarse_d, row, u, faces, ahead, back = call(
        conduct_kernel, "conduct",
        [sds(CAP_NEW, 6, 24, FINE.width), fine, fine, sds(CAP_NEW, 6, 16, 256), coarse, coarse,
         sds(1, 128), fine] + fine_faces,
        [(ABSENT + 1, BOTH_ROWS, 128)],
        (info, source, coef, level, faces, before, after),
    )

    def sweep(lev, u, g, start, faces, ahead, back, name):
        before, after = exchange(ahead, back)
        return call(
            lambda *refs: sweep_kernel(lev, *refs), name,
            [fine, *fine_faces] if lev is FINE else [coarse, *coarse_faces],
            fine_table if lev is FINE else coarse_table,
            (info, u, g, start, faces, before, after),
        )

    u0, faces, ahead, back = sweep(FINE, u, fine_g, fine_s, faces, ahead, back, "pre")
    before, after = exchange(ahead, back)
    coarse_s, faces, ahead, back = call(
        residual_kernel, "residual", [coarse, *coarse_faces],
        fine_table + [(CAP_NEW, 24, FINE.width), sums],
        (info, u0, fine_g, fine_s, fine_d, coarse_w, faces, before, after),
    )
    e, faces, ahead, back = sweep(
        COARSE, coarse_s, coarse_g, coarse_s, faces, ahead, back, "coarse_pre"
    )
    before, after = exchange(ahead, back)
    rows = call(
        total_kernel, "totals", [sds(NCOARSE, 128)], coarse_table,
        (info, e, coarse_g, coarse_s, coarse_d, row, faces, before, after),
    )
    rows = lax.all_to_all(rows, "curve", 0, 0, tiled=True)
    e, faces, ahead, back = call(
        solve_kernel, "solve", [coarse, *coarse_faces], [], (info, rows, e)
    )
    e, faces, ahead, back = sweep(COARSE, e, coarse_g, coarse_s, faces, ahead, back, "coarse_post")
    before, after = exchange(ahead, back)
    u, faces, ahead, back = call(
        refine_kernel, "refine", [fine, *fine_faces],
        coarse_table + [(CAP_NEW, 16, 256), (FINE.tiles, 24, 128)],
        (info, e, coarse_g, coarse_s, faces, before, after, u0),
    )
    u, faces, ahead, back = sweep(FINE, u, fine_g, fine_s, faces, ahead, back, "post")
    before, after = exchange(ahead, back)
    return call(
        last_kernel, "last", [sds(CAP_NEW, 24, 576)], fine_table,
        (info, u, fine_g, fine_s, faces, before, after),
    )


def solution(mesh):
    in_specs = (
        P(("group", "curve"), None, None),
        P(("group", "curve"), None, None),
        P("group", None),
        P("group", None),
        P("group", None, None),
        P("group", None),
    )
    out_specs = P(("group", "curve"), None, None)
    return jax.shard_map(body, mesh=mesh, in_specs=in_specs, out_specs=out_specs, check_vma=False)
```

```python
import jax
import jax.numpy as jnp
from jax import lax
from jax.experimental import pallas as pl
from jax.experimental.pallas import tpu as pltpu
from jax.sharding import PartitionSpec as P

OMEGA = 0.8
KEEP = 1.0 - OMEGA
CAP_OLD = 7
CAP_NEW = 5
REACH = 3
NBG = 128
NCOARSE = 32
AXES = ("group", "curve")
F32 = jnp.float32
I32 = jnp.int32

HELD, PICK, TABLE, CELL, BAND = 0, 1, 8, 32, 40
SEND_X, SEND_Y, AT_X, AT_Y = 64, 65, 66, 67
ABSENT = 2 * REACH + CAP_NEW


class Level:
    def __init__(self, side, rows, width, high_at, x_low, x_high, face_rows, factor):
        self.side, self.rows, self.width = side, rows, width
        self.last = side * side - side - (width - 128)
        self.high_at = high_at
        self.x_low, self.x_high, self.face_rows = x_low, x_high, face_rows
        self.tiles = width // 128
        self.factor = factor


FINE = Level(24, 24, 640, 40, 24, 32, 40, 1.0)
COARSE = Level(12, 16, 256, 68, 12, 14, 16, 0.25)
BOTH_ROWS = FINE.face_rows + COARSE.face_rows


def iota(shape, axis):
    return lax.broadcasted_iota(I32, shape, axis)


def over(value, side):
    return (value * 43691) >> (20 if side == 24 else 19)


def pack_faces(lev, field, faces, k, base):
    lane = iota((lev.rows, 128), 1)
    tail = field[:, lev.width - 128 :]
    move = lev.high_at - lev.last
    if move:
        tail = pltpu.roll(tail, move, 1)
    faces[k, base : base + lev.rows, :] = jnp.where(lane < lev.side, field[:, :128], tail)
    for j in range(lev.tiles):
        part = slice(128 * j, 128 * j + 128)
        low, high = base + lev.x_low + j, base + lev.x_high + j
        faces[k, low : low + 1, :] = field[0:1, part]
        faces[k, high : high + 1, :] = field[lev.side - 1 : lev.side, part]


def send_faces(info, faces, x_out, y_out):
    x_first, y_first = info[SEND_X], info[SEND_Y]
    for j in range(REACH):
        x_out[j] = faces[x_first + j]
        y_out[j] = faces[y_first + j]


def fill_table(info, table, x_in, faces, y_in):
    x_first, y_first = info[AT_X], info[AT_Y]
    for j in range(REACH):
        table[x_first + j] = x_in[j]
        table[y_first + j] = y_in[j]
    table[REACH : REACH + CAP_NEW] = faces[...]
    table[ABSENT] = jnp.zeros(table.shape[1:], F32)


def ghosts_of(lev, info, table, k, base):
    row = [info[TABLE + 4 * k + f] for f in range(4)]
    x_low = jnp.concatenate(
        [table[row[0], pl.ds(base + lev.x_high + j, 1), :] for j in range(lev.tiles)], axis=1
    )
    x_high = jnp.concatenate(
        [table[row[1], pl.ds(base + lev.x_low + j, 1), :] for j in range(lev.tiles)], axis=1
    )
    y_low = pltpu.roll(table[row[2], pl.ds(base, lev.rows), :], 128 - lev.high_at, 1)
    y_high = pltpu.roll(table[row[3], pl.ds(base, lev.rows), :], lev.last, 1)
    return row, x_low, x_high, y_low, y_high


def neighbour_sum(lev, field, g, ghosts):
    _, x_low, x_high, y_low, y_high = ghosts
    rows, width, side = lev.rows, lev.width, lev.side
    row = iota((rows, width), 0)
    lane = iota((rows, 128), 1)
    total = g[0] * pltpu.roll(field, 1, 1) + g[1] * pltpu.roll(field, width - 1, 1)
    total += g[2] * pltpu.roll(field, side, 1) + g[3] * pltpu.roll(field, width - side, 1)
    total += g[4] * jnp.where(row == 0, x_low, pltpu.roll(field, 1, 0))
    total += g[5] * jnp.where(row == side - 1, x_high, pltpu.roll(field, rows - 1, 0))
    low = jnp.where(lane < side, g[2][:, :128] * y_low, 0.0)
    on_high = (lane >= lev.last) & (lane < lev.last + side)
    high = jnp.where(on_high, g[3][:, width - 128 :] * y_high, 0.0)
    parts = [low, high]
    if width > 256:
        parts = [low, jnp.zeros((rows, width - 256), F32), high]
    return total + jnp.concatenate(parts, axis=1)


def conductances(lev, cell, ghosts):
    present, x_low, x_high, y_low, y_high = ghosts
    present = [p != ABSENT for p in present]
    rows, width, side = lev.rows, lev.width, lev.side
    row, lane = iota((rows, width), 0), iota((rows, width), 1)
    depth = lane - side * over(lane, side)
    last = side - 1
    end = side * side
    x_low = jnp.where(present[0], x_low, cell[0:1, :])
    x_high = jnp.where(present[1], x_high, cell[last : last + 1, :])
    y_low = jnp.where(present[2], y_low, cell[:, :128])
    y_high = jnp.where(present[3], y_high, cell[:, width - 128 :])
    spare = jnp.ones((rows, width - 128), F32)
    y_low = jnp.concatenate([y_low, spare], axis=1)
    y_high = jnp.concatenate([spare, y_high], axis=1)
    high_y = (lane >= end - side) & (lane < end)
    across = [
        jnp.where(depth == 0, cell, pltpu.roll(cell, 1, 1)),
        jnp.where(depth == last, cell, pltpu.roll(cell, width - 1, 1)),
        jnp.where(lane < side, y_low, pltpu.roll(cell, side, 1)),
        jnp.where(high_y, y_high, pltpu.roll(cell, width - side, 1)),
        jnp.where(row == 0, x_low, pltpu.roll(cell, 1, 0)),
        jnp.where(row == last, x_high, pltpu.roll(cell, rows - 1, 0)),
    ]
    q = [2.0 * cell * other / (cell + other) * lev.factor for other in across]
    diagonal = q[0] + q[1] + q[2] + q[3] + q[4] + q[5]
    inside = (lane < end) & (row < side)
    weight = jnp.where(inside, OMEGA / diagonal, 0.0)
    g = [weight * one for one in q]
    g[0] = jnp.where(depth == 0, 0.0, g[0])
    g[1] = jnp.where(depth == last, 0.0, g[1])
    masks = (row, lane, depth, inside, high_y)
    return q, g, weight, diagonal, masks


def both_totals(values):
    return jnp.sum(jnp.sum(values, axis=0, keepdims=True), axis=1, keepdims=True)


def spread_matrix():
    lane = iota((1, FINE.width), 1)
    y = over(lane, 24)
    group = 12 * (y >> 1) + ((lane - 24 * y) >> 1)
    group = jnp.where(lane < 576, group, -1)
    return (iota((COARSE.width, FINE.width), 0) == group).astype(F32).astype(jnp.bfloat16)


def split_three(values):
    high = values.astype(jnp.bfloat16)
    rest = values - high.astype(F32)
    mid = rest.astype(jnp.bfloat16)
    low = (rest - mid.astype(F32)).astype(jnp.bfloat16)
    return high, mid, low


def coarsen_blocks(fine, scratch):
    spread = spread_matrix()
    total = None
    for part in split_three(fine):
        one = lax.dot_general(
            part, spread, (((1,), (1,)), ((), ())), preferred_element_type=F32
        )
        total = one if total is None else total + one
    scratch[0] = total[:, :128]
    scratch[1] = total[:, 128:]


def coarse_rows(scratch, k):
    even, odd = pl.ds(24 * k, 12, stride=2), pl.ds(24 * k + 1, 12, stride=2)
    halves = [scratch[t, even, :] + scratch[t, odd, :] for t in range(2)]
    return 0.125 * jnp.concatenate(halves, axis=1)


def first_kernel(
    new_in, old_in, near_in, map_in, rhs_in, coef_in,
    x_out, y_out, info, rhs_ref, coef_ref, new_ref, old_ref, near_ref, map_ref, sems,
):
    pairs = (
        (new_in, new_ref), (old_in, old_ref), (near_in, near_ref), (map_in, map_ref),
        (rhs_in, rhs_ref), (coef_in, coef_ref),
    )
    copies = [pltpu.make_async_copy(a, b, sems.at[i]) for i, (a, b) in enumerate(pairs)]
    for copy in copies:
        copy.start()
    curve = lax.axis_index("curve")
    group = lax.axis_index("group")
    up = lax.rem(curve, 2) == 1
    for copy in copies[:4]:
        copy.wait()
    new, old = new_ref[...], old_ref[...]

    def count(mask):
        return jnp.sum(jnp.where(mask, 1.0, 0.0)).astype(I32)

    new_first, held = count(new < curve), count(new == curve)
    old_first, old_count = count(old < curve), count(old == curve)
    last = jnp.clip(old_count - 1, 0, CAP_OLD - 1)
    x_slot, y_slot = jnp.where(up, last, 0), jnp.where(up, 0, last)
    for copy in copies[4:]:
        copy.wait()
    x_out[0] = rhs_ref[x_slot]
    x_out[1] = coef_ref[x_slot]
    y_out[0] = rhs_ref[y_slot]
    y_out[1] = coef_ref[y_slot]
    info[HELD] = held
    final = jnp.maximum(held - REACH, 0)
    info[SEND_X], info[SEND_Y] = jnp.where(up, final, 0), jnp.where(up, 0, final)
    info[AT_X] = jnp.where(up, REACH + CAP_NEW, 0)
    info[AT_Y] = jnp.where(up, 0, REACH + CAP_NEW)
    from_next, from_previous = jnp.where(up, 0, CAP_OLD + 1), jnp.where(up, CAP_OLD + 1, 0)
    first_id = group * NBG + new_first
    finish = first_id + held
    for k in range(CAP_NEW):
        block = new_first + k
        pick = jnp.where(block >= old_first + old_count, from_next, 1 + block - old_first)
        pick = jnp.where(block < old_first, from_previous, pick)
        info[PICK + k] = jnp.clip(pick, 0, CAP_OLD + 1)
        occupied = k < held
        safe = jnp.clip(block, 0, NBG - 1)
        cell = map_ref[0, safe]
        info[CELL + k] = jnp.where(occupied, cell, -1)
        for f in range(4):
            near = near_ref[f, safe]
            present = occupied & (near >= 0)
            slot = jnp.where(near >= finish, REACH + CAP_NEW - finish, REACH - first_id) + near
            slot = jnp.clip(slot, 0, ABSENT - 1)
            info[TABLE + 4 * k + f] = jnp.where(present, slot, ABSENT)
            local = near - group * NBG
            inside = present & (local >= 0) & (local < NBG)
            other = map_ref[0, jnp.clip(local, 0, NBG - 1)]
            info[BAND + 4 * k + f] = jnp.where(inside, 8 * k + 3 + other - cell, -1)


def gather_kernel(
    info, rhs_ref, coef_ref, x_in, y_in, source, coef, faces, x_out, y_out, level, scratch
):
    source[...] = jnp.zeros(source.shape, F32)
    coef[...] = jnp.ones(coef.shape, F32)
    for k in range(CAP_NEW):
        pick = info[PICK + k]
        slot = jnp.clip(pick - 1, 0, CAP_OLD - 1)
        occupied = k < info[HELD]
        for i, (table, out, rest) in enumerate(((rhs_ref, source, 0.0), (coef_ref, coef, 1.0))):
            block = jnp.where(pick == 0, x_in[i], table[slot])
            block = jnp.where(pick == CAP_OLD + 1, y_in[i], block)
            out[k, :, 0:576] = jnp.where(occupied, block, rest)
    coarsen_blocks(coef[...].reshape(CAP_NEW * 24, FINE.width), scratch)
    row, lane = iota((16, 256), 0), iota((16, 256), 1)
    for k in range(CAP_NEW):
        pack_faces(FINE, coef[k], faces, k, 0)
        level[k] = jnp.ones((16, 256), F32)
        level[k, 0:12, :] = coarse_rows(scratch, k)
        level[k] = jnp.where((row < 12) & (lane < 144), level[k], 1.0)
        pack_faces(COARSE, level[k], faces, k, FINE.face_rows)
    send_faces(info, faces, x_out, y_out)


def conduct_kernel(
    info, source, coef, level, faces_in, x_in, y_in,
    fine_g, fine_s, fine_d, coarse_g, coarse_w, coarse_d, row_out, u, faces, x_out, y_out, table,
):
    fill_table(info, table, x_in, faces_in, y_in)
    lane_row = iota((1, 128), 1)
    band = jnp.zeros((1, 128), F32)
    for k in range(CAP_NEW):
        ghosts = ghosts_of(FINE, info, table, k, 0)
        _, g, weight, diagonal, _ = conductances(FINE, coef[k], ghosts)
        for i in range(6):
            fine_g[k, i] = g[i]
        fine_d[k] = (1.0 / OMEGA) * diagonal
        start = weight * source[k]
        fine_s[k] = start
        u[k] = start
        pack_faces(FINE, start, faces, k, 0)

        ghosts = ghosts_of(COARSE, info, table, k, FINE.face_rows)
        q, g, weight, diagonal, masks = conductances(COARSE, level[k], ghosts)
        row, lane, depth, inside, high_y = masks
        for i in range(6):
            coarse_g[k, i] = g[i]
        coarse_w[k] = weight
        coarse_d[k] = (1.0 / OMEGA) * diagonal
        face = [
            both_totals(jnp.where(inside & (row == 0), q[4], 0.0)),
            both_totals(jnp.where(inside & (row == 11), q[5], 0.0)),
            both_totals(jnp.where(inside & (lane < 12), q[2], 0.0)),
            both_totals(jnp.where(inside & high_y, q[3], 0.0)),
        ]
        ends = jnp.where(inside & (depth == 0), q[0], 0.0)
        ends += jnp.where(inside & (depth == 11), q[1], 0.0)
        surface = face[0] + face[1] + face[2] + face[3] + both_totals(ends)
        occupied = k < info[HELD]
        band += jnp.where((lane_row == 8 * k + 3) & occupied, surface, 0.0)
        for f in range(4):
            band -= jnp.where(lane_row == info[BAND + 4 * k + f], face[f], 0.0)
        band += jnp.where(lane_row == 64 + k, info[CELL + k].astype(F32), 0.0)
    row_out[...] = band
    send_faces(info, faces, x_out, y_out)


def sweep_kernel(lev, info, u_in, g, start, faces_in, x_in, y_in, u, faces, x_out, y_out, table):
    fill_table(info, table, x_in, faces_in, y_in)
    for k in range(CAP_NEW):
        field = u_in[k]
        ghosts = ghosts_of(lev, info, table, k, 0)
        new = KEEP * field + (start[k] + neighbour_sum(lev, field, g.at[k], ghosts))
        u[k] = new
        pack_faces(lev, new, faces, k, 0)
    send_faces(info, faces, x_out, y_out)


def residual_kernel(
    info, u_in, g, start, diagonal, weight, faces_in, x_in, y_in,
    coarse_s, faces, x_out, y_out, table, rest, scratch,
):
    fill_table(info, table, x_in, faces_in, y_in)
    for k in range(CAP_NEW):
        field = u_in[k]
        ghosts = ghosts_of(FINE, info, table, k, 0)
        inner = start[k] + neighbour_sum(FINE, field, g.at[k], ghosts)
        rest[k] = diagonal[k] * (inner - OMEGA * field)
    coarsen_blocks(rest[...].reshape(CAP_NEW * 24, FINE.width), scratch)
    for k in range(CAP_NEW):
        coarse_s[k] = jnp.zeros((16, 256), F32)
        coarse_s[k, 0:12, :] = weight[k, 0:12, :] * coarse_rows(scratch, k)
        pack_faces(COARSE, coarse_s[k], faces, k, 0)
    send_faces(info, faces, x_out, y_out)


def total_kernel(info, u_in, g, start, diagonal, row_in, faces_in, x_in, y_in, rows_out, table):
    fill_table(info, table, x_in, faces_in, y_in)
    lane_row = iota((1, 128), 1)
    row, lane = iota((16, 256), 0), iota((16, 256), 1)
    inside = (row < 12) & (lane < 144)
    band = row_in[...]
    for k in range(CAP_NEW):
        field = u_in[k]
        ghosts = ghosts_of(COARSE, info, table, k, 0)
        inner = start[k] + neighbour_sum(COARSE, field, g.at[k], ghosts)
        rest = jnp.where(inside, diagonal[k] * (inner - OMEGA * field), 0.0)
        occupied = k < info[HELD]
        band += jnp.where((lane_row == 8 * k + 7) & occupied, both_totals(rest), 0.0)
    rows_out[...] = jnp.broadcast_to(band, rows_out.shape)


def solve_kernel(info, rows_in, u_in, u, faces, x_out, y_out):
    rows = rows_in[...]
    shape = (NCOARSE, 128)
    row, lane = iota(shape, 0), iota(shape, 1)
    cells = iota((NCOARSE, NCOARSE), 1).astype(F32)
    band = jnp.zeros(shape, F32)
    for k in range(CAP_NEW):
        member = (rows[:, 64 + k : 65 + k] == cells).astype(F32)
        part = rows if k == 0 else pltpu.roll(rows, 128 - 8 * k, 1)
        part = jnp.where(lane < 8, part, 0.0)
        band += lax.dot_general(
            member, part, (((0,), (0,)), ((), ())),
            precision=lax.Precision.HIGHEST, preferred_element_type=F32,
        )
    matrix = jnp.where(lane == 64, band[:, 7:8], 0.0)
    for o in range(7):
        matrix += jnp.where(lane == row + (o - REACH), band[:, o : o + 1], 0.0)

    def drop(current, j):
        pivot = current[j : j + 1, :]
        share = current[:, j : j + 1] / pivot[:, j : j + 1]
        return jnp.where(iota((NCOARSE, 1), 0) == j, 0.0, share) * pivot

    apart = (NCOARSE - REACH - 1) // 2
    for j in range(apart):
        matrix = matrix - (drop(matrix, j) + drop(matrix, NCOARSE - 1 - j))
    for j in range(apart, NCOARSE - apart):
        matrix = matrix - drop(matrix, j)
    pivots = jnp.sum(jnp.where(lane == row, matrix, 0.0), axis=1, keepdims=True)
    answer = matrix[:, 64:65] / pivots
    at = iota((NCOARSE, 1), 0)
    row, lane = iota((16, 256), 0), iota((16, 256), 1)
    inside = (row < 12) & (lane < 144)
    for k in range(CAP_NEW):
        lift = jnp.sum(jnp.where(at == info[CELL + k], answer, 0.0), axis=0, keepdims=True)
        new = u_in[k] + jnp.where(inside, lift, 0.0)
        u[k] = new
        pack_faces(COARSE, new, faces, k, 0)
    send_faces(info, faces, x_out, y_out)


def refine_kernel(
    info, e_in, g, start, faces_in, x_in, y_in, u_in, u, faces, x_out, y_out, table, coarse, rest
):
    fill_table(info, table, x_in, faces_in, y_in)
    for k in range(CAP_NEW):
        field = e_in[k]
        ghosts = ghosts_of(COARSE, info, table, k, 0)
        coarse[k] = KEEP * field + (start[k] + neighbour_sum(COARSE, field, g.at[k], ghosts))
    spread = spread_matrix()
    total = None
    for part in split_three(coarse[...].reshape(CAP_NEW * 16, 256)):
        one = jnp.dot(part, spread, preferred_element_type=F32)
        total = one if total is None else total + one
    for k in range(CAP_NEW):
        twelve = total[16 * k : 16 * k + 12, :]
        for t in range(FINE.tiles):
            part = slice(128 * t, 128 * t + 128)
            rest[t, pl.ds(0, 12, stride=2), :] = twelve[:, part]
            rest[t, pl.ds(1, 12, stride=2), :] = twelve[:, part]
        new = u_in[k] + jnp.concatenate([rest[t] for t in range(FINE.tiles)], axis=1)
        u[k] = new
        pack_faces(FINE, new, faces, k, 0)
    send_faces(info, faces, x_out, y_out)


def last_kernel(info, u_in, g, start, faces_in, x_in, y_in, out, table):
    fill_table(info, table, x_in, faces_in, y_in)
    for k in range(CAP_NEW):
        field = u_in[k]
        ghosts = ghosts_of(FINE, info, table, k, 0)
        new = KEEP * field + (start[k] + neighbour_sum(FINE, field, g.at[k], ghosts))
        out[k] = jnp.where(k < info[HELD], new[:, 0:576], 0.0)


def sds(*shape):
    return jax.ShapeDtypeStruct(shape, F32)


ROOM = 63
SMEM = pl.BlockSpec(memory_space=pltpu.SMEM)
VMEM = pl.BlockSpec(memory_space=pltpu.VMEM)
HBM = pl.BlockSpec(memory_space=pltpu.HBM)


def call(kernel, name, outs, scratch, args, in_specs=None, out_specs=None, room=24):
    many = len(outs) > 1
    return pl.pallas_call(
        kernel,
        out_shape=outs if many else outs[0],
        in_specs=in_specs or [SMEM] + [VMEM] * (len(args) - 1),
        out_specs=out_specs or ([VMEM] * len(outs) if many else VMEM),
        scratch_shapes=[pltpu.VMEM(s, F32) if isinstance(s, tuple) else s for s in scratch],
        compiler_params=pltpu.CompilerParams(vmem_limit_bytes=room * 1024 * 1024),
        name=name,
    )(*args)


def swap(block, axis, first):
    starts = range(first, lax.axis_size(axis) - 1, 2)
    return lax.ppermute(block, axis, [(i, i + 1) for i in starts] + [(i + 1, i) for i in starts])


def exchange(x_out, y_out, axis=AXES):
    x_in = swap(x_out, axis, 1)
    return x_in, swap(y_out, axis, 0)


def face_outs(rows):
    return [sds(CAP_NEW, rows, 128), sds(REACH, rows, 128), sds(REACH, rows, 128)]


def body(rhs_old, coef_old, old_owner, new_owner, neighbours, coarse_map):
    near = jnp.transpose(neighbours[0])
    pair, old = sds(2, 24, 576), sds(CAP_OLD, 24, 576)
    x_out, y_out, info, rhs_old, coef_old = call(
        first_kernel, "owners",
        [pair, pair, jax.ShapeDtypeStruct((128,), I32), old, old],
        [
            pltpu.VMEM((1, 128), I32), pltpu.VMEM((1, 128), I32),
            pltpu.SMEM((4, 128), I32), pltpu.SMEM((1, 128), I32),
            pltpu.SemaphoreType.DMA((6,)),
        ],
        (new_owner, old_owner, near, coarse_map, rhs_old, coef_old),
        [HBM] * 6, [VMEM, VMEM, SMEM, VMEM, VMEM], ROOM,
    )
    x_in, y_in = exchange(x_out, y_out, "curve")

    fine = sds(CAP_NEW, 24, FINE.width)
    coarse = sds(CAP_NEW, 16, 256)
    fine_table = [(ABSENT + 1, FINE.face_rows, 128)]
    coarse_table = [(ABSENT + 1, COARSE.face_rows, 128)]
    fine_faces, coarse_faces = face_outs(FINE.face_rows), face_outs(COARSE.face_rows)
    sums = (2, CAP_NEW * 24, 128)

    source, coef, faces, x_out, y_out, level = call(
        gather_kernel, "collect", [fine, fine] + face_outs(BOTH_ROWS) + [coarse], [sums],
        (info, rhs_old, coef_old, x_in, y_in),
    )
    x_in, y_in = exchange(x_out, y_out)
    fine_g, fine_s, fine_d, coarse_g, coarse_w, coarse_d, row, u, faces, x_out, y_out = call(
        conduct_kernel, "conduct",
        [sds(CAP_NEW, 6, 24, FINE.width), fine, fine, sds(CAP_NEW, 6, 16, 256), coarse, coarse,
         sds(1, 128), fine] + fine_faces,
        [(ABSENT + 1, BOTH_ROWS, 128)],
        (info, source, coef, level, faces, x_in, y_in),
    )

    def sweep(lev, u, g, start, faces, x_out, y_out, name):
        x_in, y_in = exchange(x_out, y_out)
        return call(
            lambda *refs: sweep_kernel(lev, *refs), name,
            [fine, *fine_faces] if lev is FINE else [coarse, *coarse_faces],
            fine_table if lev is FINE else coarse_table,
            (info, u, g, start, faces, x_in, y_in),
        )

    u0, faces, x_out, y_out = sweep(FINE, u, fine_g, fine_s, faces, x_out, y_out, "pre")
    x_in, y_in = exchange(x_out, y_out)
    coarse_s, faces, x_out, y_out = call(
        residual_kernel, "residual", [coarse, *coarse_faces],
        fine_table + [(CAP_NEW, 24, FINE.width), sums],
        (info, u0, fine_g, fine_s, fine_d, coarse_w, faces, x_in, y_in),
    )
    e, faces, x_out, y_out = sweep(
        COARSE, coarse_s, coarse_g, coarse_s, faces, x_out, y_out, "coarse_pre"
    )
    x_in, y_in = exchange(x_out, y_out)
    rows = call(
        total_kernel, "totals", [sds(NCOARSE, 128)], coarse_table,
        (info, e, coarse_g, coarse_s, coarse_d, row, faces, x_in, y_in),
    )
    rows = lax.all_to_all(rows, "curve", 0, 0, tiled=True)
    e, faces, x_out, y_out = call(
        solve_kernel, "solve", [coarse, *coarse_faces], [], (info, rows, e)
    )
    e, faces, x_out, y_out = sweep(COARSE, e, coarse_g, coarse_s, faces, x_out, y_out, "coarse_post")
    x_in, y_in = exchange(x_out, y_out)
    u, faces, x_out, y_out = call(
        refine_kernel, "refine", [fine, *fine_faces],
        coarse_table + [(CAP_NEW, 16, 256), (FINE.tiles, 24, 128)],
        (info, e, coarse_g, coarse_s, faces, x_in, y_in, u0),
    )
    u, faces, x_out, y_out = sweep(FINE, u, fine_g, fine_s, faces, x_out, y_out, "post")
    x_in, y_in = exchange(x_out, y_out)
    return call(
        last_kernel, "last", [sds(CAP_NEW, 24, 576)], fine_table,
        (info, u, fine_g, fine_s, faces, x_in, y_in),
    )


def solution(mesh):
    in_specs = (
        P(("group", "curve"), None, None),
        P(("group", "curve"), None, None),
        P("group", None),
        P("group", None),
        P("group", None, None),
        P("group", None),
    )
    out_specs = P(("group", "curve"), None, None)
    return jax.shard_map(body, mesh=mesh, in_specs=in_specs, out_specs=out_specs, check_vma=False)
```

```python
import jax
import jax.numpy as jnp
from jax import lax
from jax.experimental import pallas as pl
from jax.experimental.pallas import tpu as pltpu
from jax.sharding import PartitionSpec as P

OMEGA = 0.8
KEEP = 1.0 - OMEGA
CAP_OLD = 7
CAP_NEW = 5
REACH = 3
NBG = 128
NCOARSE = 32
AXES = ("group", "curve")
F32 = jnp.float32
I32 = jnp.int32

HELD, PICK, TABLE, CELL, BAND = 0, 1, 8, 32, 40
SEND_X, SEND_Y, AT_X, AT_Y = 64, 65, 66, 67
ABSENT = 2 * REACH + CAP_NEW


class Level:
    def __init__(self, side, rows, width, high_at, x_low, x_high, face_rows, factor):
        self.side, self.rows, self.width = side, rows, width
        self.last = side * side - side - (width - 128)
        self.high_at = high_at
        self.x_low, self.x_high, self.face_rows = x_low, x_high, face_rows
        self.tiles = width // 128
        self.factor = factor


FINE = Level(24, 24, 640, 40, 24, 32, 40, 1.0)
COARSE = Level(12, 16, 256, 68, 12, 14, 16, 0.25)
BOTH_ROWS = FINE.face_rows + COARSE.face_rows


def iota(shape, axis):
    return lax.broadcasted_iota(I32, shape, axis)


def over(value, side):
    return (value * 43691) >> (20 if side == 24 else 19)


def pack_faces(lev, field, faces, k, base):
    lane = iota((lev.rows, 128), 1)
    tail = field[:, lev.width - 128 :]
    move = lev.high_at - lev.last
    if move:
        tail = pltpu.roll(tail, move, 1)
    faces[k, base : base + lev.rows, :] = jnp.where(lane < lev.side, field[:, :128], tail)
    for j in range(lev.tiles):
        part = slice(128 * j, 128 * j + 128)
        low, high = base + lev.x_low + j, base + lev.x_high + j
        faces[k, low : low + 1, :] = field[0:1, part]
        faces[k, high : high + 1, :] = field[lev.side - 1 : lev.side, part]


def send_faces(info, faces, x_out, y_out):
    x_first, y_first = info[SEND_X], info[SEND_Y]
    for j in range(REACH):
        x_out[j] = faces[x_first + j]
        y_out[j] = faces[y_first + j]


def fill_table(info, table, x_in, faces, y_in):
    x_first, y_first = info[AT_X], info[AT_Y]
    for j in range(REACH):
        table[x_first + j] = x_in[j]
        table[y_first + j] = y_in[j]
    table[REACH : REACH + CAP_NEW] = faces[...]
    table[ABSENT] = jnp.zeros(table.shape[1:], F32)


def ghosts_of(lev, info, table, k, base):
    row = [info[TABLE + 4 * k + f] for f in range(4)]
    x_low = jnp.concatenate(
        [table[row[0], pl.ds(base + lev.x_high + j, 1), :] for j in range(lev.tiles)], axis=1
    )
    x_high = jnp.concatenate(
        [table[row[1], pl.ds(base + lev.x_low + j, 1), :] for j in range(lev.tiles)], axis=1
    )
    y_low = pltpu.roll(table[row[2], pl.ds(base, lev.rows), :], 128 - lev.high_at, 1)
    y_high = pltpu.roll(table[row[3], pl.ds(base, lev.rows), :], lev.last, 1)
    return row, x_low, x_high, y_low, y_high


def neighbour_sum(lev, field, g, ghosts):
    _, x_low, x_high, y_low, y_high = ghosts
    rows, width, side = lev.rows, lev.width, lev.side
    row = iota((rows, width), 0)
    lane = iota((rows, 128), 1)
    total = g[0] * pltpu.roll(field, 1, 1) + g[1] * pltpu.roll(field, width - 1, 1)
    total += g[2] * pltpu.roll(field, side, 1) + g[3] * pltpu.roll(field, width - side, 1)
    total += g[4] * jnp.where(row == 0, x_low, pltpu.roll(field, 1, 0))
    total += g[5] * jnp.where(row == side - 1, x_high, pltpu.roll(field, rows - 1, 0))
    low = jnp.where(lane < side, g[2][:, :128] * y_low, 0.0)
    on_high = (lane >= lev.last) & (lane < lev.last + side)
    high = jnp.where(on_high, g[3][:, width - 128 :] * y_high, 0.0)
    parts = [low, high]
    if width > 256:
        parts = [low, jnp.zeros((rows, width - 256), F32), high]
    return total + jnp.concatenate(parts, axis=1)


def conductances(lev, cell, ghosts):
    present, x_low, x_high, y_low, y_high = ghosts
    present = [p != ABSENT for p in present]
    rows, width, side = lev.rows, lev.width, lev.side
    row, lane = iota((rows, width), 0), iota((rows, width), 1)
    depth = lane - side * over(lane, side)
    last = side - 1
    end = side * side
    x_low = jnp.where(present[0], x_low, cell[0:1, :])
    x_high = jnp.where(present[1], x_high, cell[last : last + 1, :])
    y_low = jnp.where(present[2], y_low, cell[:, :128])
    y_high = jnp.where(present[3], y_high, cell[:, width - 128 :])
    spare = jnp.ones((rows, width - 128), F32)
    y_low = jnp.concatenate([y_low, spare], axis=1)
    y_high = jnp.concatenate([spare, y_high], axis=1)
    high_y = (lane >= end - side) & (lane < end)
    across = [
        jnp.where(depth == 0, cell, pltpu.roll(cell, 1, 1)),
        jnp.where(depth == last, cell, pltpu.roll(cell, width - 1, 1)),
        jnp.where(lane < side, y_low, pltpu.roll(cell, side, 1)),
        jnp.where(high_y, y_high, pltpu.roll(cell, width - side, 1)),
        jnp.where(row == 0, x_low, pltpu.roll(cell, 1, 0)),
        jnp.where(row == last, x_high, pltpu.roll(cell, rows - 1, 0)),
    ]
    q = [2.0 * cell * other / (cell + other) * lev.factor for other in across]
    diagonal = q[0] + q[1] + q[2] + q[3] + q[4] + q[5]
    inside = (lane < end) & (row < side)
    weight = jnp.where(inside, OMEGA / diagonal, 0.0)
    g = [weight * one for one in q]
    g[0] = jnp.where(depth == 0, 0.0, g[0])
    g[1] = jnp.where(depth == last, 0.0, g[1])
    masks = (row, lane, depth, inside, high_y)
    return q, g, weight, diagonal, masks


def both_totals(values):
    return jnp.sum(jnp.sum(values, axis=0, keepdims=True), axis=1, keepdims=True)


def spread_matrix():
    lane = iota((1, FINE.width), 1)
    y = over(lane, 24)
    group = 12 * (y >> 1) + ((lane - 24 * y) >> 1)
    group = jnp.where(lane < 576, group, -1)
    return (iota((COARSE.width, FINE.width), 0) == group).astype(F32).astype(jnp.bfloat16)


def split_three(values):
    high = values.astype(jnp.bfloat16)
    rest = values - high.astype(F32)
    mid = rest.astype(jnp.bfloat16)
    low = (rest - mid.astype(F32)).astype(jnp.bfloat16)
    return high, mid, low


def coarsen_blocks(fine, scratch):
    spread = spread_matrix()
    total = None
    for part in split_three(fine):
        one = lax.dot_general(
            part, spread, (((1,), (1,)), ((), ())), preferred_element_type=F32
        )
        total = one if total is None else total + one
    scratch[0] = total[:, :128]
    scratch[1] = total[:, 128:]


def coarse_rows(scratch, k):
    even, odd = pl.ds(24 * k, 12, stride=2), pl.ds(24 * k + 1, 12, stride=2)
    halves = [scratch[t, even, :] + scratch[t, odd, :] for t in range(2)]
    return 0.125 * jnp.concatenate(halves, axis=1)


def first_kernel(
    new_in, old_in, near_in, map_in, rhs_in, coef_in,
    y_out, x_out, info, rhs_ref, coef_ref, new_ref, old_ref, near_ref, map_ref, sems,
):
    pairs = (
        (new_in, new_ref), (old_in, old_ref), (near_in, near_ref), (map_in, map_ref),
        (rhs_in, rhs_ref), (coef_in, coef_ref),
    )
    copies = [pltpu.make_async_copy(a, b, sems.at[i]) for i, (a, b) in enumerate(pairs)]
    for copy in copies:
        copy.start()
    curve = lax.axis_index("curve")
    group = lax.axis_index("group")
    up = lax.rem(curve, 2) == 1
    for copy in copies[:4]:
        copy.wait()
    new, old = new_ref[...], old_ref[...]

    def count(mask):
        return jnp.sum(jnp.where(mask, 1.0, 0.0)).astype(I32)

    new_first, held = count(new < curve), count(new == curve)
    old_first, old_count = count(old < curve), count(old == curve)
    last = jnp.clip(old_count - 1, 0, CAP_OLD - 1)
    x_slot, y_slot = jnp.where(up, last, 0), jnp.where(up, 0, last)
    for copy in copies[4:]:
        copy.wait()
    x_out[0] = rhs_ref[x_slot]
    x_out[1] = coef_ref[x_slot]
    y_out[0] = rhs_ref[y_slot]
    y_out[1] = coef_ref[y_slot]
    info[HELD] = held
    final = jnp.maximum(held - REACH, 0)
    info[SEND_X], info[SEND_Y] = jnp.where(up, final, 0), jnp.where(up, 0, final)
    info[AT_X] = jnp.where(up, REACH + CAP_NEW, 0)
    info[AT_Y] = jnp.where(up, 0, REACH + CAP_NEW)
    from_next, from_previous = jnp.where(up, 0, CAP_OLD + 1), jnp.where(up, CAP_OLD + 1, 0)
    first_id = group * NBG + new_first
    finish = first_id + held
    for k in range(CAP_NEW):
        block = new_first + k
        pick = jnp.where(block >= old_first + old_count, from_next, 1 + block - old_first)
        pick = jnp.where(block < old_first, from_previous, pick)
        info[PICK + k] = jnp.clip(pick, 0, CAP_OLD + 1)
        occupied = k < held
        safe = jnp.clip(block, 0, NBG - 1)
        cell = map_ref[0, safe]
        info[CELL + k] = jnp.where(occupied, cell, -1)
        for f in range(4):
            near = near_ref[f, safe]
            present = occupied & (near >= 0)
            slot = jnp.where(near >= finish, REACH + CAP_NEW - finish, REACH - first_id) + near
            slot = jnp.clip(slot, 0, ABSENT - 1)
            info[TABLE + 4 * k + f] = jnp.where(present, slot, ABSENT)
            local = near - group * NBG
            inside = present & (local >= 0) & (local < NBG)
            other = map_ref[0, jnp.clip(local, 0, NBG - 1)]
            info[BAND + 4 * k + f] = jnp.where(inside, 8 * k + 3 + other - cell, -1)


def place_kernel(info, rhs_ref, coef_ref, source, coef):
    source[...] = jnp.zeros(source.shape, F32)
    coef[...] = jnp.ones(coef.shape, F32)
    for k in range(CAP_NEW):
        slot = jnp.clip(info[PICK + k] - 1, 0, CAP_OLD - 1)
        occupied = k < info[HELD]
        source[k, :, 0:576] = jnp.where(occupied, rhs_ref[slot], 0.0)
        coef[k, :, 0:576] = jnp.where(occupied, coef_ref[slot], 1.0)


def patched(info, field, i, k, x_in, y_in):
    pick = info[PICK + k]
    occupied = k < info[HELD]
    block = jnp.where(occupied & (pick == 0), x_in[i], field[k, :, 0:576])
    return jnp.where(occupied & (pick == CAP_OLD + 1), y_in[i], block)


def collect_kernel(info, kept, y_in, x_in, coef, faces, x_out, y_out):
    coef[...] = kept[...]
    for k in range(CAP_NEW):
        coef[k, :, 0:576] = patched(info, kept, 1, k, x_in, y_in)
        pack_faces(FINE, coef[k], faces, k, 0)
    send_faces(info, faces, x_out, y_out)


def level_kernel(info, kept, y_in, x_in, coef, source, level, faces, scratch):
    source[...] = kept[...]
    for k in range(CAP_NEW):
        source[k, :, 0:576] = patched(info, kept, 0, k, x_in, y_in)
    coarsen_blocks(coef[...].reshape(CAP_NEW * 24, FINE.width), scratch)
    row, lane = iota((16, 256), 0), iota((16, 256), 1)
    for k in range(CAP_NEW):
        level[k] = jnp.ones((16, 256), F32)
        level[k, 0:12, :] = coarse_rows(scratch, k)
        level[k] = jnp.where((row < 12) & (lane < 144), level[k], 1.0)
        pack_faces(COARSE, level[k], faces, k, 0)


def conduct_kernel(
    info, source, coef, faces_in, coarse_faces, x_in, y_in,
    fine_g, fine_s, fine_d, u, faces, x_out, y_out, table,
):
    fill_table(info, table, x_in, faces_in, y_in)
    for k in range(CAP_NEW):
        ghosts = ghosts_of(FINE, info, table, k, 0)
        _, g, weight, diagonal, _ = conductances(FINE, coef[k], ghosts)
        for i in range(6):
            fine_g[k, i] = g[i]
        fine_d[k] = (1.0 / OMEGA) * diagonal
        start = weight * source[k]
        fine_s[k] = start
        u[k] = start
        pack_faces(FINE, start, faces, k, 0)
    faces[:, FINE.face_rows : BOTH_ROWS, :] = coarse_faces[...]
    send_faces(info, faces, x_out, y_out)


def coarse_conduct_kernel(
    info, level, faces_in, x_in, y_in, coarse_g, coarse_w, coarse_d, row_out, table
):
    fill_table(info, table, x_in, faces_in, y_in)
    lane_row = iota((1, 128), 1)
    band = jnp.zeros((1, 128), F32)
    for k in range(CAP_NEW):
        ghosts = ghosts_of(COARSE, info, table, k, FINE.face_rows)
        q, g, weight, diagonal, masks = conductances(COARSE, level[k], ghosts)
        row, lane, depth, inside, high_y = masks
        for i in range(6):
            coarse_g[k, i] = g[i]
        coarse_w[k] = weight
        coarse_d[k] = (1.0 / OMEGA) * diagonal
        face = [
            both_totals(jnp.where(inside & (row == 0), q[4], 0.0)),
            both_totals(jnp.where(inside & (row == 11), q[5], 0.0)),
            both_totals(jnp.where(inside & (lane < 12), q[2], 0.0)),
            both_totals(jnp.where(inside & high_y, q[3], 0.0)),
        ]
        ends = jnp.where(inside & (depth == 0), q[0], 0.0)
        ends += jnp.where(inside & (depth == 11), q[1], 0.0)
        surface = face[0] + face[1] + face[2] + face[3] + both_totals(ends)
        occupied = k < info[HELD]
        band += jnp.where((lane_row == 8 * k + 3) & occupied, surface, 0.0)
        for f in range(4):
            band -= jnp.where(lane_row == info[BAND + 4 * k + f], face[f], 0.0)
        band += jnp.where(lane_row == 64 + k, info[CELL + k].astype(F32), 0.0)
    row_out[...] = band


def sweep_kernel(lev, info, u_in, g, start, faces_in, x_in, y_in, u, faces, x_out, y_out, table):
    fill_table(info, table, x_in, faces_in, y_in)
    for k in range(CAP_NEW):
        field = u_in[k]
        ghosts = ghosts_of(lev, info, table, k, 0)
        new = KEEP * field + (start[k] + neighbour_sum(lev, field, g.at[k], ghosts))
        u[k] = new
        pack_faces(lev, new, faces, k, 0)
    send_faces(info, faces, x_out, y_out)


def residual_kernel(
    info, u_in, g, start, diagonal, weight, faces_in, x_in, y_in,
    coarse_s, faces, x_out, y_out, table, rest, scratch,
):
    fill_table(info, table, x_in, faces_in, y_in)
    for k in range(CAP_NEW):
        field = u_in[k]
        ghosts = ghosts_of(FINE, info, table, k, 0)
        inner = start[k] + neighbour_sum(FINE, field, g.at[k], ghosts)
        rest[k] = diagonal[k] * (inner - OMEGA * field)
    coarsen_blocks(rest[...].reshape(CAP_NEW * 24, FINE.width), scratch)
    for k in range(CAP_NEW):
        coarse_s[k] = jnp.zeros((16, 256), F32)
        coarse_s[k, 0:12, :] = weight[k, 0:12, :] * coarse_rows(scratch, k)
        pack_faces(COARSE, coarse_s[k], faces, k, 0)
    send_faces(info, faces, x_out, y_out)


def total_kernel(info, u_in, g, start, diagonal, row_in, faces_in, x_in, y_in, rows_out, table):
    fill_table(info, table, x_in, faces_in, y_in)
    lane_row = iota((1, 128), 1)
    row, lane = iota((16, 256), 0), iota((16, 256), 1)
    inside = (row < 12) & (lane < 144)
    band = row_in[...]
    for k in range(CAP_NEW):
        field = u_in[k]
        ghosts = ghosts_of(COARSE, info, table, k, 0)
        inner = start[k] + neighbour_sum(COARSE, field, g.at[k], ghosts)
        rest = jnp.where(inside, diagonal[k] * (inner - OMEGA * field), 0.0)
        occupied = k < info[HELD]
        band += jnp.where((lane_row == 8 * k + 7) & occupied, both_totals(rest), 0.0)
    rows_out[...] = jnp.broadcast_to(band, rows_out.shape)


def solve_kernel(info, rows_in, u_in, u, faces, x_out, y_out):
    rows = rows_in[...]
    shape = (NCOARSE, 128)
    row, lane = iota(shape, 0), iota(shape, 1)
    cells = iota((NCOARSE, NCOARSE), 1).astype(F32)
    band = jnp.zeros(shape, F32)
    for k in range(CAP_NEW):
        member = (rows[:, 64 + k : 65 + k] == cells).astype(F32)
        part = rows if k == 0 else pltpu.roll(rows, 128 - 8 * k, 1)
        part = jnp.where(lane < 8, part, 0.0)
        band += lax.dot_general(
            member, part, (((0,), (0,)), ((), ())),
            precision=lax.Precision.HIGHEST, preferred_element_type=F32,
        )
    matrix = jnp.where(lane == 64, band[:, 7:8], 0.0)
    for o in range(7):
        matrix += jnp.where(lane == row + (o - REACH), band[:, o : o + 1], 0.0)

    def drop(current, j):
        pivot = current[j : j + 1, :]
        share = current[:, j : j + 1] / pivot[:, j : j + 1]
        return jnp.where(iota((NCOARSE, 1), 0) == j, 0.0, share) * pivot

    apart = (NCOARSE - REACH - 1) // 2
    for j in range(apart):
        matrix = matrix - (drop(matrix, j) + drop(matrix, NCOARSE - 1 - j))
    for j in range(apart, NCOARSE - apart):
        matrix = matrix - drop(matrix, j)
    pivots = jnp.sum(jnp.where(lane == row, matrix, 0.0), axis=1, keepdims=True)
    answer = matrix[:, 64:65] / pivots
    at = iota((NCOARSE, 1), 0)
    row, lane = iota((16, 256), 0), iota((16, 256), 1)
    inside = (row < 12) & (lane < 144)
    for k in range(CAP_NEW):
        lift = jnp.sum(jnp.where(at == info[CELL + k], answer, 0.0), axis=0, keepdims=True)
        new = u_in[k] + jnp.where(inside, lift, 0.0)
        u[k] = new
        pack_faces(COARSE, new, faces, k, 0)
    send_faces(info, faces, x_out, y_out)


def refine_kernel(
    info, e_in, g, start, faces_in, x_in, y_in, u_in, u, faces, x_out, y_out, table, coarse, rest
):
    fill_table(info, table, x_in, faces_in, y_in)
    for k in range(CAP_NEW):
        field = e_in[k]
        ghosts = ghosts_of(COARSE, info, table, k, 0)
        coarse[k] = KEEP * field + (start[k] + neighbour_sum(COARSE, field, g.at[k], ghosts))
    spread = spread_matrix()
    total = None
    for part in split_three(coarse[...].reshape(CAP_NEW * 16, 256)):
        one = jnp.dot(part, spread, preferred_element_type=F32)
        total = one if total is None else total + one
    for k in range(CAP_NEW):
        twelve = total[16 * k : 16 * k + 12, :]
        for t in range(FINE.tiles):
            part = slice(128 * t, 128 * t + 128)
            rest[t, pl.ds(0, 12, stride=2), :] = twelve[:, part]
            rest[t, pl.ds(1, 12, stride=2), :] = twelve[:, part]
        new = u_in[k] + jnp.concatenate([rest[t] for t in range(FINE.tiles)], axis=1)
        u[k] = new
        pack_faces(FINE, new, faces, k, 0)
    send_faces(info, faces, x_out, y_out)


def last_kernel(info, u_in, g, start, faces_in, x_in, y_in, out, table):
    fill_table(info, table, x_in, faces_in, y_in)
    for k in range(CAP_NEW):
        field = u_in[k]
        ghosts = ghosts_of(FINE, info, table, k, 0)
        new = KEEP * field + (start[k] + neighbour_sum(FINE, field, g.at[k], ghosts))
        out[k] = jnp.where(k < info[HELD], new[:, 0:576], 0.0)


def sds(*shape):
    return jax.ShapeDtypeStruct(shape, F32)


SMEM = pl.BlockSpec(memory_space=pltpu.SMEM)
VMEM = pl.BlockSpec(memory_space=pltpu.VMEM)
HBM = pl.BlockSpec(memory_space=pltpu.HBM)


def call(kernel, name, outs, scratch, args, in_specs=None, out_specs=None):
    many = len(outs) > 1
    return pl.pallas_call(
        kernel,
        out_shape=outs if many else outs[0],
        in_specs=in_specs or [SMEM] + [VMEM] * (len(args) - 1),
        out_specs=out_specs or ([VMEM] * len(outs) if many else VMEM),
        scratch_shapes=[pltpu.VMEM(s, F32) if isinstance(s, tuple) else s for s in scratch],
        cost_estimate=pl.CostEstimate(flops=10_000_000, bytes_accessed=4_000_000, transcendentals=0),
        compiler_params=pltpu.CompilerParams(vmem_limit_bytes=24 * 1024 * 1024),
        name=name,
    )(*args)


def swap(block, axis, first):
    starts = range(first, lax.axis_size(axis) - 1, 2)
    return lax.ppermute(block, axis, [(i, i + 1) for i in starts] + [(i + 1, i) for i in starts])


def exchange(x_out, y_out):
    x_in = swap(x_out, AXES, 1)
    return x_in, swap(y_out, AXES, 0)


def face_outs(rows):
    return [sds(CAP_NEW, rows, 128), sds(REACH, rows, 128), sds(REACH, rows, 128)]


def body(rhs_old, coef_old, old_owner, new_owner, neighbours, coarse_map):
    near = jnp.transpose(neighbours[0])
    rhs_old, coef_old, new_owner, old_owner, near, coarse_map = (
        pltpu.with_memory_space_constraint(a, pltpu.HBM)
        for a in (rhs_old, coef_old, new_owner, old_owner, near, coarse_map)
    )
    pair, old = sds(2, 24, 576), sds(CAP_OLD, 24, 576)
    y_out, x_out, info, rhs_old, coef_old = call(
        first_kernel, "owners",
        [pair, pair, jax.ShapeDtypeStruct((128,), I32), old, old],
        [
            pltpu.VMEM((1, 128), I32), pltpu.VMEM((1, 128), I32),
            pltpu.SMEM((4, 128), I32), pltpu.SMEM((1, 128), I32),
            pltpu.SemaphoreType.DMA((6,)),
        ],
        (new_owner, old_owner, near, coarse_map, rhs_old, coef_old),
        [HBM] * 6, [VMEM, VMEM, SMEM, VMEM, VMEM],
    )
    y_in, x_in = swap(y_out, "curve", 0), swap(x_out, "curve", 1)

    fine = sds(CAP_NEW, 24, FINE.width)
    coarse = sds(CAP_NEW, 16, 256)
    fine_table = [(ABSENT + 1, FINE.face_rows, 128)]
    coarse_table = [(ABSENT + 1, COARSE.face_rows, 128)]
    fine_faces, coarse_faces = face_outs(FINE.face_rows), face_outs(COARSE.face_rows)
    sums = (2, CAP_NEW * 24, 128)

    source, coef = call(place_kernel, "place", [fine, fine], [], (info, rhs_old, coef_old))
    coef, faces, x_out, y_out = call(
        collect_kernel, "collect", [fine] + fine_faces, [], (info, coef, y_in, x_in)
    )
    source, level, coarse_own = call(
        level_kernel, "level", [fine, coarse, coarse_faces[0]], [sums],
        (info, source, y_in, x_in, coef),
    )
    x_in, y_in = exchange(x_out, y_out)
    fine_g, fine_s, fine_d, u, faces, x_out, y_out = call(
        conduct_kernel, "conduct",
        [sds(CAP_NEW, 6, 24, FINE.width), fine, fine, fine] + face_outs(BOTH_ROWS), fine_table,
        (info, source, coef, faces, coarse_own, x_in, y_in),
    )
    x_in, y_in = exchange(x_out, y_out)
    coarse_g, coarse_w, coarse_d, row = call(
        coarse_conduct_kernel, "coarse_conduct",
        [sds(CAP_NEW, 6, 16, 256), coarse, coarse, sds(1, 128)],
        [(ABSENT + 1, BOTH_ROWS, 128)],
        (info, level, faces, x_in, y_in),
    )
    u0, faces, x_out, y_out = call(
        lambda *refs: sweep_kernel(FINE, *refs), "pre", [fine, *fine_faces],
        [(ABSENT + 1, BOTH_ROWS, 128)],
        (info, u, fine_g, fine_s, faces, x_in, y_in),
    )

    def sweep(lev, u, g, start, faces, x_out, y_out, name):
        x_in, y_in = exchange(x_out, y_out)
        return call(
            lambda *refs: sweep_kernel(lev, *refs), name,
            [fine, *fine_faces] if lev is FINE else [coarse, *coarse_faces],
            fine_table if lev is FINE else coarse_table,
            (info, u, g, start, faces, x_in, y_in),
        )

    x_in, y_in = exchange(x_out, y_out)
    coarse_s, faces, x_out, y_out = call(
        residual_kernel, "residual", [coarse, *coarse_faces],
        fine_table + [(CAP_NEW, 24, FINE.width), sums],
        (info, u0, fine_g, fine_s, fine_d, coarse_w, faces, x_in, y_in),
    )
    e, faces, x_out, y_out = sweep(
        COARSE, coarse_s, coarse_g, coarse_s, faces, x_out, y_out, "coarse_pre"
    )
    x_in, y_in = exchange(x_out, y_out)
    rows = call(
        total_kernel, "totals", [sds(NCOARSE, 128)], coarse_table,
        (info, e, coarse_g, coarse_s, coarse_d, row, faces, x_in, y_in),
    )
    rows = lax.all_to_all(rows, "curve", 0, 0, tiled=True)
    e, faces, x_out, y_out = call(
        solve_kernel, "solve", [coarse, *coarse_faces], [], (info, rows, e)
    )
    e, faces, x_out, y_out = sweep(COARSE, e, coarse_g, coarse_s, faces, x_out, y_out, "coarse_post")
    x_in, y_in = exchange(x_out, y_out)
    u, faces, x_out, y_out = call(
        refine_kernel, "refine", [fine, *fine_faces],
        coarse_table + [(CAP_NEW, 16, 256), (FINE.tiles, 24, 128)],
        (info, e, coarse_g, coarse_s, faces, x_in, y_in, u0),
    )
    u, faces, x_out, y_out = sweep(FINE, u, fine_g, fine_s, faces, x_out, y_out, "post")
    x_in, y_in = exchange(x_out, y_out)
    return call(
        last_kernel, "last", [sds(CAP_NEW, 24, 576)], fine_table,
        (info, u, fine_g, fine_s, faces, x_in, y_in),
    )


def solution(mesh):
    in_specs = (
        P(("group", "curve"), None, None),
        P(("group", "curve"), None, None),
        P("group", None),
        P("group", None),
        P("group", None, None),
        P("group", None),
    )
    out_specs = P(("group", "curve"), None, None)
    return jax.shard_map(body, mesh=mesh, in_specs=in_specs, out_specs=out_specs, check_vma=False)
```

```python
import jax
import jax.numpy as jnp
from jax import lax
from jax.experimental import pallas as pl
from jax.experimental.pallas import tpu as pltpu
from jax.sharding import PartitionSpec as P

OMEGA = 0.8
KEEP = 1.0 - OMEGA
CAP_OLD = 7
CAP_NEW = 5
REACH = 3
NBG = 128
NCOARSE = 32
AXES = ("group", "curve")
F32 = jnp.float32
I32 = jnp.int32

HELD, PICK, TABLE, CELL, BAND = 0, 1, 8, 32, 40
SEND_X, SEND_Y, AT_X, AT_Y = 64, 65, 66, 67
SPARE, OTHER, BESIDE, FACING = 7, 72, 96, 116
OPPOSITE = (1, 0, 3, 2)
LIFT_ROW = 13
ABSENT = 2 * REACH + CAP_NEW


class Level:
    def __init__(self, side, rows, width, high_at, x_low, x_high, face_rows, factor):
        self.side, self.rows, self.width = side, rows, width
        self.last = side * side - side - (width - 128)
        self.high_at = high_at
        self.x_low, self.x_high, self.face_rows = x_low, x_high, face_rows
        self.tiles = width // 128
        self.factor = factor


FINE = Level(24, 24, 640, 40, 24, 32, 40, 1.0)
COARSE = Level(12, 16, 256, 68, 12, 14, 16, 0.25)
BOTH_ROWS = FINE.face_rows + COARSE.face_rows


def iota(shape, axis):
    return lax.broadcasted_iota(I32, shape, axis)


def over(value, side):
    return (value * 43691) >> (20 if side == 24 else 19)


def pack_faces(lev, field, faces, k, base):
    pack_fields(lev, field, field, faces, k, base)


def pack_fields(lev, y_field, x_field, faces, k, base, y_high=None, x_high=None):
    y_high = y_field if y_high is None else y_high
    x_high = x_field if x_high is None else x_high
    lane = iota((lev.rows, 128), 1)
    tail = y_high[:, lev.width - 128 :]
    move = lev.high_at - lev.last
    if move:
        tail = pltpu.roll(tail, move, 1)
    faces[k, base : base + lev.rows, :] = jnp.where(lane < lev.side, y_field[:, :128], tail)
    for j in range(lev.tiles):
        part = slice(128 * j, 128 * j + 128)
        low, high = base + lev.x_low + j, base + lev.x_high + j
        faces[k, low : low + 1, :] = x_field[0:1, part]
        faces[k, high : high + 1, :] = x_high[lev.side - 1 : lev.side, part]


def send_faces(info, faces, x_out, y_out):
    x_first, y_first = info[SEND_X], info[SEND_Y]
    for j in range(REACH):
        x_out[j] = faces[x_first + j]
        y_out[j] = faces[y_first + j]


def fill_table(info, table, x_in, faces, y_in):
    x_first, y_first = info[AT_X], info[AT_Y]
    for j in range(REACH):
        table[x_first + j] = x_in[j, 0 : table.shape[1]]
        table[y_first + j] = y_in[j]
    table[REACH : REACH + CAP_NEW] = faces[...]
    table[ABSENT] = jnp.zeros(table.shape[1:], F32)


def x_line(lev, table, slot, first):
    return jnp.concatenate([table[slot, pl.ds(first + j, 1), :] for j in range(lev.tiles)], axis=1)


def ghosts_of(lev, info, table, k, base):
    row = [info[TABLE + 4 * k + f] for f in range(4)]
    x_low = x_line(lev, table, row[0], base + lev.x_high)
    x_high = x_line(lev, table, row[1], base + lev.x_low)
    y_low = pltpu.roll(table[row[2], pl.ds(base, lev.rows), :], 128 - lev.high_at, 1)
    y_high = pltpu.roll(table[row[3], pl.ds(base, lev.rows), :], lev.last, 1)
    return row, x_low, x_high, y_low, y_high


def neighbour_sum(lev, field, g, ghosts):
    _, x_low, x_high, y_low, y_high = ghosts
    rows, width, side = lev.rows, lev.width, lev.side
    row = iota((rows, width), 0)
    lane = iota((rows, 128), 1)
    total = g[0] * pltpu.roll(field, 1, 1) + g[1] * pltpu.roll(field, width - 1, 1)
    total += g[2] * pltpu.roll(field, side, 1) + g[3] * pltpu.roll(field, width - side, 1)
    total += g[4] * jnp.where(row == 0, x_low, pltpu.roll(field, 1, 0))
    total += g[5] * jnp.where(row == side - 1, x_high, pltpu.roll(field, rows - 1, 0))
    low = jnp.where(lane < side, g[2][:, :128] * y_low, 0.0)
    on_high = (lane >= lev.last) & (lane < lev.last + side)
    high = jnp.where(on_high, g[3][:, width - 128 :] * y_high, 0.0)
    parts = [low, high]
    if width > 256:
        parts = [low, jnp.zeros((rows, width - 256), F32), high]
    return total + jnp.concatenate(parts, axis=1)


def conductances(lev, cell, ghosts):
    present, x_low, x_high, y_low, y_high = ghosts
    present = [p != ABSENT for p in present]
    rows, width, side = lev.rows, lev.width, lev.side
    row, lane = iota((rows, width), 0), iota((rows, width), 1)
    depth = lane - side * over(lane, side)
    last = side - 1
    end = side * side
    x_low = jnp.where(present[0], x_low, cell[0:1, :])
    x_high = jnp.where(present[1], x_high, cell[last : last + 1, :])
    y_low = jnp.where(present[2], y_low, cell[:, :128])
    y_high = jnp.where(present[3], y_high, cell[:, width - 128 :])
    spare = jnp.ones((rows, width - 128), F32)
    y_low = jnp.concatenate([y_low, spare], axis=1)
    y_high = jnp.concatenate([spare, y_high], axis=1)
    high_y = (lane >= end - side) & (lane < end)
    across = [
        jnp.where(depth == 0, cell, pltpu.roll(cell, 1, 1)),
        jnp.where(depth == last, cell, pltpu.roll(cell, width - 1, 1)),
        jnp.where(lane < side, y_low, pltpu.roll(cell, side, 1)),
        jnp.where(high_y, y_high, pltpu.roll(cell, width - side, 1)),
        jnp.where(row == 0, x_low, pltpu.roll(cell, 1, 0)),
        jnp.where(row == last, x_high, pltpu.roll(cell, rows - 1, 0)),
    ]
    q = [2.0 * cell * other / (cell + other) * lev.factor for other in across]
    diagonal = q[0] + q[1] + q[2] + q[3] + q[4] + q[5]
    inside = (lane < end) & (row < side)
    weight = jnp.where(inside, OMEGA / diagonal, 0.0)
    g = [weight * one for one in q]
    g[0] = jnp.where(depth == 0, 0.0, g[0])
    g[1] = jnp.where(depth == last, 0.0, g[1])
    masks = (row, lane, depth, inside, high_y)
    return q, g, weight, diagonal, masks


def both_totals(values):
    return jnp.sum(jnp.sum(values, axis=0, keepdims=True), axis=1, keepdims=True)


def spread_matrix():
    lane = iota((1, FINE.width), 1)
    y = over(lane, 24)
    group = 12 * (y >> 1) + ((lane - 24 * y) >> 1)
    group = jnp.where(lane < 576, group, -1)
    return (iota((COARSE.width, FINE.width), 0) == group).astype(F32).astype(jnp.bfloat16)


def split_three(values):
    high, rest = values.astype(jnp.bfloat16), values - values.astype(jnp.bfloat16).astype(F32)
    mid = rest.astype(jnp.bfloat16)
    return high, mid, (rest - mid.astype(F32)).astype(jnp.bfloat16)


def split_two(values):
    high = values.astype(jnp.bfloat16)
    return high, (values - high.astype(F32)).astype(jnp.bfloat16)


def coarsen_blocks(fine, spread, scratch):
    total = sum(
        lax.dot_general(part, spread, (((1,), (1,)), ((), ())), preferred_element_type=F32)
        for part in split_two(fine)
    )
    scratch[0] = total[:, :128]
    scratch[1] = total[:, 128:]


def coarse_rows(scratch, k):
    even, odd = pl.ds(24 * k, 12, stride=2), pl.ds(24 * k + 1, 12, stride=2)
    halves = [scratch[t, even, :] + scratch[t, odd, :] for t in range(2)]
    return 0.125 * jnp.concatenate(halves, axis=1)


def first_kernel(
    new_in, old_in, near_in, map_in, rhs_in, coef_in,
    y_out, x_out, info, rhs_ref, coef_ref, new_ref, old_ref, near_ref, map_ref, sems,
):
    pairs = (
        (new_in, new_ref), (old_in, old_ref), (near_in, near_ref), (map_in, map_ref),
        (rhs_in, rhs_ref), (coef_in, coef_ref),
    )
    copies = [pltpu.make_async_copy(a, b, sems.at[i]) for i, (a, b) in enumerate(pairs)]
    for copy in copies:
        copy.start()
    curve = lax.axis_index("curve")
    group = lax.axis_index("group")
    up = lax.rem(curve, 2) == 1
    for copy in copies[:4]:
        copy.wait()
    new, old = new_ref[...], old_ref[...]

    def count(mask):
        return jnp.sum(jnp.where(mask, 1.0, 0.0)).astype(I32)

    new_first, held = count(new < curve), count(new == curve)
    old_first, old_count = count(old < curve), count(old == curve)
    last = jnp.clip(old_count - 1, 0, CAP_OLD - 1)
    x_slot, y_slot = jnp.where(up, last, 0), jnp.where(up, 0, last)
    for copy in copies[4:]:
        copy.wait()
    x_out[0] = rhs_ref[x_slot]
    x_out[1] = coef_ref[x_slot]
    y_out[0] = rhs_ref[y_slot]
    y_out[1] = coef_ref[y_slot]
    info[HELD] = held
    final = jnp.maximum(held - REACH, 0)
    info[SEND_X], info[SEND_Y] = jnp.where(up, final, 0), jnp.where(up, 0, final)
    info[AT_X] = jnp.where(up, REACH + CAP_NEW, 0)
    info[AT_Y] = jnp.where(up, 0, REACH + CAP_NEW)
    for i in range(4 * REACH):
        info[FACING + i] = -1
    x_at = jnp.where(up, REACH + CAP_NEW, 0)
    from_next, from_previous = jnp.where(up, 0, CAP_OLD + 1), jnp.where(up, CAP_OLD + 1, 0)
    first_id = group * NBG + new_first
    finish = first_id + held
    for k in range(CAP_NEW):
        block = new_first + k
        pick = jnp.where(block >= old_first + old_count, from_next, 1 + block - old_first)
        pick = jnp.where(block < old_first, from_previous, pick)
        info[PICK + k] = jnp.clip(pick, 0, CAP_OLD + 1)
        occupied = k < held
        safe = jnp.clip(block, 0, NBG - 1)
        cell = map_ref[0, safe]
        info[CELL + k] = jnp.where(occupied, cell, -1)
        for f in range(4):
            near = near_ref[f, safe]
            present = occupied & (near >= 0)
            slot = jnp.where(near >= finish, REACH + CAP_NEW - finish, REACH - first_id) + near
            slot = jnp.clip(slot, 0, ABSENT - 1)
            info[TABLE + 4 * k + f] = jnp.where(present, slot, ABSENT)
            local = near - group * NBG
            inside = present & (local >= 0) & (local < NBG)
            other = map_ref[0, jnp.clip(local, 0, NBG - 1)]
            info[BAND + 4 * k + f] = jnp.where(inside, 8 * k + 3 + other - cell, -1)
            info[BESIDE + 4 * k + f] = jnp.where(inside, other, -1)
            outside = present & jnp.logical_not(inside)
            place = jnp.clip(slot - x_at, 0, REACH - 1)
            info[OTHER + 4 * k + f] = jnp.where(outside, place, REACH)
            info[jnp.where(outside, FACING + 4 * place + OPPOSITE[f], SPARE)] = cell


def place_kernel(info, rhs_ref, coef_ref, source, coef):
    source[...] = jnp.zeros(source.shape, F32)
    coef[...] = jnp.ones(coef.shape, F32)
    for k in range(CAP_NEW):
        slot = jnp.clip(info[PICK + k] - 1, 0, CAP_OLD - 1)
        occupied = k < info[HELD]
        source[k, :, 0:576] = jnp.where(occupied, rhs_ref[slot], 0.0)
        coef[k, :, 0:576] = jnp.where(occupied, coef_ref[slot], 1.0)


def patched(info, field, i, k, x_in, y_in):
    pick = info[PICK + k]
    occupied = k < info[HELD]
    block = jnp.where(occupied & (pick == 0), x_in[i], field[k, :, 0:576])
    return jnp.where(occupied & (pick == CAP_OLD + 1), y_in[i], block)


def collect_kernel(info, kept, y_in, x_in, coef, faces, x_out, y_out):
    coef[...] = kept[...]
    for k in range(CAP_NEW):
        coef[k, :, 0:576] = patched(info, kept, 1, k, x_in, y_in)
        pack_faces(FINE, coef[k], faces, k, 0)
    send_faces(info, faces, x_out, y_out)


def level_kernel(info, kept, y_in, x_in, coef, source, level, faces, spread, scratch):
    source[...] = kept[...]
    for k in range(CAP_NEW):
        source[k, :, 0:576] = patched(info, kept, 0, k, x_in, y_in)
    spread[...] = spread_matrix()
    coarsen_blocks(coef[...].reshape(CAP_NEW * 24, FINE.width), spread[...], scratch)
    row, lane = iota((16, 256), 0), iota((16, 256), 1)
    for k in range(CAP_NEW):
        level[k] = jnp.ones((16, 256), F32)
        level[k, 0:12, :] = coarse_rows(scratch, k)
        level[k] = jnp.where((row < 12) & (lane < 144), level[k], 1.0)
        pack_faces(COARSE, level[k], faces, k, 0)


def conduct_kernel(
    info, source, coef, faces_in, coarse_faces, x_in, y_in,
    fine_g, fine_s, fine_d, u, faces, x_out, y_out, table,
):
    fill_table(info, table, x_in, faces_in, y_in)
    for k in range(CAP_NEW):
        ghosts = ghosts_of(FINE, info, table, k, 0)
        _, g, weight, diagonal, _ = conductances(FINE, coef[k], ghosts)
        for i in range(6):
            fine_g[k, i] = g[i]
        fine_d[k] = (1.0 / OMEGA) * diagonal
        start = weight * source[k]
        fine_s[k] = start
        u[k] = start
        pack_faces(FINE, start, faces, k, 0)
    faces[:, FINE.face_rows : BOTH_ROWS, :] = coarse_faces[...]
    send_faces(info, faces, x_out, y_out)


def coarse_conduct_kernel(
    info, level, faces_in, x_in, y_in, coarse_g, coarse_w, coarse_d, g_faces, row_out, table
):
    fill_table(info, table, x_in, faces_in, y_in)
    lane_row = iota((1, 128), 1)
    band = jnp.zeros((1, 128), F32)
    for k in range(CAP_NEW):
        ghosts = ghosts_of(COARSE, info, table, k, FINE.face_rows)
        q, g, weight, diagonal, masks = conductances(COARSE, level[k], ghosts)
        row, lane, depth, inside, high_y = masks
        for i in range(6):
            coarse_g[k, i] = g[i]
        coarse_w[k] = weight
        pack_fields(COARSE, g[2], g[4], g_faces, k, 0, g[3], g[5])
        low_y = jnp.where(lane < 12, g[2], 0.0)
        x_edge = jnp.where(lane >= 132, g[3], low_y)
        y_edge = jnp.where(row == 0, g[4], jnp.where(row == 11, g[5], 0.0))
        pack_fields(COARSE, y_edge, x_edge, g_faces, k, 16)
        coarse_d[k] = (1.0 / OMEGA) * diagonal
        face = [
            both_totals(jnp.where(inside & (row == 0), q[4], 0.0)),
            both_totals(jnp.where(inside & (row == 11), q[5], 0.0)),
            both_totals(jnp.where(inside & (lane < 12), q[2], 0.0)),
            both_totals(jnp.where(inside & high_y, q[3], 0.0)),
        ]
        ends = jnp.where(inside & (depth == 0), q[0], 0.0)
        ends += jnp.where(inside & (depth == 11), q[1], 0.0)
        surface = face[0] + face[1] + face[2] + face[3] + both_totals(ends)
        occupied = k < info[HELD]
        band += jnp.where((lane_row == 8 * k + 3) & occupied, surface, 0.0)
        for f in range(4):
            band -= jnp.where(lane_row == info[BAND + 4 * k + f], face[f], 0.0)
        band += jnp.where(lane_row == 64 + k, info[CELL + k].astype(F32), 0.0)
    row_out[...] = band


def sweep_kernel(lev, info, u_in, g, start, faces_in, x_in, y_in, u, faces, x_out, y_out, table):
    fill_table(info, table, x_in, faces_in, y_in)
    for k in range(CAP_NEW):
        field = u_in[k]
        ghosts = ghosts_of(lev, info, table, k, 0)
        new = KEEP * field + (start[k] + neighbour_sum(lev, field, g.at[k], ghosts))
        u[k] = new
        pack_faces(lev, new, faces, k, 0)
    send_faces(info, faces, x_out, y_out)


def residual_kernel(
    info, u_in, g, start, diagonal, weight, spread, g_faces, faces_in, x_in, y_in,
    coarse_s, faces, x_out, y_out, table, rest, scratch,
):
    fill_table(info, table, x_in, faces_in, y_in)
    for k in range(CAP_NEW):
        field = u_in[k]
        ghosts = ghosts_of(FINE, info, table, k, 0)
        inner = start[k] + neighbour_sum(FINE, field, g.at[k], ghosts)
        rest[k] = diagonal[k] * (inner - OMEGA * field)
    coarsen_blocks(rest[...].reshape(CAP_NEW * 24, FINE.width), spread[...], scratch)
    for k in range(CAP_NEW):
        coarse_s[k] = jnp.zeros((16, 256), F32)
        coarse_s[k, 0:12, :] = weight[k, 0:12, :] * coarse_rows(scratch, k)
        pack_faces(COARSE, coarse_s[k], faces, k, 0)
    x_first, y_first = info[SEND_X], info[SEND_Y]
    for j in range(REACH):
        x_out[j, 0:16] = faces[x_first + j]
        x_out[j, 16:48] = g_faces[x_first + j]
        y_out[j] = faces[y_first + j]


def total_kernel(info, u_in, g, start, diagonal, row_in, faces_in, x_in, y_in, rows_out, table):
    fill_table(info, table, x_in, faces_in, y_in)
    lane_row = iota((1, 128), 1)
    row, lane = iota((16, 256), 0), iota((16, 256), 1)
    inside = (row < 12) & (lane < 144)
    band = row_in[...]
    for k in range(CAP_NEW):
        field = u_in[k]
        ghosts = ghosts_of(COARSE, info, table, k, 0)
        inner = start[k] + neighbour_sum(COARSE, field, g.at[k], ghosts)
        rest = jnp.where(inside, diagonal[k] * (inner - OMEGA * field), 0.0)
        occupied = k < info[HELD]
        band += jnp.where((lane_row == 8 * k + 7) & occupied, both_totals(rest), 0.0)
    rows_out[...] = jnp.broadcast_to(band, rows_out.shape)


def lifted(answer, cell):
    at = iota((NCOARSE, 1), 0)
    return jnp.sum(jnp.where(at == cell, answer, 0.0), axis=0, keepdims=True)


def solve_kernel(
    info, rows_in, u_in, g, start, faces_in, x_in, y_in, u, answer_out, faces, x_out, table
):
    fill_table(info, table, x_in, faces_in, y_in)
    rows = rows_in[...]
    shape = (NCOARSE, 128)
    row, lane = iota(shape, 0), iota(shape, 1)
    cells = iota((NCOARSE, NCOARSE), 1).astype(F32)
    member = jnp.concatenate(
        [(rows[:, 64 + k : 65 + k] == cells).astype(F32) for k in range(CAP_NEW)], axis=0
    ).astype(jnp.bfloat16)
    shifts = [rows] + [pltpu.roll(rows, 128 - 8 * k, 1) for k in range(1, CAP_NEW)]
    band = sum(
        lax.dot_general(member, part, (((0,), (0,)), ((), ())), preferred_element_type=F32)
        for part in split_three(jnp.concatenate(shifts, axis=0))
    )
    matrix = jnp.where(lane == 64, band[:, 7:8], 0.0)
    for o in range(7):
        matrix += jnp.where(lane == row + (o - REACH), band[:, o : o + 1], 0.0)

    def drop(current, j):
        pivot = current[j : j + 1, :]
        share = current[:, j : j + 1] / pivot[:, j : j + 1]
        return jnp.where(iota((NCOARSE, 1), 0) == j, 0.0, share) * pivot

    apart = (NCOARSE - REACH - 1) // 2
    for j in range(apart):
        matrix = matrix - (drop(matrix, j) + drop(matrix, NCOARSE - 1 - j))
    for j in range(apart, NCOARSE - apart):
        matrix = matrix - drop(matrix, j)
    pivots = jnp.sum(jnp.where(lane == row, matrix, 0.0), axis=1, keepdims=True)
    answer = matrix[:, 64:65] / pivots
    answer_out[...] = jnp.broadcast_to(answer, shape)
    row, lane = iota((16, 256), 0), iota((16, 256), 1)
    inside = (row < 12) & (lane < 144)
    for k in range(CAP_NEW):
        lift = lifted(answer, info[CELL + k])
        slots, *sides = ghosts_of(COARSE, info, table, k, 0)
        sides = [v + lifted(answer, info[BESIDE + 4 * k + f]) for f, v in enumerate(sides)]
        field = u_in[k] + jnp.where(inside, lift, 0.0)
        new = KEEP * field + (start[k] + neighbour_sum(COARSE, field, g.at[k], (slots, *sides)))
        u[k] = new
        pack_faces(COARSE, new, faces, k, 0)
        faces[k, LIFT_ROW : LIFT_ROW + 1, 64:128] = jnp.broadcast_to(lift, (1, 64))
    for j in range(REACH):
        x_out[j] = faces[info[SEND_X] + j]


def across_kernel(
    info, u_in, g, answer_in, x_in, g_in, u, faces, ghosts, y_out, table
):
    table[0:REACH] = x_in[...]
    table[REACH] = jnp.zeros((16, 128), F32)
    row, lane = iota((16, 256), 0), iota((16, 256), 1)
    answer = answer_in[...][:, 0:1]
    for k in range(CAP_NEW):
        lift = [
            table[info[OTHER + 4 * k + f], LIFT_ROW : LIFT_ROW + 1, 64:65] for f in range(4)
        ]
        new = u_in[k] + jnp.where(row == 0, g[k, 4] * lift[0], 0.0)
        new += jnp.where(row == 11, g[k, 5] * lift[1], 0.0)
        new += jnp.where(lane < 12, g[k, 2] * lift[2], 0.0)
        new += jnp.where((lane >= 132) & (lane < 144), g[k, 3] * lift[3], 0.0)
        u[k] = new
        pack_faces(COARSE, new, faces, k, 0)
    row, lane = iota((16, 128), 0), iota((16, 128), 1)
    for j in range(REACH):
        lift = [lifted(answer, info[FACING + 4 * j + f]) for f in range(4)]
        face = jnp.where(lane < 64, lift[2], lift[3])
        face = jnp.where(row >= 14, lift[1], jnp.where(row >= 12, lift[0], face))
        edge = jnp.where(row == 0, lift[0], jnp.where(row == 11, lift[1], 0.0))
        edge = jnp.where((row == 12) | (row == 14), lift[2], edge)
        edge = jnp.where((row == 13) | (row == 15), lift[3], edge)
        ghosts[j] = x_in[j] + face * g_in[j, 16:32] + edge * g_in[j, 32:48]
        y_out[j] = faces[info[SEND_Y] + j]


def refine_kernel(
    info, e_in, g, start, faces_in, x_in, y_in, u_in, spread, u, faces, x_out, y_out, table, coarse, rest
):
    fill_table(info, table, x_in, faces_in, y_in)
    for k in range(CAP_NEW):
        field = e_in[k]
        ghosts = ghosts_of(COARSE, info, table, k, 0)
        coarse[k] = KEEP * field + (start[k] + neighbour_sum(COARSE, field, g.at[k], ghosts))
    total = sum(
        jnp.dot(part, spread[...], preferred_element_type=F32)
        for part in split_two(coarse[...].reshape(CAP_NEW * 16, 256))
    )
    for k in range(CAP_NEW):
        twelve = total[16 * k : 16 * k + 12, :]
        for t in range(FINE.tiles):
            part = slice(128 * t, 128 * t + 128)
            rest[t, pl.ds(0, 12, stride=2), :] = twelve[:, part]
            rest[t, pl.ds(1, 12, stride=2), :] = twelve[:, part]
        new = u_in[k] + jnp.concatenate([rest[t] for t in range(FINE.tiles)], axis=1)
        u[k] = new
        pack_faces(FINE, new, faces, k, 0)
    send_faces(info, faces, x_out, y_out)


def last_kernel(info, u_in, g, start, faces_in, x_in, y_in, out, table):
    fill_table(info, table, x_in, faces_in, y_in)
    for k in range(CAP_NEW):
        field = u_in[k]
        ghosts = ghosts_of(FINE, info, table, k, 0)
        new = KEEP * field + (start[k] + neighbour_sum(FINE, field, g.at[k], ghosts))
        out[k] = jnp.where(k < info[HELD], new[:, 0:576], 0.0)


def sds(*shape):
    return jax.ShapeDtypeStruct(shape, F32)


SMEM = pl.BlockSpec(memory_space=pltpu.SMEM)
VMEM = pl.BlockSpec(memory_space=pltpu.VMEM)
HBM = pl.BlockSpec(memory_space=pltpu.HBM)


def call(kernel, name, outs, scratch, args, in_specs=None, out_specs=None):
    many = len(outs) > 1
    return pl.pallas_call(
        kernel,
        out_shape=outs if many else outs[0],
        in_specs=in_specs or [SMEM] + [VMEM] * (len(args) - 1),
        out_specs=out_specs or ([VMEM] * len(outs) if many else VMEM),
        scratch_shapes=[pltpu.VMEM(s, F32) if isinstance(s, tuple) else s for s in scratch],
        cost_estimate=pl.CostEstimate(flops=10_000_000, bytes_accessed=4_000_000, transcendentals=0),
        compiler_params=pltpu.CompilerParams(vmem_limit_bytes=24 * 1024 * 1024),
        name=name,
    )(*args)


def swap(block, axis, first):
    starts = range(first, lax.axis_size(axis) - 1, 2)
    return lax.ppermute(block, axis, [(i, i + 1) for i in starts] + [(i + 1, i) for i in starts])


def exchange(x_out, y_out):
    x_in = swap(x_out, AXES, 1)
    return x_in, swap(y_out, AXES, 0)


def face_outs(rows):
    return [sds(CAP_NEW, rows, 128), sds(REACH, rows, 128), sds(REACH, rows, 128)]


def body(rhs_old, coef_old, old_owner, new_owner, neighbours, coarse_map):
    near = jnp.transpose(neighbours[0])
    rhs_old, coef_old, new_owner, old_owner, near, coarse_map = (
        pltpu.with_memory_space_constraint(a, pltpu.HBM)
        for a in (rhs_old, coef_old, new_owner, old_owner, near, coarse_map)
    )
    pair, old = sds(2, 24, 576), sds(CAP_OLD, 24, 576)
    y_out, x_out, info, rhs_old, coef_old = call(
        first_kernel, "owners",
        [pair, pair, jax.ShapeDtypeStruct((128,), I32), old, old],
        [
            pltpu.VMEM((1, 128), I32), pltpu.VMEM((1, 128), I32),
            pltpu.SMEM((4, 128), I32), pltpu.SMEM((1, 128), I32),
            pltpu.SemaphoreType.DMA((6,)),
        ],
        (new_owner, old_owner, near, coarse_map, rhs_old, coef_old),
        [HBM] * 6, [VMEM, VMEM, SMEM, VMEM, VMEM],
    )
    y_in, x_in = swap(y_out, "curve", 0), swap(x_out, "curve", 1)

    fine = sds(CAP_NEW, 24, FINE.width)
    coarse = sds(CAP_NEW, 16, 256)
    fine_table = [(ABSENT + 1, FINE.face_rows, 128)]
    coarse_table = [(ABSENT + 1, COARSE.face_rows, 128)]
    fine_faces, coarse_faces = face_outs(FINE.face_rows), face_outs(COARSE.face_rows)
    sums = (2, CAP_NEW * 24, 128)

    source, coef = call(place_kernel, "place", [fine, fine], [], (info, rhs_old, coef_old))
    coef, faces, x_out, y_out = call(
        collect_kernel, "collect", [fine] + fine_faces, [], (info, coef, y_in, x_in)
    )
    source, level, coarse_own, spread = call(
        level_kernel, "level",
        [fine, coarse, coarse_faces[0], jax.ShapeDtypeStruct((256, FINE.width), jnp.bfloat16)],
        [sums],
        (info, source, y_in, x_in, coef),
    )
    x_in, y_in = exchange(x_out, y_out)
    fine_g, fine_s, fine_d, u, faces, x_out, y_out = call(
        conduct_kernel, "conduct",
        [sds(CAP_NEW, 6, 24, FINE.width), fine, fine, fine] + face_outs(BOTH_ROWS), fine_table,
        (info, source, coef, faces, coarse_own, x_in, y_in),
    )
    x_in, y_in = exchange(x_out, y_out)
    coarse_g, coarse_w, coarse_d, g_faces, row = call(
        coarse_conduct_kernel, "coarse_conduct",
        [sds(CAP_NEW, 6, 16, 256), coarse, coarse, sds(CAP_NEW, 32, 128), sds(1, 128)],
        [(ABSENT + 1, BOTH_ROWS, 128)],
        (info, level, faces, x_in, y_in),
    )
    u0, faces, x_out, y_out = call(
        lambda *refs: sweep_kernel(FINE, *refs), "pre", [fine, *fine_faces],
        [(ABSENT + 1, BOTH_ROWS, 128)],
        (info, u, fine_g, fine_s, faces, x_in, y_in),
    )

    def sweep(lev, u, g, start, faces, x_out, y_out, name):
        x_in, y_in = exchange(x_out, y_out)
        return call(
            lambda *refs: sweep_kernel(lev, *refs), name,
            [fine, *fine_faces] if lev is FINE else [coarse, *coarse_faces],
            fine_table if lev is FINE else coarse_table,
            (info, u, g, start, faces, x_in, y_in),
        )

    x_in, y_in = exchange(x_out, y_out)
    coarse_s, faces, x_out, y_out = call(
        residual_kernel, "residual",
        [coarse, coarse_faces[0], sds(REACH, 48, 128), coarse_faces[2]],
        fine_table + [(CAP_NEW, 24, FINE.width), sums],
        (info, u0, fine_g, fine_s, fine_d, coarse_w, spread, g_faces, faces, x_in, y_in),
    )
    g_in, y_in = exchange(x_out, y_out)
    e, faces, x_out, y_out = call(
        lambda *refs: sweep_kernel(COARSE, *refs), "coarse_pre", [coarse, *coarse_faces],
        coarse_table, (info, coarse_s, coarse_g, coarse_s, faces, g_in, y_in),
    )
    x_in, y_in = exchange(x_out, y_out)
    rows = call(
        total_kernel, "totals", [sds(NCOARSE, 128)], coarse_table,
        (info, e, coarse_g, coarse_s, coarse_d, row, faces, x_in, y_in),
    )
    rows = lax.all_to_all(rows, "curve", 0, 0, tiled=True)
    e, answer, faces, x_out = call(
        solve_kernel, "solve", [coarse, sds(NCOARSE, 128), *coarse_faces[:2]], coarse_table,
        (info, rows, e, coarse_g, coarse_s, faces, x_in, y_in),
    )
    x_in = swap(x_out, AXES, 1)
    e, faces, x_in, y_out = call(
        across_kernel, "across", [coarse, *coarse_faces], [(REACH + 1, 16, 128)],
        (info, e, coarse_g, answer, x_in, g_in),
    )
    y_in = swap(y_out, AXES, 0)
    u, faces, x_out, y_out = call(
        refine_kernel, "refine", [fine, *fine_faces],
        coarse_table + [(CAP_NEW, 16, 256), (FINE.tiles, 24, 128)],
        (info, e, coarse_g, coarse_s, faces, x_in, y_in, u0, spread),
    )
    u, faces, x_out, y_out = sweep(FINE, u, fine_g, fine_s, faces, x_out, y_out, "post")
    x_in, y_in = exchange(x_out, y_out)
    return call(
        last_kernel, "last", [sds(CAP_NEW, 24, 576)], fine_table,
        (info, u, fine_g, fine_s, faces, x_in, y_in),
    )


def solution(mesh):
    in_specs = (
        P(("group", "curve"), None, None),
        P(("group", "curve"), None, None),
        P("group", None),
        P("group", None),
        P("group", None, None),
        P("group", None),
    )
    out_specs = P(("group", "curve"), None, None)
    return jax.shard_map(body, mesh=mesh, in_specs=in_specs, out_specs=out_specs, check_vma=False)
```

```python
import jax
import jax.numpy as jnp
from jax import lax
from jax.experimental import pallas as pl
from jax.experimental.pallas import tpu as pltpu
from jax.sharding import PartitionSpec as P

OMEGA = 0.8
KEEP = 1.0 - OMEGA
CAP_OLD = 7
CAP_NEW = 5
REACH = 3
NBG = 128
NCOARSE = 32
AXES = ("group", "curve")
F32 = jnp.float32
I32 = jnp.int32

HELD, PICK, TABLE, CELL, BAND = 0, 1, 8, 32, 40
SEND_X, SEND_Y, AT_X, AT_Y = 64, 65, 66, 67
SPARE, OTHER, BESIDE, FACING = 7, 72, 96, 116
OPPOSITE = (1, 0, 3, 2)
LIFT_ROW = 13
ABSENT = 2 * REACH + CAP_NEW


class Level:
    def __init__(self, side, rows, width, high_at, x_low, x_high, face_rows, factor):
        self.side, self.rows, self.width = side, rows, width
        self.last = side * side - side - (width - 128)
        self.high_at = high_at
        self.x_low, self.x_high, self.face_rows = x_low, x_high, face_rows
        self.tiles = width // 128
        self.factor = factor


FINE = Level(24, 24, 640, 40, 24, 32, 40, 1.0)
COARSE = Level(12, 16, 256, 68, 12, 14, 16, 0.25)
BOTH_ROWS = FINE.face_rows + COARSE.face_rows


def iota(shape, axis):
    return lax.broadcasted_iota(I32, shape, axis)


def over(value, side):
    return (value * 43691) >> (20 if side == 24 else 19)


def pack_faces(lev, field, faces, k, base):
    pack_fields(lev, field, field, faces, k, base)


def pack_fields(lev, y_field, x_field, faces, k, base, y_high=None, x_high=None):
    y_high = y_field if y_high is None else y_high
    x_high = x_field if x_high is None else x_high
    lane = iota((lev.rows, 128), 1)
    tail = y_high[:, lev.width - 128 :]
    move = lev.high_at - lev.last
    if move:
        tail = pltpu.roll(tail, move, 1)
    faces[k, base : base + lev.rows, :] = jnp.where(lane < lev.side, y_field[:, :128], tail)
    for j in range(lev.tiles):
        part = slice(128 * j, 128 * j + 128)
        low, high = base + lev.x_low + j, base + lev.x_high + j
        faces[k, low : low + 1, :] = x_field[0:1, part]
        faces[k, high : high + 1, :] = x_high[lev.side - 1 : lev.side, part]


def send_faces(info, faces, x_out, y_out):
    x_first, y_first = info[SEND_X], info[SEND_Y]
    for j in range(REACH):
        x_out[j] = faces[x_first + j]
        y_out[j] = faces[y_first + j]


def fill_table(info, table, x_in, faces, y_in):
    x_first, y_first = info[AT_X], info[AT_Y]
    for j in range(REACH):
        table[x_first + j] = x_in[j, 0 : table.shape[1]]
        table[y_first + j] = y_in[j]
    table[REACH : REACH + CAP_NEW] = faces[...]
    table[ABSENT] = jnp.zeros(table.shape[1:], F32)


def x_line(lev, table, slot, first):
    return jnp.concatenate([table[slot, pl.ds(first + j, 1), :] for j in range(lev.tiles)], axis=1)


def ghosts_of(lev, info, table, k, base):
    row = [info[TABLE + 4 * k + f] for f in range(4)]
    x_low = x_line(lev, table, row[0], base + lev.x_high)
    x_high = x_line(lev, table, row[1], base + lev.x_low)
    y_low = pltpu.roll(table[row[2], pl.ds(base, lev.rows), :], 128 - lev.high_at, 1)
    y_high = pltpu.roll(table[row[3], pl.ds(base, lev.rows), :], lev.last, 1)
    return row, x_low, x_high, y_low, y_high


def interior_sum(lev, field, g):
    rows, width, side = lev.rows, lev.width, lev.side
    row = iota((rows, width), 0)
    total = g[0] * pltpu.roll(field, 1, 1) + g[1] * pltpu.roll(field, width - 1, 1)
    total += g[2] * pltpu.roll(field, side, 1) + g[3] * pltpu.roll(field, width - side, 1)
    total += g[4] * jnp.where(row == 0, 0.0, pltpu.roll(field, 1, 0))
    return total + g[5] * jnp.where(row == side - 1, 0.0, pltpu.roll(field, rows - 1, 0))


def add_ghosts(lev, out, g, ghosts):
    _, x_low, x_high, y_low, y_high = ghosts
    last, tail = lev.side - 1, lev.width - 128
    lane = iota((lev.rows, 128), 1)
    on_high = (lane >= lev.last) & (lane < lev.last + lev.side)
    out[0:1, :] += g[4, 0:1, :] * x_low
    out[last : last + 1, :] += g[5, last : last + 1, :] * x_high
    out[:, 0:128] += jnp.where(lane < lev.side, g[2, :, 0:128] * y_low, 0.0)
    out[:, tail:] += jnp.where(on_high, g[3, :, tail:] * y_high, 0.0)


def inner_kernel(u_in, g, start, part):
    for k in range(CAP_NEW):
        field = u_in[k]
        part[k] = KEEP * field + (start[k] + interior_sum(FINE, field, g.at[k]))


def neighbour_sum(lev, field, g, ghosts):
    _, x_low, x_high, y_low, y_high = ghosts
    rows, width, side = lev.rows, lev.width, lev.side
    row = iota((rows, width), 0)
    lane = iota((rows, 128), 1)
    total = g[0] * pltpu.roll(field, 1, 1) + g[1] * pltpu.roll(field, width - 1, 1)
    total += g[2] * pltpu.roll(field, side, 1) + g[3] * pltpu.roll(field, width - side, 1)
    total += g[4] * jnp.where(row == 0, x_low, pltpu.roll(field, 1, 0))
    total += g[5] * jnp.where(row == side - 1, x_high, pltpu.roll(field, rows - 1, 0))
    low = jnp.where(lane < side, g[2][:, :128] * y_low, 0.0)
    on_high = (lane >= lev.last) & (lane < lev.last + side)
    high = jnp.where(on_high, g[3][:, width - 128 :] * y_high, 0.0)
    parts = [low, high]
    if width > 256:
        parts = [low, jnp.zeros((rows, width - 256), F32), high]
    return total + jnp.concatenate(parts, axis=1)


def conductances(lev, cell, ghosts):
    present, x_low, x_high, y_low, y_high = ghosts
    present = [p != ABSENT for p in present]
    rows, width, side = lev.rows, lev.width, lev.side
    row, lane = iota((rows, width), 0), iota((rows, width), 1)
    depth = lane - side * over(lane, side)
    last = side - 1
    end = side * side
    x_low = jnp.where(present[0], x_low, cell[0:1, :])
    x_high = jnp.where(present[1], x_high, cell[last : last + 1, :])
    y_low = jnp.where(present[2], y_low, cell[:, :128])
    y_high = jnp.where(present[3], y_high, cell[:, width - 128 :])
    spare = jnp.ones((rows, width - 128), F32)
    y_low = jnp.concatenate([y_low, spare], axis=1)
    y_high = jnp.concatenate([spare, y_high], axis=1)
    high_y = (lane >= end - side) & (lane < end)
    across = [
        jnp.where(depth == 0, cell, pltpu.roll(cell, 1, 1)),
        jnp.where(depth == last, cell, pltpu.roll(cell, width - 1, 1)),
        jnp.where(lane < side, y_low, pltpu.roll(cell, side, 1)),
        jnp.where(high_y, y_high, pltpu.roll(cell, width - side, 1)),
        jnp.where(row == 0, x_low, pltpu.roll(cell, 1, 0)),
        jnp.where(row == last, x_high, pltpu.roll(cell, rows - 1, 0)),
    ]
    q = [2.0 * cell * other / (cell + other) * lev.factor for other in across]
    diagonal = q[0] + q[1] + q[2] + q[3] + q[4] + q[5]
    inside = (lane < end) & (row < side)
    weight = jnp.where(inside, OMEGA / diagonal, 0.0)
    g = [weight * one for one in q]
    g[0] = jnp.where(depth == 0, 0.0, g[0])
    g[1] = jnp.where(depth == last, 0.0, g[1])
    masks = (row, lane, depth, inside, high_y)
    return q, g, weight, diagonal, masks


def both_totals(values):
    return jnp.sum(jnp.sum(values, axis=0, keepdims=True), axis=1, keepdims=True)


def spread_matrix():
    lane = iota((1, FINE.width), 1)
    y = over(lane, 24)
    group = 12 * (y >> 1) + ((lane - 24 * y) >> 1)
    group = jnp.where(lane < 576, group, -1)
    return (iota((COARSE.width, FINE.width), 0) == group).astype(F32).astype(jnp.bfloat16)


def split_three(values):
    high, rest = values.astype(jnp.bfloat16), values - values.astype(jnp.bfloat16).astype(F32)
    mid = rest.astype(jnp.bfloat16)
    return high, mid, (rest - mid.astype(F32)).astype(jnp.bfloat16)


def split_two(values):
    high = values.astype(jnp.bfloat16)
    return high, (values - high.astype(F32)).astype(jnp.bfloat16)


def coarsen_blocks(fine, spread, scratch):
    total = sum(
        lax.dot_general(part, spread, (((1,), (1,)), ((), ())), preferred_element_type=F32)
        for part in split_two(fine)
    )
    scratch[0] = total[:, :128]
    scratch[1] = total[:, 128:]


def coarse_rows(scratch, k):
    even, odd = pl.ds(24 * k, 12, stride=2), pl.ds(24 * k + 1, 12, stride=2)
    halves = [scratch[t, even, :] + scratch[t, odd, :] for t in range(2)]
    return 0.125 * jnp.concatenate(halves, axis=1)


def first_kernel(
    new_in, old_in, near_in, map_in, rhs_in, coef_in,
    y_out, x_out, info, rhs_ref, coef_ref, new_ref, old_ref, near_ref, map_ref, sems,
):
    pairs = (
        (new_in, new_ref), (old_in, old_ref), (near_in, near_ref), (map_in, map_ref),
        (rhs_in, rhs_ref), (coef_in, coef_ref),
    )
    copies = [pltpu.make_async_copy(a, b, sems.at[i]) for i, (a, b) in enumerate(pairs)]
    for copy in copies:
        copy.start()
    curve = lax.axis_index("curve")
    group = lax.axis_index("group")
    up = lax.rem(curve, 2) == 1
    for copy in copies[:4]:
        copy.wait()
    new, old = new_ref[...], old_ref[...]

    def count(mask):
        return jnp.sum(jnp.where(mask, 1.0, 0.0)).astype(I32)

    new_first, held = count(new < curve), count(new == curve)
    old_first, old_count = count(old < curve), count(old == curve)
    last = jnp.clip(old_count - 1, 0, CAP_OLD - 1)
    x_slot, y_slot = jnp.where(up, last, 0), jnp.where(up, 0, last)
    for copy in copies[4:]:
        copy.wait()
    x_out[0] = rhs_ref[x_slot]
    x_out[1] = coef_ref[x_slot]
    y_out[0] = rhs_ref[y_slot]
    y_out[1] = coef_ref[y_slot]
    info[HELD] = held
    final = jnp.maximum(held - REACH, 0)
    info[SEND_X], info[SEND_Y] = jnp.where(up, final, 0), jnp.where(up, 0, final)
    info[AT_X] = jnp.where(up, REACH + CAP_NEW, 0)
    info[AT_Y] = jnp.where(up, 0, REACH + CAP_NEW)
    for i in range(4 * REACH):
        info[FACING + i] = -1
    x_at = jnp.where(up, REACH + CAP_NEW, 0)
    from_next, from_previous = jnp.where(up, 0, CAP_OLD + 1), jnp.where(up, CAP_OLD + 1, 0)
    first_id = group * NBG + new_first
    finish = first_id + held
    for k in range(CAP_NEW):
        block = new_first + k
        pick = jnp.where(block >= old_first + old_count, from_next, 1 + block - old_first)
        pick = jnp.where(block < old_first, from_previous, pick)
        info[PICK + k] = jnp.clip(pick, 0, CAP_OLD + 1)
        occupied = k < held
        safe = jnp.clip(block, 0, NBG - 1)
        cell = map_ref[0, safe]
        info[CELL + k] = jnp.where(occupied, cell, -1)
        for f in range(4):
            near = near_ref[f, safe]
            present = occupied & (near >= 0)
            slot = jnp.where(near >= finish, REACH + CAP_NEW - finish, REACH - first_id) + near
            slot = jnp.clip(slot, 0, ABSENT - 1)
            info[TABLE + 4 * k + f] = jnp.where(present, slot, ABSENT)
            local = near - group * NBG
            inside = present & (local >= 0) & (local < NBG)
            other = map_ref[0, jnp.clip(local, 0, NBG - 1)]
            info[BAND + 4 * k + f] = jnp.where(inside, 8 * k + 3 + other - cell, -1)
            info[BESIDE + 4 * k + f] = jnp.where(inside, other, -1)
            outside = present & jnp.logical_not(inside)
            place = jnp.clip(slot - x_at, 0, REACH - 1)
            info[OTHER + 4 * k + f] = jnp.where(outside, place, REACH)
            info[jnp.where(outside, FACING + 4 * place + OPPOSITE[f], SPARE)] = cell


def place_kernel(info, rhs_ref, coef_ref, source, coef):
    source[...] = jnp.zeros(source.shape, F32)
    coef[...] = jnp.ones(coef.shape, F32)
    for k in range(CAP_NEW):
        slot = jnp.clip(info[PICK + k] - 1, 0, CAP_OLD - 1)
        occupied = k < info[HELD]
        source[k, :, 0:576] = jnp.where(occupied, rhs_ref[slot], 0.0)
        coef[k, :, 0:576] = jnp.where(occupied, coef_ref[slot], 1.0)


def patched(info, field, i, k, x_in, y_in):
    pick = info[PICK + k]
    occupied = k < info[HELD]
    block = jnp.where(occupied & (pick == 0), x_in[i], field[k, :, 0:576])
    return jnp.where(occupied & (pick == CAP_OLD + 1), y_in[i], block)


def collect_kernel(info, kept, y_in, x_in, coef, faces, x_out, y_out):
    coef[...] = kept[...]
    for k in range(CAP_NEW):
        coef[k, :, 0:576] = patched(info, kept, 1, k, x_in, y_in)
        pack_faces(FINE, coef[k], faces, k, 0)
    send_faces(info, faces, x_out, y_out)


def level_kernel(info, kept, y_in, x_in, coef, source, level, faces, spread, scratch):
    source[...] = kept[...]
    for k in range(CAP_NEW):
        source[k, :, 0:576] = patched(info, kept, 0, k, x_in, y_in)
    spread[...] = spread_matrix()
    coarsen_blocks(coef[...].reshape(CAP_NEW * 24, FINE.width), spread[...], scratch)
    row, lane = iota((16, 256), 0), iota((16, 256), 1)
    for k in range(CAP_NEW):
        level[k] = jnp.ones((16, 256), F32)
        level[k, 0:12, :] = coarse_rows(scratch, k)
        level[k] = jnp.where((row < 12) & (lane < 144), level[k], 1.0)
        pack_faces(COARSE, level[k], faces, k, 0)


def conduct_kernel(
    info, source, coef, faces_in, coarse_faces, x_in, y_in,
    fine_g, fine_s, fine_d, u, faces, x_out, y_out, table,
):
    fill_table(info, table, x_in, faces_in, y_in)
    for k in range(CAP_NEW):
        ghosts = ghosts_of(FINE, info, table, k, 0)
        _, g, weight, diagonal, _ = conductances(FINE, coef[k], ghosts)
        for i in range(6):
            fine_g[k, i] = g[i]
        fine_d[k] = (1.0 / OMEGA) * diagonal
        start = weight * source[k]
        fine_s[k] = start
        u[k] = start
        pack_faces(FINE, start, faces, k, 0)
    faces[:, FINE.face_rows : BOTH_ROWS, :] = coarse_faces[...]
    send_faces(info, faces, x_out, y_out)


def coarse_conduct_kernel(
    info, level, faces_in, x_in, y_in, coarse_g, coarse_w, coarse_d, alpha, g_faces, row_out, table
):
    fill_table(info, table, x_in, faces_in, y_in)
    lane_row = iota((1, 128), 1)
    band = jnp.zeros((1, 128), F32)
    for k in range(CAP_NEW):
        ghosts = ghosts_of(COARSE, info, table, k, FINE.face_rows)
        q, g, weight, diagonal, masks = conductances(COARSE, level[k], ghosts)
        row, lane, depth, inside, high_y = masks
        for i in range(6):
            coarse_g[k, i] = g[i]
        coarse_w[k] = weight
        one = g[0] + g[1]
        one += jnp.where(lane < 12, 0.0, g[2]) + jnp.where(high_y, 0.0, g[3])
        one += jnp.where(row == 0, 0.0, g[4]) + jnp.where(row == 11, 0.0, g[5])
        alpha[k] = jnp.where(inside, KEEP + one, 0.0)
        pack_fields(COARSE, g[2], g[4], g_faces, k, 0, g[3], g[5])
        low_y = jnp.where(lane < 12, g[2], 0.0)
        x_edge = jnp.where(lane >= 132, g[3], low_y)
        y_edge = jnp.where(row == 0, g[4], jnp.where(row == 11, g[5], 0.0))
        pack_fields(COARSE, y_edge, x_edge, g_faces, k, 16)
        coarse_d[k] = (1.0 / OMEGA) * diagonal
        face = [
            both_totals(jnp.where(inside & (row == 0), q[4], 0.0)),
            both_totals(jnp.where(inside & (row == 11), q[5], 0.0)),
            both_totals(jnp.where(inside & (lane < 12), q[2], 0.0)),
            both_totals(jnp.where(inside & high_y, q[3], 0.0)),
        ]
        ends = jnp.where(inside & (depth == 0), q[0], 0.0)
        ends += jnp.where(inside & (depth == 11), q[1], 0.0)
        surface = face[0] + face[1] + face[2] + face[3] + both_totals(ends)
        occupied = k < info[HELD]
        band += jnp.where((lane_row == 8 * k + 3) & occupied, surface, 0.0)
        for f in range(4):
            band -= jnp.where(lane_row == info[BAND + 4 * k + f], face[f], 0.0)
        band += jnp.where(lane_row == 64 + k, info[CELL + k].astype(F32), 0.0)
    row_out[...] = band


def sweep_kernel(info, u_in, g, start, faces_in, x_in, y_in, u, faces, x_out, y_out, table):
    fill_table(info, table, x_in, faces_in, y_in)
    for k in range(CAP_NEW):
        field = u_in[k]
        ghosts = ghosts_of(COARSE, info, table, k, 0)
        new = KEEP * field + (start[k] + neighbour_sum(COARSE, field, g.at[k], ghosts))
        u[k] = new
        pack_faces(COARSE, new, faces, k, 0)
    send_faces(info, faces, x_out, y_out)


def finish_kernel(info, part, g, faces_in, x_in, y_in, u, faces, x_out, y_out, table):
    fill_table(info, table, x_in, faces_in, y_in)
    for k in range(CAP_NEW):
        u[k] = part[k]
        add_ghosts(FINE, u.at[k], g.at[k], ghosts_of(FINE, info, table, k, 0))
        pack_faces(FINE, u[k], faces, k, 0)
    send_faces(info, faces, x_out, y_out)


def residual_kernel(
    info, u_in, part, g, diagonal, weight, spread, g_faces, faces_in, x_in, y_in,
    coarse_s, faces, x_out, y_out, table, rest, scratch,
):
    fill_table(info, table, x_in, faces_in, y_in)
    for k in range(CAP_NEW):
        rest[k] = part[k]
        add_ghosts(FINE, rest.at[k], g.at[k], ghosts_of(FINE, info, table, k, 0))
        rest[k] = diagonal[k] * (rest[k] - u_in[k])
    coarsen_blocks(rest[...].reshape(CAP_NEW * 24, FINE.width), spread[...], scratch)
    for k in range(CAP_NEW):
        coarse_s[k] = jnp.zeros((16, 256), F32)
        coarse_s[k, 0:12, :] = weight[k, 0:12, :] * coarse_rows(scratch, k)
        pack_faces(COARSE, coarse_s[k], faces, k, 0)
    x_first, y_first = info[SEND_X], info[SEND_Y]
    for j in range(REACH):
        x_out[j, 0:16] = faces[x_first + j]
        x_out[j, 16:48] = g_faces[x_first + j]
        y_out[j] = faces[y_first + j]


def total_kernel(
    info, u_in, g, start, diagonal, row_in, faces_in, x_in, y_in, rows_out, swept, table
):
    fill_table(info, table, x_in, faces_in, y_in)
    lane_row = iota((1, 128), 1)
    row, lane = iota((16, 256), 0), iota((16, 256), 1)
    inside = (row < 12) & (lane < 144)
    band = row_in[...]
    for k in range(CAP_NEW):
        field = u_in[k]
        ghosts = ghosts_of(COARSE, info, table, k, 0)
        inner = start[k] + neighbour_sum(COARSE, field, g.at[k], ghosts)
        swept[k] = KEEP * field + inner
        rest = jnp.where(inside, diagonal[k] * (inner - OMEGA * field), 0.0)
        occupied = k < info[HELD]
        band += jnp.where((lane_row == 8 * k + 7) & occupied, both_totals(rest), 0.0)
    rows_out[...] = jnp.broadcast_to(band, rows_out.shape)


def lifted(answer, cell):
    at = iota((NCOARSE, 128), 0)
    return jnp.sum(jnp.where(at == cell, answer, 0.0), axis=0, keepdims=True)


def wide(line):
    return jnp.concatenate([line, line], axis=1)


def surface_lift(g, lift):
    row, lane = iota((16, 256), 0), iota((16, 256), 1)
    total = jnp.where(row == 0, g[4] * lift[0], 0.0)
    total += jnp.where(row == 11, g[5] * lift[1], 0.0)
    total += jnp.where(lane < 12, g[2] * lift[2], 0.0)
    return total + jnp.where((lane >= 132) & (lane < 144), g[3] * lift[3], 0.0)


def solve_kernel(
    info, rows_in, swept, g, alpha, u, answer_out, faces, x_out
):
    rows = rows_in[...]
    shape = (NCOARSE, 128)
    row, lane = iota(shape, 0), iota(shape, 1)
    cells = iota((NCOARSE, NCOARSE), 1).astype(F32)
    member = jnp.concatenate(
        [(rows[:, 64 + k : 65 + k] == cells).astype(F32) for k in range(CAP_NEW)], axis=0
    ).astype(jnp.bfloat16)
    shifts = [rows] + [pltpu.roll(rows, 128 - 8 * k, 1) for k in range(1, CAP_NEW)]
    band = sum(
        lax.dot_general(member, part, (((0,), (0,)), ((), ())), preferred_element_type=F32)
        for part in split_three(jnp.concatenate(shifts, axis=0))
    )
    matrix = jnp.where(lane == 64, band[:, 7:8], 0.0)
    for o in range(7):
        matrix += jnp.where(lane == row + (o - REACH), band[:, o : o + 1], 0.0)

    lists = [[i for i in (t, 9 + t, 18 + t, 27 + t) if i < NCOARSE] for t in range(6)]
    lists += [[6 + t, 24 + t] for t in range(REACH)] + [[15 + t] for t in range(REACH)]
    for pivots in lists:
        drop = None
        for j in pivots:
            column = jnp.broadcast_to(matrix[:, j : j + 1], shape)
            scaled = matrix[j : j + 1, :] / column[j : j + 1, :]
            one = jnp.where(row == j, 0.0, column) * scaled
            drop = one if drop is None else drop + one
        matrix = matrix - drop
    pivots = jnp.sum(jnp.where(lane == row, matrix, 0.0), axis=1, keepdims=True)
    answer = jnp.broadcast_to(matrix[:, 64:65], shape) / jnp.broadcast_to(pivots, shape)
    answer_out[...] = answer
    for k in range(CAP_NEW):
        lift = lifted(answer, info[CELL + k])
        beside = [wide(lifted(answer, info[BESIDE + 4 * k + f])) for f in range(4)]
        new = swept[k] + wide(lift) * alpha[k] + surface_lift(g.at[k], beside)
        u[k] = new
        pack_faces(COARSE, new, faces, k, 0)
        faces[k, LIFT_ROW : LIFT_ROW + 1, 64:128] = lift[:, 64:128]
    for j in range(REACH):
        x_out[j] = faces[info[SEND_X] + j]


def across_kernel(
    info, u_in, g, answer_in, x_in, g_in, u, faces, ghosts, y_out, table
):
    table[0:REACH] = x_in[...]
    table[REACH] = jnp.zeros((16, 128), F32)
    answer = answer_in[...]
    upper = iota((1, 128), 1) >= 64
    for k in range(CAP_NEW):
        lift = [table[info[OTHER + 4 * k + f], pl.ds(LIFT_ROW, 1), :] for f in range(4)]
        lift = [wide(jnp.where(upper, line, pltpu.roll(line, 64, 1))) for line in lift]
        new = u_in[k] + surface_lift(g.at[k], lift)
        u[k] = new
        pack_faces(COARSE, new, faces, k, 0)
    row, lane = iota((16, 128), 0), iota((16, 128), 1)
    for j in range(REACH):
        lift = [lifted(answer, info[FACING + 4 * j + f]) for f in range(4)]
        face = jnp.where(lane < 64, lift[2], lift[3])
        face = jnp.where(row >= 14, lift[1], jnp.where(row >= 12, lift[0], face))
        edge = jnp.where(row == 0, lift[0], jnp.where(row == 11, lift[1], 0.0))
        edge = jnp.where((row == 12) | (row == 14), lift[2], edge)
        edge = jnp.where((row == 13) | (row == 15), lift[3], edge)
        ghosts[j] = x_in[j] + face * g_in[j, 16:32] + edge * g_in[j, 32:48]
        y_out[j] = faces[info[SEND_Y] + j]


def refine_kernel(
    info, e_in, g, start, faces_in, x_in, y_in, u_in, spread, u, faces, x_out, y_out, table, coarse, rest
):
    fill_table(info, table, x_in, faces_in, y_in)
    for k in range(CAP_NEW):
        field = e_in[k]
        ghosts = ghosts_of(COARSE, info, table, k, 0)
        coarse[k] = KEEP * field + (start[k] + neighbour_sum(COARSE, field, g.at[k], ghosts))
    total = sum(
        jnp.dot(part, spread[...], preferred_element_type=F32)
        for part in split_two(coarse[...].reshape(CAP_NEW * 16, 256))
    )
    for k in range(CAP_NEW):
        twelve = total[16 * k : 16 * k + 12, :]
        for t in range(FINE.tiles):
            part = slice(128 * t, 128 * t + 128)
            rest[t, pl.ds(0, 12, stride=2), :] = twelve[:, part]
            rest[t, pl.ds(1, 12, stride=2), :] = twelve[:, part]
        new = u_in[k] + jnp.concatenate([rest[t] for t in range(FINE.tiles)], axis=1)
        u[k] = new
        pack_faces(FINE, new, faces, k, 0)
    send_faces(info, faces, x_out, y_out)


def last_kernel(info, part, g, faces_in, x_in, y_in, out, table, u, block, sems):
    fill_table(info, table, x_in, faces_in, y_in)
    copies = [
        pltpu.make_async_copy(block.at[k], out.at[k], sems.at[k]) for k in range(CAP_NEW)
    ]
    for k in range(CAP_NEW):
        u[...] = part[k]
        add_ghosts(FINE, u, g.at[k], ghosts_of(FINE, info, table, k, 0))
        block[k] = jnp.where(k < info[HELD], u[:, 0:576], 0.0)
        copies[k].start()
    for copy in copies:
        copy.wait()


def sds(*shape):
    return jax.ShapeDtypeStruct(shape, F32)


SMEM = pl.BlockSpec(memory_space=pltpu.SMEM)
VMEM = pl.BlockSpec(memory_space=pltpu.VMEM)
HBM = pl.BlockSpec(memory_space=pltpu.HBM)


def call(kernel, name, outs, scratch, args, in_specs=None, out_specs=None):
    many = len(outs) > 1
    return pl.pallas_call(
        kernel,
        out_shape=outs if many else outs[0],
        in_specs=in_specs or [SMEM] + [VMEM] * (len(args) - 1),
        out_specs=out_specs or ([VMEM] * len(outs) if many else VMEM),
        scratch_shapes=[pltpu.VMEM(s, F32) if isinstance(s, tuple) else s for s in scratch],
        cost_estimate=pl.CostEstimate(flops=10_000_000, bytes_accessed=4_000_000, transcendentals=0),
        compiler_params=pltpu.CompilerParams(vmem_limit_bytes=24 * 1024 * 1024),
        name=name,
    )(*args)


def swap(block, axis, first):
    starts = range(first, lax.axis_size(axis) - 1, 2)
    return lax.ppermute(block, axis, [(i, i + 1) for i in starts] + [(i + 1, i) for i in starts])


def exchange(x_out, y_out):
    x_in = swap(x_out, AXES, 1)
    return x_in, swap(y_out, AXES, 0)


def face_outs(rows):
    return [sds(CAP_NEW, rows, 128), sds(REACH, rows, 128), sds(REACH, rows, 128)]


def body(rhs_old, coef_old, old_owner, new_owner, neighbours, coarse_map):
    near = jnp.transpose(neighbours[0])
    rhs_old, coef_old, new_owner, old_owner, near, coarse_map = (
        pltpu.with_memory_space_constraint(a, pltpu.HBM)
        for a in (rhs_old, coef_old, new_owner, old_owner, near, coarse_map)
    )
    pair, old = sds(2, 24, 576), sds(CAP_OLD, 24, 576)
    y_out, x_out, info, rhs_old, coef_old = call(
        first_kernel, "owners",
        [pair, pair, jax.ShapeDtypeStruct((128,), I32), old, old],
        [
            pltpu.VMEM((1, 128), I32), pltpu.VMEM((1, 128), I32),
            pltpu.SMEM((4, 128), I32), pltpu.SMEM((1, 128), I32),
            pltpu.SemaphoreType.DMA((6,)),
        ],
        (new_owner, old_owner, near, coarse_map, rhs_old, coef_old),
        [HBM] * 6, [VMEM, VMEM, SMEM, VMEM, VMEM],
    )
    y_in, x_in = swap(y_out, "curve", 0), swap(x_out, "curve", 1)

    fine = sds(CAP_NEW, 24, FINE.width)
    coarse = sds(CAP_NEW, 16, 256)
    fine_table = [(ABSENT + 1, FINE.face_rows, 128)]
    coarse_table = [(ABSENT + 1, COARSE.face_rows, 128)]
    fine_faces, coarse_faces = face_outs(FINE.face_rows), face_outs(COARSE.face_rows)
    sums = (2, CAP_NEW * 24, 128)

    source, coef = call(place_kernel, "place", [fine, fine], [], (info, rhs_old, coef_old))
    coef, faces, x_out, y_out = call(
        collect_kernel, "collect", [fine] + fine_faces, [], (info, coef, y_in, x_in)
    )
    source, level, coarse_own, spread = call(
        level_kernel, "level",
        [fine, coarse, coarse_faces[0], jax.ShapeDtypeStruct((256, FINE.width), jnp.bfloat16)],
        [sums],
        (info, source, y_in, x_in, coef),
    )
    x_in, y_in = exchange(x_out, y_out)
    fine_g, fine_s, fine_d, u, faces, x_out, y_out = call(
        conduct_kernel, "conduct",
        [sds(CAP_NEW, 6, 24, FINE.width), fine, fine, fine] + face_outs(BOTH_ROWS), fine_table,
        (info, source, coef, faces, coarse_own, x_in, y_in),
    )
    x_in, y_in = exchange(x_out, y_out)
    coarse_g, coarse_w, coarse_d, alpha, g_faces, row = call(
        coarse_conduct_kernel, "coarse_conduct",
        [sds(CAP_NEW, 6, 16, 256), coarse, coarse, coarse, sds(CAP_NEW, 32, 128), sds(1, 128)],
        [(ABSENT + 1, BOTH_ROWS, 128)],
        (info, level, faces, x_in, y_in),
    )

    def inner(u, name):
        return call(inner_kernel, name, [fine], [], (u, fine_g, fine_s), [VMEM] * 3)

    part = inner(u, "pre_inner")
    u0, faces, x_out, y_out = call(
        finish_kernel, "pre", [fine, *fine_faces], [(ABSENT + 1, BOTH_ROWS, 128)],
        (info, part, fine_g, faces, x_in, y_in),
    )
    x_in, y_in = exchange(x_out, y_out)
    part = inner(u0, "residual_inner")
    coarse_s, faces, x_out, y_out = call(
        residual_kernel, "residual",
        [coarse, coarse_faces[0], sds(REACH, 48, 128), coarse_faces[2]],
        fine_table + [(CAP_NEW, 24, FINE.width), sums],
        (info, u0, part, fine_g, fine_d, coarse_w, spread, g_faces, faces, x_in, y_in),
    )
    g_in, y_in = exchange(x_out, y_out)
    e, faces, x_out, y_out = call(
        sweep_kernel, "coarse_pre", [coarse, *coarse_faces],
        coarse_table, (info, coarse_s, coarse_g, coarse_s, faces, g_in, y_in),
    )
    x_in, y_in = exchange(x_out, y_out)
    rows, swept = call(
        total_kernel, "totals", [sds(NCOARSE, 128), coarse], coarse_table,
        (info, e, coarse_g, coarse_s, coarse_d, row, faces, x_in, y_in),
    )
    rows = lax.all_to_all(rows, "curve", 0, 0, tiled=True)
    e, answer, faces, x_out = call(
        solve_kernel, "solve", [coarse, sds(NCOARSE, 128), *coarse_faces[:2]], [],
        (info, rows, swept, coarse_g, alpha),
    )
    x_in = swap(x_out, AXES, 1)
    e, faces, x_in, y_out = call(
        across_kernel, "across", [coarse, *coarse_faces], [(REACH + 1, 16, 128)],
        (info, e, coarse_g, answer, x_in, g_in),
    )
    y_in = swap(y_out, AXES, 0)
    u, faces, x_out, y_out = call(
        refine_kernel, "refine", [fine, *fine_faces],
        coarse_table + [(CAP_NEW, 16, 256), (FINE.tiles, 24, 128)],
        (info, e, coarse_g, coarse_s, faces, x_in, y_in, u0, spread),
    )
    x_in, y_in = exchange(x_out, y_out)
    part = inner(u, "post_inner")
    u, faces, x_out, y_out = call(
        finish_kernel, "post", [fine, *fine_faces], fine_table,
        (info, part, fine_g, faces, x_in, y_in),
    )
    x_in, y_in = exchange(x_out, y_out)
    part = inner(u, "last_inner")
    return call(
        last_kernel, "last", [sds(CAP_NEW, 24, 576)],
        fine_table
        + [(24, FINE.width), (CAP_NEW, 24, 576), pltpu.SemaphoreType.DMA((CAP_NEW,))],
        (info, part, fine_g, faces, x_in, y_in), None, pl.BlockSpec(memory_space=pl.ANY),
    )


def solution(mesh):
    in_specs = (
        P(("group", "curve"), None, None),
        P(("group", "curve"), None, None),
        P("group", None),
        P("group", None),
        P("group", None, None),
        P("group", None),
    )
    out_specs = P(("group", "curve"), None, None)
    return jax.shard_map(body, mesh=mesh, in_specs=in_specs, out_specs=out_specs, check_vma=False)
```

```python
import jax
import jax.numpy as jnp
from jax import lax
from jax.experimental import pallas as pl
from jax.experimental.pallas import tpu as pltpu
from jax.sharding import PartitionSpec as P

OMEGA = 0.8
KEEP = 1.0 - OMEGA
CAP_OLD = 7
CAP_NEW = 5
REACH = 3
NBG = 128
NCOARSE = 32
AXES = ("group", "curve")
F32 = jnp.float32
I32 = jnp.int32

HELD, PICK, TABLE, CELL, BAND = 0, 1, 8, 32, 40
SEND_X, SEND_Y, AT_X, AT_Y = 64, 65, 66, 67
SPARE, OTHER, BESIDE, FACING = 7, 72, 96, 116
OPPOSITE = (1, 0, 3, 2)
LIFT_ROW = 13
ABSENT = 2 * REACH + CAP_NEW


class Level:
    def __init__(self, side, rows, width, high_at, x_low, x_high, face_rows, factor):
        self.side, self.rows, self.width = side, rows, width
        self.last = side * side - side - (width - 128)
        self.high_at = high_at
        self.x_low, self.x_high, self.face_rows = x_low, x_high, face_rows
        self.tiles = width // 128
        self.factor = factor


FINE = Level(24, 24, 640, 40, 24, 32, 40, 1.0)
COARSE = Level(12, 16, 256, 68, 12, 14, 16, 0.25)
BOTH_ROWS = FINE.face_rows + COARSE.face_rows


def iota(shape, axis):
    return lax.broadcasted_iota(I32, shape, axis)


def over(value, side):
    return (value * 43691) >> (20 if side == 24 else 19)


def pack_faces(lev, field, faces, k, base):
    pack_fields(lev, field, field, faces, k, base)


def pack_fields(lev, y_field, x_field, faces, k, base, y_high=None, x_high=None):
    y_high = y_field if y_high is None else y_high
    x_high = x_field if x_high is None else x_high
    lane = iota((lev.rows, 128), 1)
    tail = y_high[:, lev.width - 128 :]
    move = lev.high_at - lev.last
    if move:
        tail = pltpu.roll(tail, move, 1)
    faces[k, base : base + lev.rows, :] = jnp.where(lane < lev.side, y_field[:, :128], tail)
    for j in range(lev.tiles):
        part = slice(128 * j, 128 * j + 128)
        low, high = base + lev.x_low + j, base + lev.x_high + j
        faces[k, low : low + 1, :] = x_field[0:1, part]
        faces[k, high : high + 1, :] = x_high[lev.side - 1 : lev.side, part]


def send_faces(info, faces, x_out, y_out):
    x_first, y_first = info[SEND_X], info[SEND_Y]
    for j in range(REACH):
        x_out[j] = faces[x_first + j]
        y_out[j] = faces[y_first + j]


def fill_table(info, table, x_in, faces, y_in):
    x_first, y_first = info[AT_X], info[AT_Y]
    for j in range(REACH):
        table[x_first + j] = x_in[j, 0 : table.shape[1]]
        table[y_first + j] = y_in[j]
    table[REACH : REACH + CAP_NEW] = faces[...]
    table[ABSENT] = jnp.zeros(table.shape[1:], F32)


def x_line(lev, table, slot, first):
    return jnp.concatenate([table[slot, pl.ds(first + j, 1), :] for j in range(lev.tiles)], axis=1)


def ghosts_of(lev, info, table, k, base):
    row = [info[TABLE + 4 * k + f] for f in range(4)]
    x_low = x_line(lev, table, row[0], base + lev.x_high)
    x_high = x_line(lev, table, row[1], base + lev.x_low)
    y_low = pltpu.roll(table[row[2], pl.ds(base, lev.rows), :], 128 - lev.high_at, 1)
    y_high = pltpu.roll(table[row[3], pl.ds(base, lev.rows), :], lev.last, 1)
    return row, x_low, x_high, y_low, y_high


def interior_sum(lev, field, g):
    rows, width, side = lev.rows, lev.width, lev.side
    row = iota((rows, width), 0)
    total = g[0] * pltpu.roll(field, 1, 1) + g[1] * pltpu.roll(field, width - 1, 1)
    total += g[2] * pltpu.roll(field, side, 1) + g[3] * pltpu.roll(field, width - side, 1)
    total += g[4] * jnp.where(row == 0, 0.0, pltpu.roll(field, 1, 0))
    return total + g[5] * jnp.where(row == side - 1, 0.0, pltpu.roll(field, rows - 1, 0))


def add_ghosts(lev, out, g, ghosts):
    _, x_low, x_high, y_low, y_high = ghosts
    last, tail = lev.side - 1, lev.width - 128
    lane = iota((lev.rows, 128), 1)
    on_high = (lane >= lev.last) & (lane < lev.last + lev.side)
    out[0:1, :] += g[4, 0:1, :] * x_low
    out[last : last + 1, :] += g[5, last : last + 1, :] * x_high
    out[:, 0:128] += jnp.where(lane < lev.side, g[2, :, 0:128] * y_low, 0.0)
    out[:, tail:] += jnp.where(on_high, g[3, :, tail:] * y_high, 0.0)


def inner_kernel(u_in, g, start, part):
    for k in range(CAP_NEW):
        field = u_in[k]
        part[k] = KEEP * field + (start[k] + interior_sum(FINE, field, g.at[k]))


def neighbour_sum(lev, field, g, ghosts):
    _, x_low, x_high, y_low, y_high = ghosts
    rows, width, side = lev.rows, lev.width, lev.side
    row = iota((rows, width), 0)
    lane = iota((rows, 128), 1)
    total = g[0] * pltpu.roll(field, 1, 1) + g[1] * pltpu.roll(field, width - 1, 1)
    total += g[2] * pltpu.roll(field, side, 1) + g[3] * pltpu.roll(field, width - side, 1)
    total += g[4] * jnp.where(row == 0, x_low, pltpu.roll(field, 1, 0))
    total += g[5] * jnp.where(row == side - 1, x_high, pltpu.roll(field, rows - 1, 0))
    low = jnp.where(lane < side, g[2][:, :128] * y_low, 0.0)
    on_high = (lane >= lev.last) & (lane < lev.last + side)
    high = jnp.where(on_high, g[3][:, width - 128 :] * y_high, 0.0)
    parts = [low, high]
    if width > 256:
        parts = [low, jnp.zeros((rows, width - 256), F32), high]
    return total + jnp.concatenate(parts, axis=1)


def conductances(lev, cell, ghosts):
    present, x_low, x_high, y_low, y_high = ghosts
    present = [p != ABSENT for p in present]
    rows, width, side = lev.rows, lev.width, lev.side
    row, lane = iota((rows, width), 0), iota((rows, width), 1)
    depth = lane - side * over(lane, side)
    last = side - 1
    end = side * side
    x_low = jnp.where(present[0], x_low, cell[0:1, :])
    x_high = jnp.where(present[1], x_high, cell[last : last + 1, :])
    y_low = jnp.where(present[2], y_low, cell[:, :128])
    y_high = jnp.where(present[3], y_high, cell[:, width - 128 :])
    spare = jnp.ones((rows, width - 128), F32)
    y_low = jnp.concatenate([y_low, spare], axis=1)
    y_high = jnp.concatenate([spare, y_high], axis=1)
    high_y = (lane >= end - side) & (lane < end)
    across = [
        jnp.where(depth == 0, cell, pltpu.roll(cell, 1, 1)),
        jnp.where(depth == last, cell, pltpu.roll(cell, width - 1, 1)),
        jnp.where(lane < side, y_low, pltpu.roll(cell, side, 1)),
        jnp.where(high_y, y_high, pltpu.roll(cell, width - side, 1)),
        jnp.where(row == 0, x_low, pltpu.roll(cell, 1, 0)),
        jnp.where(row == last, x_high, pltpu.roll(cell, rows - 1, 0)),
    ]
    q = [2.0 * cell * other / (cell + other) * lev.factor for other in across]
    diagonal = q[0] + q[1] + q[2] + q[3] + q[4] + q[5]
    inside = (lane < end) & (row < side)
    weight = jnp.where(inside, OMEGA / diagonal, 0.0)
    g = [weight * one for one in q]
    g[0] = jnp.where(depth == 0, 0.0, g[0])
    g[1] = jnp.where(depth == last, 0.0, g[1])
    masks = (row, lane, depth, inside, high_y)
    return q, g, weight, diagonal, masks


def both_totals(values):
    return jnp.sum(jnp.sum(values, axis=0, keepdims=True), axis=1, keepdims=True)


def spread_matrix():
    lane = iota((1, FINE.width), 1)
    y = over(lane, 24)
    group = 12 * (y >> 1) + ((lane - 24 * y) >> 1)
    group = jnp.where(lane < 576, group, -1)
    return (iota((COARSE.width, FINE.width), 0) == group).astype(F32).astype(jnp.bfloat16)


def split_three(values):
    high, rest = values.astype(jnp.bfloat16), values - values.astype(jnp.bfloat16).astype(F32)
    mid = rest.astype(jnp.bfloat16)
    return high, mid, (rest - mid.astype(F32)).astype(jnp.bfloat16)


def split_two(values):
    high = values.astype(jnp.bfloat16)
    return high, (values - high.astype(F32)).astype(jnp.bfloat16)


def coarsen_blocks(fine, spread, scratch):
    total = sum(
        lax.dot_general(part, spread, (((1,), (1,)), ((), ())), preferred_element_type=F32)
        for part in split_two(fine)
    )
    scratch[0] = total[:, :128]
    scratch[1] = total[:, 128:]


def coarse_rows(scratch, k):
    even, odd = pl.ds(24 * k, 12, stride=2), pl.ds(24 * k + 1, 12, stride=2)
    halves = [scratch[t, even, :] + scratch[t, odd, :] for t in range(2)]
    return 0.125 * jnp.concatenate(halves, axis=1)


def first_kernel(
    new_in, old_in, near_in, map_in, rhs_in, coef_in,
    y_out, x_out, info, rhs_ref, coef_ref, new_ref, old_ref, near_ref, map_ref, sems,
):
    pairs = (
        (new_in, new_ref), (old_in, old_ref), (near_in, near_ref), (map_in, map_ref),
        (rhs_in, rhs_ref), (coef_in, coef_ref),
    )
    copies = [pltpu.make_async_copy(a, b, sems.at[i]) for i, (a, b) in enumerate(pairs)]
    for copy in copies:
        copy.start()
    curve = lax.axis_index("curve")
    group = lax.axis_index("group")
    up = lax.rem(curve, 2) == 1
    for copy in copies[:4]:
        copy.wait()
    new, old = new_ref[...], old_ref[...]

    def count(mask):
        return jnp.sum(jnp.where(mask, 1.0, 0.0)).astype(I32)

    new_first, held = count(new < curve), count(new == curve)
    old_first, old_count = count(old < curve), count(old == curve)
    last = jnp.clip(old_count - 1, 0, CAP_OLD - 1)
    x_slot, y_slot = jnp.where(up, last, 0), jnp.where(up, 0, last)
    for copy in copies[4:]:
        copy.wait()
    x_out[0] = rhs_ref[x_slot]
    x_out[1] = coef_ref[x_slot]
    y_out[0] = rhs_ref[y_slot]
    y_out[1] = coef_ref[y_slot]
    info[HELD] = held
    final = jnp.maximum(held - REACH, 0)
    info[SEND_X], info[SEND_Y] = jnp.where(up, final, 0), jnp.where(up, 0, final)
    info[AT_X] = jnp.where(up, REACH + CAP_NEW, 0)
    info[AT_Y] = jnp.where(up, 0, REACH + CAP_NEW)
    for i in range(4 * REACH):
        info[FACING + i] = -1
    x_at = jnp.where(up, REACH + CAP_NEW, 0)
    from_next, from_previous = jnp.where(up, 0, CAP_OLD + 1), jnp.where(up, CAP_OLD + 1, 0)
    first_id = group * NBG + new_first
    finish = first_id + held
    for k in range(CAP_NEW):
        block = new_first + k
        pick = jnp.where(block >= old_first + old_count, from_next, 1 + block - old_first)
        pick = jnp.where(block < old_first, from_previous, pick)
        info[PICK + k] = jnp.clip(pick, 0, CAP_OLD + 1)
        occupied = k < held
        safe = jnp.clip(block, 0, NBG - 1)
        cell = map_ref[0, safe]
        info[CELL + k] = jnp.where(occupied, cell, -1)
        for f in range(4):
            near = near_ref[f, safe]
            present = occupied & (near >= 0)
            slot = jnp.where(near >= finish, REACH + CAP_NEW - finish, REACH - first_id) + near
            slot = jnp.clip(slot, 0, ABSENT - 1)
            info[TABLE + 4 * k + f] = jnp.where(present, slot, ABSENT)
            local = near - group * NBG
            inside = present & (local >= 0) & (local < NBG)
            other = map_ref[0, jnp.clip(local, 0, NBG - 1)]
            info[BAND + 4 * k + f] = jnp.where(inside, 8 * k + 3 + other - cell, -1)
            info[BESIDE + 4 * k + f] = jnp.where(inside, other, -1)
            outside = present & jnp.logical_not(inside)
            place = jnp.clip(slot - x_at, 0, REACH - 1)
            info[OTHER + 4 * k + f] = jnp.where(outside, place, REACH)
            info[jnp.where(outside, FACING + 4 * place + OPPOSITE[f], SPARE)] = cell


def place_kernel(info, rhs_ref, coef_ref, source, coef):
    source[...] = jnp.zeros(source.shape, F32)
    coef[...] = jnp.ones(coef.shape, F32)
    for k in range(CAP_NEW):
        slot = jnp.clip(info[PICK + k] - 1, 0, CAP_OLD - 1)
        occupied = k < info[HELD]
        source[k, :, 0:576] = jnp.where(occupied, rhs_ref[slot], 0.0)
        coef[k, :, 0:576] = jnp.where(occupied, coef_ref[slot], 1.0)


def patched(info, field, i, k, x_in, y_in):
    pick = info[PICK + k]
    occupied = k < info[HELD]
    block = jnp.where(occupied & (pick == 0), x_in[i], field[k, :, 0:576])
    return jnp.where(occupied & (pick == CAP_OLD + 1), y_in[i], block)


def collect_kernel(info, kept, y_in, x_in, coef, faces, x_out, y_out):
    coef[...] = kept[...]
    for k in range(CAP_NEW):
        coef[k, :, 0:576] = patched(info, kept, 1, k, x_in, y_in)
        pack_faces(FINE, coef[k], faces, k, 0)
    send_faces(info, faces, x_out, y_out)


def level_kernel(info, kept, y_in, x_in, coef, source, level, faces, spread, scratch):
    source[...] = kept[...]
    for k in range(CAP_NEW):
        source[k, :, 0:576] = patched(info, kept, 0, k, x_in, y_in)
    spread[...] = spread_matrix()
    coarsen_blocks(coef[...].reshape(CAP_NEW * 24, FINE.width), spread[...], scratch)
    row, lane = iota((16, 256), 0), iota((16, 256), 1)
    for k in range(CAP_NEW):
        level[k] = jnp.ones((16, 256), F32)
        level[k, 0:12, :] = coarse_rows(scratch, k)
        level[k] = jnp.where((row < 12) & (lane < 144), level[k], 1.0)
        pack_faces(COARSE, level[k], faces, k, 0)


def start_kernel(
    info, source, coef, faces_in, coarse_faces, x_in, y_in, u, faces, x_out, y_out, table
):
    fill_table(info, table, x_in, faces_in, y_in)
    for k in range(CAP_NEW):
        ghosts = ghosts_of(FINE, info, table, k, 0)
        _, _, weight, _, _ = conductances(FINE, coef[k], ghosts)
        start = weight * source[k]
        u[k] = start
        pack_faces(FINE, start, faces, k, 0)
    faces[:, FINE.face_rows : BOTH_ROWS, :] = coarse_faces[...]
    send_faces(info, faces, x_out, y_out)


def conduct_kernel(info, coef, faces_in, x_in, y_in, fine_g, fine_d, table):
    fill_table(info, table, x_in, faces_in, y_in)
    for k in range(CAP_NEW):
        ghosts = ghosts_of(FINE, info, table, k, 0)
        _, g, _, diagonal, _ = conductances(FINE, coef[k], ghosts)
        for i in range(6):
            fine_g[k, i] = g[i]
        fine_d[k] = (1.0 / OMEGA) * diagonal


def coarse_conduct_kernel(
    info, level, faces_in, x_in, y_in, coarse_g, coarse_w, coarse_d, alpha, g_faces, row_out, table
):
    fill_table(info, table, x_in, faces_in, y_in)
    lane_row = iota((1, 128), 1)
    band = jnp.zeros((1, 128), F32)
    for k in range(CAP_NEW):
        ghosts = ghosts_of(COARSE, info, table, k, FINE.face_rows)
        q, g, weight, diagonal, masks = conductances(COARSE, level[k], ghosts)
        row, lane, depth, inside, high_y = masks
        for i in range(6):
            coarse_g[k, i] = g[i]
        coarse_w[k] = weight
        one = g[0] + g[1]
        one += jnp.where(lane < 12, 0.0, g[2]) + jnp.where(high_y, 0.0, g[3])
        one += jnp.where(row == 0, 0.0, g[4]) + jnp.where(row == 11, 0.0, g[5])
        alpha[k] = jnp.where(inside, KEEP + one, 0.0)
        pack_fields(COARSE, g[2], g[4], g_faces, k, 0, g[3], g[5])
        low_y = jnp.where(lane < 12, g[2], 0.0)
        x_edge = jnp.where(lane >= 132, g[3], low_y)
        y_edge = jnp.where(row == 0, g[4], jnp.where(row == 11, g[5], 0.0))
        pack_fields(COARSE, y_edge, x_edge, g_faces, k, 16)
        coarse_d[k] = (1.0 / OMEGA) * diagonal
        face = [
            both_totals(jnp.where(inside & (row == 0), q[4], 0.0)),
            both_totals(jnp.where(inside & (row == 11), q[5], 0.0)),
            both_totals(jnp.where(inside & (lane < 12), q[2], 0.0)),
            both_totals(jnp.where(inside & high_y, q[3], 0.0)),
        ]
        ends = jnp.where(inside & (depth == 0), q[0], 0.0)
        ends += jnp.where(inside & (depth == 11), q[1], 0.0)
        surface = face[0] + face[1] + face[2] + face[3] + both_totals(ends)
        occupied = k < info[HELD]
        band += jnp.where((lane_row == 8 * k + 3) & occupied, surface, 0.0)
        for f in range(4):
            band -= jnp.where(lane_row == info[BAND + 4 * k + f], face[f], 0.0)
        band += jnp.where(lane_row == 64 + k, info[CELL + k].astype(F32), 0.0)
    row_out[...] = band


def sweep_kernel(info, u_in, g, start, faces_in, x_in, y_in, u, faces, x_out, y_out, table):
    fill_table(info, table, x_in, faces_in, y_in)
    for k in range(CAP_NEW):
        field = u_in[k]
        ghosts = ghosts_of(COARSE, info, table, k, 0)
        new = KEEP * field + (start[k] + neighbour_sum(COARSE, field, g.at[k], ghosts))
        u[k] = new
        pack_faces(COARSE, new, faces, k, 0)
    send_faces(info, faces, x_out, y_out)


def finish_kernel(info, part, g, faces_in, x_in, y_in, u, faces, x_out, y_out, table):
    fill_table(info, table, x_in, faces_in, y_in)
    for k in range(CAP_NEW):
        u[k] = part[k]
        add_ghosts(FINE, u.at[k], g.at[k], ghosts_of(FINE, info, table, k, 0))
        pack_faces(FINE, u[k], faces, k, 0)
    send_faces(info, faces, x_out, y_out)


def residual_kernel(
    info, u_in, part, g, diagonal, weight, spread, g_faces, faces_in, x_in, y_in,
    coarse_s, faces, x_out, y_out, table, rest, scratch,
):
    fill_table(info, table, x_in, faces_in, y_in)
    for k in range(CAP_NEW):
        rest[k] = part[k]
        add_ghosts(FINE, rest.at[k], g.at[k], ghosts_of(FINE, info, table, k, 0))
        rest[k] = diagonal[k] * (rest[k] - u_in[k])
    coarsen_blocks(rest[...].reshape(CAP_NEW * 24, FINE.width), spread[...], scratch)
    for k in range(CAP_NEW):
        coarse_s[k] = jnp.zeros((16, 256), F32)
        coarse_s[k, 0:12, :] = weight[k, 0:12, :] * coarse_rows(scratch, k)
        pack_faces(COARSE, coarse_s[k], faces, k, 0)
    x_first, y_first = info[SEND_X], info[SEND_Y]
    for j in range(REACH):
        x_out[j, 0:16] = faces[x_first + j]
        x_out[j, 16:48] = g_faces[x_first + j]
        y_out[j] = faces[y_first + j]


def total_kernel(
    info, u_in, g, start, diagonal, row_in, faces_in, x_in, y_in, rows_out, swept, table
):
    fill_table(info, table, x_in, faces_in, y_in)
    lane_row = iota((1, 128), 1)
    row, lane = iota((16, 256), 0), iota((16, 256), 1)
    inside = (row < 12) & (lane < 144)
    band = row_in[...]
    for k in range(CAP_NEW):
        field = u_in[k]
        ghosts = ghosts_of(COARSE, info, table, k, 0)
        inner = start[k] + neighbour_sum(COARSE, field, g.at[k], ghosts)
        swept[k] = KEEP * field + inner
        rest = jnp.where(inside, diagonal[k] * (inner - OMEGA * field), 0.0)
        occupied = k < info[HELD]
        band += jnp.where((lane_row == 8 * k + 7) & occupied, both_totals(rest), 0.0)
    rows_out[...] = jnp.broadcast_to(band, rows_out.shape)


def lifted(answer, cell):
    at = iota((NCOARSE, 128), 0)
    return jnp.sum(jnp.where(at == cell, answer, 0.0), axis=0, keepdims=True)


def wide(line):
    return jnp.concatenate([line, line], axis=1)


def surface_lift(g, lift):
    row, lane = iota((16, 256), 0), iota((16, 256), 1)
    total = jnp.where(row == 0, g[4] * lift[0], 0.0)
    total += jnp.where(row == 11, g[5] * lift[1], 0.0)
    total += jnp.where(lane < 12, g[2] * lift[2], 0.0)
    return total + jnp.where((lane >= 132) & (lane < 144), g[3] * lift[3], 0.0)


def solve_kernel(
    info, rows_in, swept, g, alpha, u, answer_out, faces, x_out
):
    rows = rows_in[...]
    shape = (NCOARSE, 128)
    row, lane = iota(shape, 0), iota(shape, 1)
    cells = iota((NCOARSE, NCOARSE), 1).astype(F32)
    member = jnp.concatenate(
        [(rows[:, 64 + k : 65 + k] == cells).astype(F32) for k in range(CAP_NEW)], axis=0
    ).astype(jnp.bfloat16)
    shifts = [rows] + [pltpu.roll(rows, 128 - 8 * k, 1) for k in range(1, CAP_NEW)]
    band = sum(
        lax.dot_general(member, part, (((0,), (0,)), ((), ())), preferred_element_type=F32)
        for part in split_three(jnp.concatenate(shifts, axis=0))
    )
    matrix = jnp.where(lane == 64, band[:, 7:8], 0.0)
    for o in range(7):
        matrix += jnp.where(lane == row + (o - REACH), band[:, o : o + 1], 0.0)

    lists = [[i for i in (t, 9 + t, 18 + t, 27 + t) if i < NCOARSE] for t in range(6)]
    lists += [[6 + t, 24 + t] for t in range(REACH)] + [[15 + t] for t in range(REACH)]
    for pivots in lists:
        drop = None
        for j in pivots:
            column = jnp.broadcast_to(matrix[:, j : j + 1], shape)
            scaled = matrix[j : j + 1, :] / column[j : j + 1, :]
            one = jnp.where(row == j, 0.0, column) * scaled
            drop = one if drop is None else drop + one
        matrix = matrix - drop
    pivots = jnp.sum(jnp.where(lane == row, matrix, 0.0), axis=1, keepdims=True)
    answer = jnp.broadcast_to(matrix[:, 64:65], shape) / jnp.broadcast_to(pivots, shape)
    answer_out[...] = answer
    for k in range(CAP_NEW):
        lift = lifted(answer, info[CELL + k])
        beside = [wide(lifted(answer, info[BESIDE + 4 * k + f])) for f in range(4)]
        new = swept[k] + wide(lift) * alpha[k] + surface_lift(g.at[k], beside)
        u[k] = new
        pack_faces(COARSE, new, faces, k, 0)
        faces[k, LIFT_ROW : LIFT_ROW + 1, 64:128] = lift[:, 64:128]
    for j in range(REACH):
        x_out[j] = faces[info[SEND_X] + j]


def across_kernel(
    info, u_in, g, answer_in, x_in, g_in, u, faces, ghosts, y_out, table
):
    table[0:REACH] = x_in[...]
    table[REACH] = jnp.zeros((16, 128), F32)
    answer = answer_in[...]
    upper = iota((1, 128), 1) >= 64
    for k in range(CAP_NEW):
        lift = [table[info[OTHER + 4 * k + f], pl.ds(LIFT_ROW, 1), :] for f in range(4)]
        lift = [wide(jnp.where(upper, line, pltpu.roll(line, 64, 1))) for line in lift]
        new = u_in[k] + surface_lift(g.at[k], lift)
        u[k] = new
        pack_faces(COARSE, new, faces, k, 0)
    row, lane = iota((16, 128), 0), iota((16, 128), 1)
    for j in range(REACH):
        lift = [lifted(answer, info[FACING + 4 * j + f]) for f in range(4)]
        face = jnp.where(lane < 64, lift[2], lift[3])
        face = jnp.where(row >= 14, lift[1], jnp.where(row >= 12, lift[0], face))
        edge = jnp.where(row == 0, lift[0], jnp.where(row == 11, lift[1], 0.0))
        edge = jnp.where((row == 12) | (row == 14), lift[2], edge)
        edge = jnp.where((row == 13) | (row == 15), lift[3], edge)
        ghosts[j] = x_in[j] + face * g_in[j, 16:32] + edge * g_in[j, 32:48]
        y_out[j] = faces[info[SEND_Y] + j]


def refine_kernel(
    info, e_in, g, start, faces_in, x_in, y_in, u_in, spread, u, faces, x_out, y_out, table, coarse, rest
):
    fill_table(info, table, x_in, faces_in, y_in)
    for k in range(CAP_NEW):
        field = e_in[k]
        ghosts = ghosts_of(COARSE, info, table, k, 0)
        coarse[k] = KEEP * field + (start[k] + neighbour_sum(COARSE, field, g.at[k], ghosts))
    total = sum(
        jnp.dot(part, spread[...], preferred_element_type=F32)
        for part in split_two(coarse[...].reshape(CAP_NEW * 16, 256))
    )
    for k in range(CAP_NEW):
        twelve = total[16 * k : 16 * k + 12, :]
        for t in range(FINE.tiles):
            part = slice(128 * t, 128 * t + 128)
            rest[t, pl.ds(0, 12, stride=2), :] = twelve[:, part]
            rest[t, pl.ds(1, 12, stride=2), :] = twelve[:, part]
        new = u_in[k] + jnp.concatenate([rest[t] for t in range(FINE.tiles)], axis=1)
        u[k] = new
        pack_faces(FINE, new, faces, k, 0)
    send_faces(info, faces, x_out, y_out)


def last_kernel(info, part, g, faces_in, x_in, y_in, out, table, u, block, sems):
    fill_table(info, table, x_in, faces_in, y_in)
    copies = [
        pltpu.make_async_copy(block.at[k], out.at[k], sems.at[k]) for k in range(CAP_NEW)
    ]
    for k in range(CAP_NEW):
        u[...] = part[k]
        add_ghosts(FINE, u, g.at[k], ghosts_of(FINE, info, table, k, 0))
        block[k] = jnp.where(k < info[HELD], u[:, 0:576], 0.0)
        copies[k].start()
    for copy in copies:
        copy.wait()


def sds(*shape):
    return jax.ShapeDtypeStruct(shape, F32)


SMEM = pl.BlockSpec(memory_space=pltpu.SMEM)
VMEM = pl.BlockSpec(memory_space=pltpu.VMEM)
HBM = pl.BlockSpec(memory_space=pltpu.HBM)


def call(kernel, name, outs, scratch, args, in_specs=None, out_specs=None):
    many = len(outs) > 1
    return pl.pallas_call(
        kernel,
        out_shape=outs if many else outs[0],
        in_specs=in_specs or [SMEM] + [VMEM] * (len(args) - 1),
        out_specs=out_specs or ([VMEM] * len(outs) if many else VMEM),
        scratch_shapes=[pltpu.VMEM(s, F32) if isinstance(s, tuple) else s for s in scratch],
        cost_estimate=pl.CostEstimate(flops=10_000_000, bytes_accessed=4_000_000, transcendentals=0),
        compiler_params=pltpu.CompilerParams(vmem_limit_bytes=24 * 1024 * 1024),
        name=name,
    )(*args)


def swap(block, axis, first):
    starts = range(first, lax.axis_size(axis) - 1, 2)
    return lax.ppermute(block, axis, [(i, i + 1) for i in starts] + [(i + 1, i) for i in starts])


def exchange(x_out, y_out):
    x_in = swap(x_out, AXES, 1)
    return x_in, swap(y_out, AXES, 0)


def face_outs(rows):
    return [sds(CAP_NEW, rows, 128), sds(REACH, rows, 128), sds(REACH, rows, 128)]


def body(rhs_old, coef_old, old_owner, new_owner, neighbours, coarse_map):
    near = jnp.transpose(neighbours[0])
    rhs_old, coef_old, new_owner, old_owner, near, coarse_map = (
        pltpu.with_memory_space_constraint(a, pltpu.HBM)
        for a in (rhs_old, coef_old, new_owner, old_owner, near, coarse_map)
    )
    pair, old = sds(2, 24, 576), sds(CAP_OLD, 24, 576)
    y_out, x_out, info, rhs_old, coef_old = call(
        first_kernel, "owners",
        [pair, pair, jax.ShapeDtypeStruct((128,), I32), old, old],
        [
            pltpu.VMEM((1, 128), I32), pltpu.VMEM((1, 128), I32),
            pltpu.SMEM((4, 128), I32), pltpu.SMEM((1, 128), I32),
            pltpu.SemaphoreType.DMA((6,)),
        ],
        (new_owner, old_owner, near, coarse_map, rhs_old, coef_old),
        [HBM] * 6, [VMEM, VMEM, SMEM, VMEM, VMEM],
    )
    y_in, x_in = swap(y_out, "curve", 0), swap(x_out, "curve", 1)

    fine = sds(CAP_NEW, 24, FINE.width)
    coarse = sds(CAP_NEW, 16, 256)
    fine_table = [(ABSENT + 1, FINE.face_rows, 128)]
    coarse_table = [(ABSENT + 1, COARSE.face_rows, 128)]
    fine_faces, coarse_faces = face_outs(FINE.face_rows), face_outs(COARSE.face_rows)
    sums = (2, CAP_NEW * 24, 128)

    source, coef = call(place_kernel, "place", [fine, fine], [], (info, rhs_old, coef_old))
    coef, faces, x_out, y_out = call(
        collect_kernel, "collect", [fine] + fine_faces, [], (info, coef, y_in, x_in)
    )
    source, level, coarse_own, spread = call(
        level_kernel, "level",
        [fine, coarse, coarse_faces[0], jax.ShapeDtypeStruct((256, FINE.width), jnp.bfloat16)],
        [sums],
        (info, source, y_in, x_in, coef),
    )
    x_in, y_in = exchange(x_out, y_out)
    u, new_faces, x_out, y_out = call(
        start_kernel, "start", [fine] + face_outs(BOTH_ROWS), fine_table,
        (info, source, coef, faces, coarse_own, x_in, y_in),
    )
    fine_s = u
    fine_g, fine_d = call(
        conduct_kernel, "conduct", [sds(CAP_NEW, 6, 24, FINE.width), fine], fine_table,
        (info, coef, faces, x_in, y_in),
    )
    faces = new_faces
    x_in, y_in = exchange(x_out, y_out)
    coarse_g, coarse_w, coarse_d, alpha, g_faces, row = call(
        coarse_conduct_kernel, "coarse_conduct",
        [sds(CAP_NEW, 6, 16, 256), coarse, coarse, coarse, sds(CAP_NEW, 32, 128), sds(1, 128)],
        [(ABSENT + 1, BOTH_ROWS, 128)],
        (info, level, faces, x_in, y_in),
    )

    def inner(u, name):
        return call(inner_kernel, name, [fine], [], (u, fine_g, fine_s), [VMEM] * 3)

    part = inner(u, "pre_inner")
    u0, faces, x_out, y_out = call(
        finish_kernel, "pre", [fine, *fine_faces], [(ABSENT + 1, BOTH_ROWS, 128)],
        (info, part, fine_g, faces, x_in, y_in),
    )
    x_in, y_in = exchange(x_out, y_out)
    part = inner(u0, "residual_inner")
    coarse_s, faces, x_out, y_out = call(
        residual_kernel, "residual",
        [coarse, coarse_faces[0], sds(REACH, 48, 128), coarse_faces[2]],
        fine_table + [(CAP_NEW, 24, FINE.width), sums],
        (info, u0, part, fine_g, fine_d, coarse_w, spread, g_faces, faces, x_in, y_in),
    )
    g_in, y_in = exchange(x_out, y_out)
    e, faces, x_out, y_out = call(
        sweep_kernel, "coarse_pre", [coarse, *coarse_faces],
        coarse_table, (info, coarse_s, coarse_g, coarse_s, faces, g_in, y_in),
    )
    x_in, y_in = exchange(x_out, y_out)
    rows, swept = call(
        total_kernel, "totals", [sds(NCOARSE, 128), coarse], coarse_table,
        (info, e, coarse_g, coarse_s, coarse_d, row, faces, x_in, y_in),
    )
    rows = lax.all_to_all(rows, "curve", 0, 0, tiled=True)
    e, answer, faces, x_out = call(
        solve_kernel, "solve", [coarse, sds(NCOARSE, 128), *coarse_faces[:2]], [],
        (info, rows, swept, coarse_g, alpha),
    )
    x_in = swap(x_out, AXES, 1)
    e, faces, x_in, y_out = call(
        across_kernel, "across", [coarse, *coarse_faces], [(REACH + 1, 16, 128)],
        (info, e, coarse_g, answer, x_in, g_in),
    )
    y_in = swap(y_out, AXES, 0)
    u, faces, x_out, y_out = call(
        refine_kernel, "refine", [fine, *fine_faces],
        coarse_table + [(CAP_NEW, 16, 256), (FINE.tiles, 24, 128)],
        (info, e, coarse_g, coarse_s, faces, x_in, y_in, u0, spread),
    )
    x_in, y_in = exchange(x_out, y_out)
    part = inner(u, "post_inner")
    u, faces, x_out, y_out = call(
        finish_kernel, "post", [fine, *fine_faces], fine_table,
        (info, part, fine_g, faces, x_in, y_in),
    )
    x_in, y_in = exchange(x_out, y_out)
    part = inner(u, "last_inner")
    return call(
        last_kernel, "last", [sds(CAP_NEW, 24, 576)],
        fine_table
        + [(24, FINE.width), (CAP_NEW, 24, 576), pltpu.SemaphoreType.DMA((CAP_NEW,))],
        (info, part, fine_g, faces, x_in, y_in), None, pl.BlockSpec(memory_space=pl.ANY),
    )


def solution(mesh):
    in_specs = (
        P(("group", "curve"), None, None),
        P(("group", "curve"), None, None),
        P("group", None),
        P("group", None),
        P("group", None, None),
        P("group", None),
    )
    out_specs = P(("group", "curve"), None, None)
    return jax.shard_map(body, mesh=mesh, in_specs=in_specs, out_specs=out_specs, check_vma=False)
```

```python
import jax
import jax.numpy as jnp
from jax import lax
from jax.experimental import pallas as pl
from jax.experimental.pallas import tpu as pltpu
from jax.sharding import PartitionSpec as P

OMEGA = 0.8
KEEP = 1.0 - OMEGA
CAP_OLD = 7
CAP_NEW = 5
REACH = 3
NBG = 128
NCOARSE = 32
AXES = ("group", "curve")
F32 = jnp.float32
I32 = jnp.int32

HELD, PICK, TABLE, CELL, BAND = 0, 1, 8, 32, 40
SEND_X, SEND_Y, AT_X, AT_Y = 64, 65, 66, 67
SPARE, OTHER, BESIDE, FACING = 7, 72, 96, 116
OPPOSITE = (1, 0, 3, 2)
LIFT_ROW = 13
ABSENT = 2 * REACH + CAP_NEW


class Level:
    def __init__(self, side, rows, width, high_at, x_low, x_high, face_rows, factor):
        self.side, self.rows, self.width = side, rows, width
        self.last = side * side - side - (width - 128)
        self.high_at = high_at
        self.x_low, self.x_high, self.face_rows = x_low, x_high, face_rows
        self.tiles = width // 128
        self.factor = factor


FINE = Level(24, 24, 640, 40, 16, 24, 32, 1.0)
COARSE = Level(12, 16, 256, 68, 12, 14, 16, 0.25)
BOTH_ROWS = FINE.face_rows + COARSE.face_rows


def iota(shape, axis):
    return lax.broadcasted_iota(I32, shape, axis)


def over(value, side):
    return (value * 43691) >> (20 if side == 24 else 19)


def pack_faces(lev, field, faces, k, base):
    pack_fields(lev, field, field, faces, k, base)


def pack_fields(lev, y_field, x_field, faces, k, base, y_high=None, x_high=None):
    y_high = y_field if y_high is None else y_high
    x_high = x_field if x_high is None else x_high
    lane = iota((lev.rows, 128), 1)
    tail = y_high[:, lev.width - 128 :]
    move = lev.high_at - lev.last
    if move:
        tail = pltpu.roll(tail, move, 1)
    slab = jnp.where(lane < lev.side, y_field[:, :128], tail)
    if lev is FINE:
        pair = jnp.where(lane[0:8] < 64, slab[0:8], pltpu.roll(slab[8:16], 64, 1))
        faces[k, base : base + 8, :] = pair
        faces[k, base + 8 : base + 16, :] = slab[16:24]
    else:
        faces[k, base : base + lev.rows, :] = slab
    for j in range(lev.tiles):
        part = slice(128 * j, 128 * j + 128)
        low, high = base + lev.x_low + j, base + lev.x_high + j
        faces[k, low : low + 1, :] = x_field[0:1, part]
        faces[k, high : high + 1, :] = x_high[lev.side - 1 : lev.side, part]


def send_faces(info, faces, x_out, y_out):
    x_first, y_first = info[SEND_X], info[SEND_Y]
    for j in range(REACH):
        x_out[j] = faces[x_first + j]
        y_out[j] = faces[y_first + j]


def fill_table(info, table, x_in, faces, y_in):
    x_first, y_first = info[AT_X], info[AT_Y]
    for j in range(REACH):
        table[x_first + j] = x_in[j, 0 : table.shape[1]]
        table[y_first + j] = y_in[j]
    table[REACH : REACH + CAP_NEW] = faces[...]
    table[ABSENT] = jnp.zeros(table.shape[1:], F32)


def x_line(lev, table, slot, first):
    return jnp.concatenate([table[slot, pl.ds(first + j, 1), :] for j in range(lev.tiles)], axis=1)


def y_slab(lev, table, slot, base):
    if lev is not FINE:
        return table[slot, pl.ds(base, lev.rows), :]
    pair = table[slot, pl.ds(base, 8), :]
    third = table[slot, pl.ds(base + 8, 8), :]
    return jnp.concatenate([pair, pltpu.roll(pair, 64, 1), third], axis=0)


def ghosts_of(lev, info, table, k, base):
    row = [info[TABLE + 4 * k + f] for f in range(4)]
    x_low = x_line(lev, table, row[0], base + lev.x_high)
    x_high = x_line(lev, table, row[1], base + lev.x_low)
    y_low = pltpu.roll(y_slab(lev, table, row[2], base), 128 - lev.high_at, 1)
    y_high = pltpu.roll(y_slab(lev, table, row[3], base), lev.last, 1)
    return row, x_low, x_high, y_low, y_high


def interior_sum(lev, field, g):
    rows, width, side = lev.rows, lev.width, lev.side
    row = iota((rows, width), 0)
    total = g[0] * pltpu.roll(field, 1, 1) + g[1] * pltpu.roll(field, width - 1, 1)
    total += g[2] * pltpu.roll(field, side, 1) + g[3] * pltpu.roll(field, width - side, 1)
    total += g[4] * jnp.where(row == 0, 0.0, pltpu.roll(field, 1, 0))
    return total + g[5] * jnp.where(row == side - 1, 0.0, pltpu.roll(field, rows - 1, 0))


def add_ghosts(lev, out, g, ghosts):
    _, x_low, x_high, y_low, y_high = ghosts
    last, tail = lev.side - 1, lev.width - 128
    lane = iota((lev.rows, 128), 1)
    on_high = (lane >= lev.last) & (lane < lev.last + lev.side)
    out[0:1, :] += g[4, 0:1, :] * x_low
    out[last : last + 1, :] += g[5, last : last + 1, :] * x_high
    out[:, 0:128] += jnp.where(lane < lev.side, g[2, :, 0:128] * y_low, 0.0)
    out[:, tail:] += jnp.where(on_high, g[3, :, tail:] * y_high, 0.0)


def inner_kernel(u_in, g, start, part):
    for k in range(CAP_NEW):
        field = u_in[k]
        part[k] = KEEP * field + (start[k] + interior_sum(FINE, field, g.at[k]))


def neighbour_sum(lev, field, g, ghosts):
    _, x_low, x_high, y_low, y_high = ghosts
    rows, width, side = lev.rows, lev.width, lev.side
    row = iota((rows, width), 0)
    lane = iota((rows, 128), 1)
    total = g[0] * pltpu.roll(field, 1, 1) + g[1] * pltpu.roll(field, width - 1, 1)
    total += g[2] * pltpu.roll(field, side, 1) + g[3] * pltpu.roll(field, width - side, 1)
    total += g[4] * jnp.where(row == 0, x_low, pltpu.roll(field, 1, 0))
    total += g[5] * jnp.where(row == side - 1, x_high, pltpu.roll(field, rows - 1, 0))
    low = jnp.where(lane < side, g[2][:, :128] * y_low, 0.0)
    on_high = (lane >= lev.last) & (lane < lev.last + side)
    high = jnp.where(on_high, g[3][:, width - 128 :] * y_high, 0.0)
    parts = [low, high]
    if width > 256:
        parts = [low, jnp.zeros((rows, width - 256), F32), high]
    return total + jnp.concatenate(parts, axis=1)


def conductances(lev, cell, ghosts):
    present, x_low, x_high, y_low, y_high = ghosts
    present = [p != ABSENT for p in present]
    rows, width, side = lev.rows, lev.width, lev.side
    row, lane = iota((rows, width), 0), iota((rows, width), 1)
    depth = lane - side * over(lane, side)
    last = side - 1
    end = side * side
    x_low = jnp.where(present[0], x_low, cell[0:1, :])
    x_high = jnp.where(present[1], x_high, cell[last : last + 1, :])
    y_low = jnp.where(present[2], y_low, cell[:, :128])
    y_high = jnp.where(present[3], y_high, cell[:, width - 128 :])
    spare = jnp.ones((rows, width - 128), F32)
    y_low = jnp.concatenate([y_low, spare], axis=1)
    y_high = jnp.concatenate([spare, y_high], axis=1)
    high_y = (lane >= end - side) & (lane < end)
    across = [
        jnp.where(depth == 0, cell, pltpu.roll(cell, 1, 1)),
        jnp.where(depth == last, cell, pltpu.roll(cell, width - 1, 1)),
        jnp.where(lane < side, y_low, pltpu.roll(cell, side, 1)),
        jnp.where(high_y, y_high, pltpu.roll(cell, width - side, 1)),
        jnp.where(row == 0, x_low, pltpu.roll(cell, 1, 0)),
        jnp.where(row == last, x_high, pltpu.roll(cell, rows - 1, 0)),
    ]
    q = [2.0 * cell * other / (cell + other) * lev.factor for other in across]
    diagonal = q[0] + q[1] + q[2] + q[3] + q[4] + q[5]
    inside = (lane < end) & (row < side)
    weight = jnp.where(inside, OMEGA / diagonal, 0.0)
    g = [weight * one for one in q]
    g[0] = jnp.where(depth == 0, 0.0, g[0])
    g[1] = jnp.where(depth == last, 0.0, g[1])
    masks = (row, lane, depth, inside, high_y)
    return q, g, weight, diagonal, masks


def both_totals(values):
    return jnp.sum(jnp.sum(values, axis=0, keepdims=True), axis=1, keepdims=True)


def spread_matrix():
    lane = iota((1, FINE.width), 1)
    y = over(lane, 24)
    group = 12 * (y >> 1) + ((lane - 24 * y) >> 1)
    group = jnp.where(lane < 576, group, -1)
    return (iota((COARSE.width, FINE.width), 0) == group).astype(F32).astype(jnp.bfloat16)


def split_three(values):
    high, rest = values.astype(jnp.bfloat16), values - values.astype(jnp.bfloat16).astype(F32)
    mid = rest.astype(jnp.bfloat16)
    return high, mid, (rest - mid.astype(F32)).astype(jnp.bfloat16)


def split_two(values):
    high = values.astype(jnp.bfloat16)
    return high, (values - high.astype(F32)).astype(jnp.bfloat16)


def coarsen_blocks(fine, spread, scratch):
    total = sum(
        lax.dot_general(part, spread, (((1,), (1,)), ((), ())), preferred_element_type=F32)
        for part in split_two(fine)
    )
    scratch[0] = total[:, :128]
    scratch[1] = total[:, 128:]


def coarse_rows(scratch, k):
    even, odd = pl.ds(24 * k, 12, stride=2), pl.ds(24 * k + 1, 12, stride=2)
    halves = [scratch[t, even, :] + scratch[t, odd, :] for t in range(2)]
    return 0.125 * jnp.concatenate(halves, axis=1)


def first_kernel(
    new_in, old_in, near_in, map_in, rhs_in, coef_in,
    y_out, x_out, info, rhs_ref, coef_ref, new_ref, old_ref, near_ref, map_ref, sems,
):
    pairs = (
        (new_in, new_ref), (old_in, old_ref), (near_in, near_ref), (map_in, map_ref),
        (rhs_in, rhs_ref), (coef_in, coef_ref),
    )
    copies = [pltpu.make_async_copy(a, b, sems.at[i]) for i, (a, b) in enumerate(pairs)]
    for copy in copies:
        copy.start()
    curve = lax.axis_index("curve")
    group = lax.axis_index("group")
    up = lax.rem(curve, 2) == 1
    for copy in copies[:4]:
        copy.wait()
    new, old = new_ref[...], old_ref[...]

    def count(mask):
        return jnp.sum(jnp.where(mask, 1.0, 0.0)).astype(I32)

    new_first, held = count(new < curve), count(new == curve)
    old_first, old_count = count(old < curve), count(old == curve)
    last = jnp.clip(old_count - 1, 0, CAP_OLD - 1)
    x_slot, y_slot = jnp.where(up, last, 0), jnp.where(up, 0, last)
    for copy in copies[4:]:
        copy.wait()
    x_out[0] = rhs_ref[x_slot]
    x_out[1] = coef_ref[x_slot]
    y_out[0] = rhs_ref[y_slot]
    y_out[1] = coef_ref[y_slot]
    info[HELD] = held
    final = jnp.maximum(held - REACH, 0)
    info[SEND_X], info[SEND_Y] = jnp.where(up, final, 0), jnp.where(up, 0, final)
    info[AT_X] = jnp.where(up, REACH + CAP_NEW, 0)
    info[AT_Y] = jnp.where(up, 0, REACH + CAP_NEW)
    for i in range(4 * REACH):
        info[FACING + i] = -1
    x_at = jnp.where(up, REACH + CAP_NEW, 0)
    from_next, from_previous = jnp.where(up, 0, CAP_OLD + 1), jnp.where(up, CAP_OLD + 1, 0)
    first_id = group * NBG + new_first
    finish = first_id + held
    for k in range(CAP_NEW):
        block = new_first + k
        pick = jnp.where(block >= old_first + old_count, from_next, 1 + block - old_first)
        pick = jnp.where(block < old_first, from_previous, pick)
        info[PICK + k] = jnp.clip(pick, 0, CAP_OLD + 1)
        occupied = k < held
        safe = jnp.clip(block, 0, NBG - 1)
        cell = map_ref[0, safe]
        info[CELL + k] = jnp.where(occupied, cell, -1)
        for f in range(4):
            near = near_ref[f, safe]
            present = occupied & (near >= 0)
            slot = jnp.where(near >= finish, REACH + CAP_NEW - finish, REACH - first_id) + near
            slot = jnp.clip(slot, 0, ABSENT - 1)
            info[TABLE + 4 * k + f] = jnp.where(present, slot, ABSENT)
            local = near - group * NBG
            inside = present & (local >= 0) & (local < NBG)
            other = map_ref[0, jnp.clip(local, 0, NBG - 1)]
            info[BAND + 4 * k + f] = jnp.where(inside, 8 * k + 3 + other - cell, -1)
            info[BESIDE + 4 * k + f] = jnp.where(inside, other, -1)
            outside = present & jnp.logical_not(inside)
            place = jnp.clip(slot - x_at, 0, REACH - 1)
            info[OTHER + 4 * k + f] = jnp.where(outside, place, REACH)
            info[jnp.where(outside, FACING + 4 * place + OPPOSITE[f], SPARE)] = cell


def place_kernel(info, rhs_ref, coef_ref, source, coef):
    source[...] = jnp.zeros(source.shape, F32)
    coef[...] = jnp.ones(coef.shape, F32)
    for k in range(CAP_NEW):
        slot = jnp.clip(info[PICK + k] - 1, 0, CAP_OLD - 1)
        occupied = k < info[HELD]
        source[k, :, 0:576] = jnp.where(occupied, rhs_ref[slot], 0.0)
        coef[k, :, 0:576] = jnp.where(occupied, coef_ref[slot], 1.0)


def patched(info, field, i, k, x_in, y_in):
    pick = info[PICK + k]
    occupied = k < info[HELD]
    block = jnp.where(occupied & (pick == 0), x_in[i], field[k, :, 0:576])
    return jnp.where(occupied & (pick == CAP_OLD + 1), y_in[i], block)


def collect_kernel(info, kept, y_in, x_in, coef, faces, x_out, y_out):
    coef[...] = kept[...]
    for k in range(CAP_NEW):
        coef[k, :, 0:576] = patched(info, kept, 1, k, x_in, y_in)
        pack_faces(FINE, coef[k], faces, k, 0)
    send_faces(info, faces, x_out, y_out)


def level_kernel(info, kept, y_in, x_in, coef, source, level, faces, spread, scratch):
    source[...] = kept[...]
    for k in range(CAP_NEW):
        source[k, :, 0:576] = patched(info, kept, 0, k, x_in, y_in)
    spread[...] = spread_matrix()
    coarsen_blocks(coef[...].reshape(CAP_NEW * 24, FINE.width), spread[...], scratch)
    row, lane = iota((16, 256), 0), iota((16, 256), 1)
    for k in range(CAP_NEW):
        level[k] = jnp.ones((16, 256), F32)
        level[k, 0:12, :] = coarse_rows(scratch, k)
        level[k] = jnp.where((row < 12) & (lane < 144), level[k], 1.0)
        pack_faces(COARSE, level[k], faces, k, 0)


def conduct_kernel(
    info, source, coef, faces_in, coarse_faces, x_in, y_in,
    fine_g, fine_s, fine_d, u, faces, x_out, y_out, table,
):
    fill_table(info, table, x_in, faces_in, y_in)
    for k in range(CAP_NEW):
        ghosts = ghosts_of(FINE, info, table, k, 0)
        _, g, weight, diagonal, _ = conductances(FINE, coef[k], ghosts)
        for i in range(6):
            fine_g[k, i] = g[i]
        fine_d[k] = (1.0 / OMEGA) * diagonal
        start = weight * source[k]
        fine_s[k] = start
        u[k] = start
        pack_faces(FINE, start, faces, k, 0)
    faces[:, FINE.face_rows : BOTH_ROWS, :] = coarse_faces[...]
    send_faces(info, faces, x_out, y_out)


def coarse_conduct_kernel(
    info, level, faces_in, x_in, y_in, coarse_g, coarse_w, coarse_d, alpha, g_faces, row_out, table
):
    fill_table(info, table, x_in, faces_in, y_in)
    lane_row = iota((1, 128), 1)
    band = jnp.zeros((1, 128), F32)
    for k in range(CAP_NEW):
        ghosts = ghosts_of(COARSE, info, table, k, FINE.face_rows)
        q, g, weight, diagonal, masks = conductances(COARSE, level[k], ghosts)
        row, lane, depth, inside, high_y = masks
        for i in range(6):
            coarse_g[k, i] = g[i]
        coarse_w[k] = weight
        one = g[0] + g[1]
        one += jnp.where(lane < 12, 0.0, g[2]) + jnp.where(high_y, 0.0, g[3])
        one += jnp.where(row == 0, 0.0, g[4]) + jnp.where(row == 11, 0.0, g[5])
        alpha[k] = jnp.where(inside, KEEP + one, 0.0)
        pack_fields(COARSE, g[2], g[4], g_faces, k, 0, g[3], g[5])
        low_y = jnp.where(lane < 12, g[2], 0.0)
        x_edge = jnp.where(lane >= 132, g[3], low_y)
        y_edge = jnp.where(row == 0, g[4], jnp.where(row == 11, g[5], 0.0))
        pack_fields(COARSE, y_edge, x_edge, g_faces, k, 16)
        coarse_d[k] = (1.0 / OMEGA) * diagonal
        face = [
            both_totals(jnp.where(inside & (row == 0), q[4], 0.0)),
            both_totals(jnp.where(inside & (row == 11), q[5], 0.0)),
            both_totals(jnp.where(inside & (lane < 12), q[2], 0.0)),
            both_totals(jnp.where(inside & high_y, q[3], 0.0)),
        ]
        ends = jnp.where(inside & (depth == 0), q[0], 0.0)
        ends += jnp.where(inside & (depth == 11), q[1], 0.0)
        surface = face[0] + face[1] + face[2] + face[3] + both_totals(ends)
        occupied = k < info[HELD]
        band += jnp.where((lane_row == 8 * k + 3) & occupied, surface, 0.0)
        for f in range(4):
            band -= jnp.where(lane_row == info[BAND + 4 * k + f], face[f], 0.0)
        band += jnp.where(lane_row == 64 + k, info[CELL + k].astype(F32), 0.0)
    row_out[...] = band


def sweep_kernel(info, u_in, g, start, faces_in, x_in, y_in, u, faces, x_out, y_out, table):
    fill_table(info, table, x_in, faces_in, y_in)
    for k in range(CAP_NEW):
        field = u_in[k]
        ghosts = ghosts_of(COARSE, info, table, k, 0)
        new = KEEP * field + (start[k] + neighbour_sum(COARSE, field, g.at[k], ghosts))
        u[k] = new
        pack_faces(COARSE, new, faces, k, 0)
    send_faces(info, faces, x_out, y_out)


def finish_kernel(info, part, g, faces_in, x_in, y_in, u, faces, x_out, y_out, table):
    fill_table(info, table, x_in, faces_in, y_in)
    for k in range(CAP_NEW):
        u[k] = part[k]
        add_ghosts(FINE, u.at[k], g.at[k], ghosts_of(FINE, info, table, k, 0))
        pack_faces(FINE, u[k], faces, k, 0)
    send_faces(info, faces, x_out, y_out)


def residual_kernel(
    info, u_in, part, g, diagonal, weight, spread, g_faces, faces_in, x_in, y_in,
    coarse_s, faces, x_out, y_out, table, rest, scratch,
):
    fill_table(info, table, x_in, faces_in, y_in)
    for k in range(CAP_NEW):
        rest[k] = part[k]
        add_ghosts(FINE, rest.at[k], g.at[k], ghosts_of(FINE, info, table, k, 0))
        rest[k] = diagonal[k] * (rest[k] - u_in[k])
    coarsen_blocks(rest[...].reshape(CAP_NEW * 24, FINE.width), spread[...], scratch)
    for k in range(CAP_NEW):
        coarse_s[k] = jnp.zeros((16, 256), F32)
        coarse_s[k, 0:12, :] = weight[k, 0:12, :] * coarse_rows(scratch, k)
        pack_faces(COARSE, coarse_s[k], faces, k, 0)
    x_first, y_first = info[SEND_X], info[SEND_Y]
    for j in range(REACH):
        x_out[j, 0:16] = faces[x_first + j]
        x_out[j, 16:48] = g_faces[x_first + j]
        y_out[j] = faces[y_first + j]


def total_kernel(
    info, u_in, g, start, diagonal, row_in, faces_in, x_in, y_in, rows_out, swept, table
):
    fill_table(info, table, x_in, faces_in, y_in)
    lane_row = iota((1, 128), 1)
    row, lane = iota((16, 256), 0), iota((16, 256), 1)
    inside = (row < 12) & (lane < 144)
    band = row_in[...]
    for k in range(CAP_NEW):
        field = u_in[k]
        ghosts = ghosts_of(COARSE, info, table, k, 0)
        inner = start[k] + neighbour_sum(COARSE, field, g.at[k], ghosts)
        swept[k] = KEEP * field + inner
        rest = jnp.where(inside, diagonal[k] * (inner - OMEGA * field), 0.0)
        occupied = k < info[HELD]
        band += jnp.where((lane_row == 8 * k + 7) & occupied, both_totals(rest), 0.0)
    rows_out[...] = jnp.broadcast_to(band, rows_out.shape)


def lifted(answer, cell):
    at = iota((NCOARSE, 128), 0)
    return jnp.sum(jnp.where(at == cell, answer, 0.0), axis=0, keepdims=True)


def wide(line):
    return jnp.concatenate([line, line], axis=1)


def surface_lift(g, lift):
    row, lane = iota((16, 256), 0), iota((16, 256), 1)
    total = jnp.where(row == 0, g[4] * lift[0], 0.0)
    total += jnp.where(row == 11, g[5] * lift[1], 0.0)
    total += jnp.where(lane < 12, g[2] * lift[2], 0.0)
    return total + jnp.where((lane >= 132) & (lane < 144), g[3] * lift[3], 0.0)


def solve_kernel(
    info, rows_in, swept, g, alpha, u, answer_out, faces, x_out
):
    rows = rows_in[...]
    shape = (NCOARSE, 128)
    row, lane = iota(shape, 0), iota(shape, 1)
    cells = iota((NCOARSE, NCOARSE), 1).astype(F32)
    member = jnp.concatenate(
        [(rows[:, 64 + k : 65 + k] == cells).astype(F32) for k in range(CAP_NEW)], axis=0
    ).astype(jnp.bfloat16)
    shifts = [rows] + [pltpu.roll(rows, 128 - 8 * k, 1) for k in range(1, CAP_NEW)]
    band = sum(
        lax.dot_general(member, part, (((0,), (0,)), ((), ())), preferred_element_type=F32)
        for part in split_three(jnp.concatenate(shifts, axis=0))
    )
    matrix = jnp.where(lane == 64, band[:, 7:8], 0.0)
    for o in range(7):
        matrix += jnp.where(lane == row + (o - REACH), band[:, o : o + 1], 0.0)

    lists = [[i for i in (t, 9 + t, 18 + t, 27 + t) if i < NCOARSE] for t in range(6)]
    lists += [[6 + t, 24 + t] for t in range(REACH)] + [[15 + t] for t in range(REACH)]
    for pivots in lists:
        drop = None
        for j in pivots:
            column = jnp.broadcast_to(matrix[:, j : j + 1], shape)
            scaled = matrix[j : j + 1, :] / column[j : j + 1, :]
            one = jnp.where(row == j, 0.0, column) * scaled
            drop = one if drop is None else drop + one
        matrix = matrix - drop
    pivots = jnp.sum(jnp.where(lane == row, matrix, 0.0), axis=1, keepdims=True)
    answer = jnp.broadcast_to(matrix[:, 64:65], shape) / jnp.broadcast_to(pivots, shape)
    answer_out[...] = answer
    for k in range(CAP_NEW):
        lift = lifted(answer, info[CELL + k])
        beside = [wide(lifted(answer, info[BESIDE + 4 * k + f])) for f in range(4)]
        new = swept[k] + wide(lift) * alpha[k] + surface_lift(g.at[k], beside)
        u[k] = new
        pack_faces(COARSE, new, faces, k, 0)
        faces[k, LIFT_ROW : LIFT_ROW + 1, 64:128] = lift[:, 64:128]
    for j in range(REACH):
        x_out[j] = faces[info[SEND_X] + j]


def across_kernel(
    info, u_in, g, answer_in, x_in, g_in, u, faces, ghosts, y_out, table
):
    table[0:REACH] = x_in[...]
    table[REACH] = jnp.zeros((16, 128), F32)
    answer = answer_in[...]
    upper = iota((1, 128), 1) >= 64
    for k in range(CAP_NEW):
        lift = [table[info[OTHER + 4 * k + f], pl.ds(LIFT_ROW, 1), :] for f in range(4)]
        lift = [wide(jnp.where(upper, line, pltpu.roll(line, 64, 1))) for line in lift]
        new = u_in[k] + surface_lift(g.at[k], lift)
        u[k] = new
        pack_faces(COARSE, new, faces, k, 0)
    row, lane = iota((16, 128), 0), iota((16, 128), 1)
    for j in range(REACH):
        lift = [lifted(answer, info[FACING + 4 * j + f]) for f in range(4)]
        face = jnp.where(lane < 64, lift[2], lift[3])
        face = jnp.where(row >= 14, lift[1], jnp.where(row >= 12, lift[0], face))
        edge = jnp.where(row == 0, lift[0], jnp.where(row == 11, lift[1], 0.0))
        edge = jnp.where((row == 12) | (row == 14), lift[2], edge)
        edge = jnp.where((row == 13) | (row == 15), lift[3], edge)
        ghosts[j] = x_in[j] + face * g_in[j, 16:32] + edge * g_in[j, 32:48]
        y_out[j] = faces[info[SEND_Y] + j]


def refine_kernel(
    info, e_in, g, start, faces_in, x_in, y_in, u_in, spread, u, faces, x_out, y_out, table, coarse, rest
):
    fill_table(info, table, x_in, faces_in, y_in)
    for k in range(CAP_NEW):
        field = e_in[k]
        ghosts = ghosts_of(COARSE, info, table, k, 0)
        coarse[k] = KEEP * field + (start[k] + neighbour_sum(COARSE, field, g.at[k], ghosts))
    total = sum(
        jnp.dot(part, spread[...], preferred_element_type=F32)
        for part in split_two(coarse[...].reshape(CAP_NEW * 16, 256))
    )
    for k in range(CAP_NEW):
        twelve = total[16 * k : 16 * k + 12, :]
        for t in range(FINE.tiles):
            part = slice(128 * t, 128 * t + 128)
            rest[t, pl.ds(0, 12, stride=2), :] = twelve[:, part]
            rest[t, pl.ds(1, 12, stride=2), :] = twelve[:, part]
        new = u_in[k] + jnp.concatenate([rest[t] for t in range(FINE.tiles)], axis=1)
        u[k] = new
        pack_faces(FINE, new, faces, k, 0)
    send_faces(info, faces, x_out, y_out)


def last_kernel(info, part, g, faces_in, x_in, y_in, out, table, u, block, sems):
    fill_table(info, table, x_in, faces_in, y_in)
    copies = [
        pltpu.make_async_copy(block.at[k], out.at[k], sems.at[k]) for k in range(CAP_NEW)
    ]
    for k in range(CAP_NEW):
        u[...] = part[k]
        add_ghosts(FINE, u, g.at[k], ghosts_of(FINE, info, table, k, 0))
        block[k] = jnp.where(k < info[HELD], u[:, 0:576], 0.0)
        copies[k].start()
    for copy in copies:
        copy.wait()


def sds(*shape):
    return jax.ShapeDtypeStruct(shape, F32)


SMEM = pl.BlockSpec(memory_space=pltpu.SMEM)
VMEM = pl.BlockSpec(memory_space=pltpu.VMEM)
HBM = pl.BlockSpec(memory_space=pltpu.HBM)


def call(kernel, name, outs, scratch, args, in_specs=None, out_specs=None):
    many = len(outs) > 1
    return pl.pallas_call(
        kernel,
        out_shape=outs if many else outs[0],
        in_specs=in_specs or [SMEM] + [VMEM] * (len(args) - 1),
        out_specs=out_specs or ([VMEM] * len(outs) if many else VMEM),
        scratch_shapes=[pltpu.VMEM(s, F32) if isinstance(s, tuple) else s for s in scratch],
        cost_estimate=pl.CostEstimate(flops=10_000_000, bytes_accessed=4_000_000, transcendentals=0),
        compiler_params=pltpu.CompilerParams(vmem_limit_bytes=24 * 1024 * 1024),
        name=name,
    )(*args)


def swap(block, axis, first):
    starts = range(first, lax.axis_size(axis) - 1, 2)
    return lax.ppermute(block, axis, [(i, i + 1) for i in starts] + [(i + 1, i) for i in starts])


def exchange(x_out, y_out):
    x_in = swap(x_out, AXES, 1)
    return x_in, swap(y_out, AXES, 0)


def face_outs(rows):
    return [sds(CAP_NEW, rows, 128), sds(REACH, rows, 128), sds(REACH, rows, 128)]


def body(rhs_old, coef_old, old_owner, new_owner, neighbours, coarse_map):
    near = jnp.transpose(neighbours[0])
    rhs_old, coef_old, new_owner, old_owner, near, coarse_map = (
        pltpu.with_memory_space_constraint(a, pltpu.HBM)
        for a in (rhs_old, coef_old, new_owner, old_owner, near, coarse_map)
    )
    pair, old = sds(2, 24, 576), sds(CAP_OLD, 24, 576)
    y_out, x_out, info, rhs_old, coef_old = call(
        first_kernel, "owners",
        [pair, pair, jax.ShapeDtypeStruct((128,), I32), old, old],
        [
            pltpu.VMEM((1, 128), I32), pltpu.VMEM((1, 128), I32),
            pltpu.SMEM((4, 128), I32), pltpu.SMEM((1, 128), I32),
            pltpu.SemaphoreType.DMA((6,)),
        ],
        (new_owner, old_owner, near, coarse_map, rhs_old, coef_old),
        [HBM] * 6, [VMEM, VMEM, SMEM, VMEM, VMEM],
    )
    y_in, x_in = swap(y_out, "curve", 0), swap(x_out, "curve", 1)

    fine = sds(CAP_NEW, 24, FINE.width)
    coarse = sds(CAP_NEW, 16, 256)
    fine_table = [(ABSENT + 1, FINE.face_rows, 128)]
    coarse_table = [(ABSENT + 1, COARSE.face_rows, 128)]
    fine_faces, coarse_faces = face_outs(FINE.face_rows), face_outs(COARSE.face_rows)
    sums = (2, CAP_NEW * 24, 128)

    source, coef = call(place_kernel, "place", [fine, fine], [], (info, rhs_old, coef_old))
    coef, faces, x_out, y_out = call(
        collect_kernel, "collect", [fine] + fine_faces, [], (info, coef, y_in, x_in)
    )
    source, level, coarse_own, spread = call(
        level_kernel, "level",
        [fine, coarse, coarse_faces[0], jax.ShapeDtypeStruct((256, FINE.width), jnp.bfloat16)],
        [sums],
        (info, source, y_in, x_in, coef),
    )
    x_in, y_in = exchange(x_out, y_out)
    fine_g, fine_s, fine_d, u, faces, x_out, y_out = call(
        conduct_kernel, "conduct",
        [sds(CAP_NEW, 6, 24, FINE.width), fine, fine, fine] + face_outs(BOTH_ROWS), fine_table,
        (info, source, coef, faces, coarse_own, x_in, y_in),
    )
    x_in, y_in = exchange(x_out, y_out)
    coarse_g, coarse_w, coarse_d, alpha, g_faces, row = call(
        coarse_conduct_kernel, "coarse_conduct",
        [sds(CAP_NEW, 6, 16, 256), coarse, coarse, coarse, sds(CAP_NEW, 32, 128), sds(1, 128)],
        [(ABSENT + 1, BOTH_ROWS, 128)],
        (info, level, faces, x_in, y_in),
    )

    def inner(u, name):
        return call(inner_kernel, name, [fine], [], (u, fine_g, fine_s), [VMEM] * 3)

    part = inner(u, "pre_inner")
    u0, faces, x_out, y_out = call(
        finish_kernel, "pre", [fine, *fine_faces], [(ABSENT + 1, BOTH_ROWS, 128)],
        (info, part, fine_g, faces, x_in, y_in),
    )
    x_in, y_in = exchange(x_out, y_out)
    part = inner(u0, "residual_inner")
    coarse_s, faces, x_out, y_out = call(
        residual_kernel, "residual",
        [coarse, coarse_faces[0], sds(REACH, 48, 128), coarse_faces[2]],
        fine_table + [(CAP_NEW, 24, FINE.width), sums],
        (info, u0, part, fine_g, fine_d, coarse_w, spread, g_faces, faces, x_in, y_in),
    )
    g_in, y_in = exchange(x_out, y_out)
    e, faces, x_out, y_out = call(
        sweep_kernel, "coarse_pre", [coarse, *coarse_faces],
        coarse_table, (info, coarse_s, coarse_g, coarse_s, faces, g_in, y_in),
    )
    x_in, y_in = exchange(x_out, y_out)
    rows, swept = call(
        total_kernel, "totals", [sds(NCOARSE, 128), coarse], coarse_table,
        (info, e, coarse_g, coarse_s, coarse_d, row, faces, x_in, y_in),
    )
    rows = lax.all_to_all(rows, "curve", 0, 0, tiled=True)
    e, answer, faces, x_out = call(
        solve_kernel, "solve", [coarse, sds(NCOARSE, 128), *coarse_faces[:2]], [],
        (info, rows, swept, coarse_g, alpha),
    )
    x_in = swap(x_out, AXES, 1)
    e, faces, x_in, y_out = call(
        across_kernel, "across", [coarse, *coarse_faces], [(REACH + 1, 16, 128)],
        (info, e, coarse_g, answer, x_in, g_in),
    )
    y_in = swap(y_out, AXES, 0)
    u, faces, x_out, y_out = call(
        refine_kernel, "refine", [fine, *fine_faces],
        coarse_table + [(CAP_NEW, 16, 256), (FINE.tiles, 24, 128)],
        (info, e, coarse_g, coarse_s, faces, x_in, y_in, u0, spread),
    )
    x_in, y_in = exchange(x_out, y_out)
    part = inner(u, "post_inner")
    u, faces, x_out, y_out = call(
        finish_kernel, "post", [fine, *fine_faces], fine_table,
        (info, part, fine_g, faces, x_in, y_in),
    )
    x_in, y_in = exchange(x_out, y_out)
    part = inner(u, "last_inner")
    return call(
        last_kernel, "last", [sds(CAP_NEW, 24, 576)],
        fine_table
        + [(24, FINE.width), (CAP_NEW, 24, 576), pltpu.SemaphoreType.DMA((CAP_NEW,))],
        (info, part, fine_g, faces, x_in, y_in), None, pl.BlockSpec(memory_space=pl.ANY),
    )


def solution(mesh):
    in_specs = (
        P(("group", "curve"), None, None),
        P(("group", "curve"), None, None),
        P("group", None),
        P("group", None),
        P("group", None, None),
        P("group", None),
    )
    out_specs = P(("group", "curve"), None, None)
    return jax.shard_map(body, mesh=mesh, in_specs=in_specs, out_specs=out_specs, check_vma=False)
```

```python
import jax
import jax.numpy as jnp
from jax import lax
from jax.experimental import pallas as pl
from jax.experimental.pallas import tpu as pltpu
from jax.sharding import PartitionSpec as P

OMEGA = 0.8
KEEP = 1.0 - OMEGA
CAP_OLD = 7
CAP_NEW = 5
REACH = 3
NBG = 128
NCOARSE = 32
AXES = ("group", "curve")
F32 = jnp.float32
I32 = jnp.int32

HELD, PICK, TABLE, CELL, BAND = 0, 1, 8, 32, 40
SEND_X, SEND_Y, AT_X, AT_Y = 64, 65, 66, 67
SPARE, OTHER, BESIDE, FACING = 7, 72, 96, 116
OPPOSITE = (1, 0, 3, 2)
LIFT_ROW = 13
ABSENT = 2 * REACH + CAP_NEW


class Level:
    def __init__(self, side, rows, width, high_at, x_low, x_high, face_rows, factor):
        self.side, self.rows, self.width = side, rows, width
        self.last = side * side - side - (width - 128)
        self.high_at = high_at
        self.x_low, self.x_high, self.face_rows = x_low, x_high, face_rows
        self.tiles = width // 128
        self.factor = factor


FINE = Level(24, 24, 640, 40, 16, 24, 32, 1.0)
COARSE = Level(12, 16, 256, 68, 12, 14, 16, 0.25)
BOTH_ROWS = FINE.face_rows + COARSE.face_rows


def iota(shape, axis):
    return lax.broadcasted_iota(I32, shape, axis)


def over(value, side):
    return (value * 43691) >> (20 if side == 24 else 19)


def pack_faces(lev, field, faces, k, base):
    pack_fields(lev, field, field, faces, k, base)


def pack_fields(lev, y_field, x_field, faces, k, base, y_high=None, x_high=None):
    y_high = y_field if y_high is None else y_high
    x_high = x_field if x_high is None else x_high
    lane = iota((lev.rows, 128), 1)
    tail = y_high[:, lev.width - 128 :]
    move = lev.high_at - lev.last
    if move:
        tail = pltpu.roll(tail, move, 1)
    slab = jnp.where(lane < lev.side, y_field[:, :128], tail)
    if lev is FINE:
        pair = jnp.where(lane[0:8] < 64, slab[0:8], pltpu.roll(slab[8:16], 64, 1))
        faces[k, base : base + 8, :] = pair
        faces[k, base + 8 : base + 16, :] = slab[16:24]
    else:
        faces[k, base : base + lev.rows, :] = slab
    for j in range(lev.tiles):
        part = slice(128 * j, 128 * j + 128)
        low, high = base + lev.x_low + j, base + lev.x_high + j
        faces[k, low : low + 1, :] = x_field[0:1, part]
        faces[k, high : high + 1, :] = x_high[lev.side - 1 : lev.side, part]


def send_faces(info, faces, x_out, y_out):
    x_first, y_first = info[SEND_X], info[SEND_Y]
    for j in range(REACH):
        x_out[j] = faces[x_first + j]
        y_out[j] = faces[y_first + j]


def fill_table(info, table, x_in, faces, y_in):
    x_first, y_first = info[AT_X], info[AT_Y]
    for j in range(REACH):
        table[x_first + j] = x_in[j, 0 : table.shape[1]]
        table[y_first + j] = y_in[j]
    table[REACH : REACH + CAP_NEW] = faces[...]
    table[ABSENT] = jnp.zeros(table.shape[1:], F32)


def x_line(lev, table, slot, first):
    return jnp.concatenate([table[slot, pl.ds(first + j, 1), :] for j in range(lev.tiles)], axis=1)


def y_slab(lev, table, slot, base):
    if lev is not FINE:
        return table[slot, pl.ds(base, lev.rows), :]
    pair = table[slot, pl.ds(base, 8), :]
    third = table[slot, pl.ds(base + 8, 8), :]
    return jnp.concatenate([pair, pltpu.roll(pair, 64, 1), third], axis=0)


def ghosts_of(lev, info, table, k, base):
    row = [info[TABLE + 4 * k + f] for f in range(4)]
    x_low = x_line(lev, table, row[0], base + lev.x_high)
    x_high = x_line(lev, table, row[1], base + lev.x_low)
    y_low = pltpu.roll(y_slab(lev, table, row[2], base), 128 - lev.high_at, 1)
    y_high = pltpu.roll(y_slab(lev, table, row[3], base), lev.last, 1)
    return row, x_low, x_high, y_low, y_high


def interior_sum(lev, field, g):
    rows, width, side = lev.rows, lev.width, lev.side
    row = iota((rows, width), 0)
    total = g[0] * pltpu.roll(field, 1, 1) + g[1] * pltpu.roll(field, width - 1, 1)
    total += g[2] * pltpu.roll(field, side, 1) + g[3] * pltpu.roll(field, width - side, 1)
    total += g[4] * jnp.where(row == 0, 0.0, pltpu.roll(field, 1, 0))
    return total + g[5] * jnp.where(row == side - 1, 0.0, pltpu.roll(field, rows - 1, 0))


def add_ghosts(lev, out, g, ghosts):
    _, x_low, x_high, y_low, y_high = ghosts
    last, tail = lev.side - 1, lev.width - 128
    lane = iota((lev.rows, 128), 1)
    on_high = (lane >= lev.last) & (lane < lev.last + lev.side)
    out[0:1, :] += g[4, 0:1, :] * x_low
    out[last : last + 1, :] += g[5, last : last + 1, :] * x_high
    out[:, 0:128] += jnp.where(lane < lev.side, g[2, :, 0:128] * y_low, 0.0)
    out[:, tail:] += jnp.where(on_high, g[3, :, tail:] * y_high, 0.0)


def inner_kernel(u_in, g, start, part):
    for k in range(CAP_NEW):
        field = u_in[k]
        part[k] = KEEP * field + (start[k] + interior_sum(FINE, field, g.at[k]))


def neighbour_sum(lev, field, g, ghosts):
    _, x_low, x_high, y_low, y_high = ghosts
    rows, width, side = lev.rows, lev.width, lev.side
    row = iota((rows, width), 0)
    lane = iota((rows, 128), 1)
    total = g[0] * pltpu.roll(field, 1, 1) + g[1] * pltpu.roll(field, width - 1, 1)
    total += g[2] * pltpu.roll(field, side, 1) + g[3] * pltpu.roll(field, width - side, 1)
    total += g[4] * jnp.where(row == 0, x_low, pltpu.roll(field, 1, 0))
    total += g[5] * jnp.where(row == side - 1, x_high, pltpu.roll(field, rows - 1, 0))
    low = jnp.where(lane < side, g[2][:, :128] * y_low, 0.0)
    on_high = (lane >= lev.last) & (lane < lev.last + side)
    high = jnp.where(on_high, g[3][:, width - 128 :] * y_high, 0.0)
    parts = [low, high]
    if width > 256:
        parts = [low, jnp.zeros((rows, width - 256), F32), high]
    return total + jnp.concatenate(parts, axis=1)


def conductances(lev, cell, ghosts):
    present, x_low, x_high, y_low, y_high = ghosts
    present = [p != ABSENT for p in present]
    rows, width, side = lev.rows, lev.width, lev.side
    row, lane = iota((rows, width), 0), iota((rows, width), 1)
    depth = lane - side * over(lane, side)
    last = side - 1
    end = side * side
    x_low = jnp.where(present[0], x_low, cell[0:1, :])
    x_high = jnp.where(present[1], x_high, cell[last : last + 1, :])
    y_low = jnp.where(present[2], y_low, cell[:, :128])
    y_high = jnp.where(present[3], y_high, cell[:, width - 128 :])
    spare = jnp.ones((rows, width - 128), F32)
    y_low = jnp.concatenate([y_low, spare], axis=1)
    y_high = jnp.concatenate([spare, y_high], axis=1)
    high_y = (lane >= end - side) & (lane < end)
    across = [
        jnp.where(depth == 0, cell, pltpu.roll(cell, 1, 1)),
        jnp.where(depth == last, cell, pltpu.roll(cell, width - 1, 1)),
        jnp.where(lane < side, y_low, pltpu.roll(cell, side, 1)),
        jnp.where(high_y, y_high, pltpu.roll(cell, width - side, 1)),
        jnp.where(row == 0, x_low, pltpu.roll(cell, 1, 0)),
        jnp.where(row == last, x_high, pltpu.roll(cell, rows - 1, 0)),
    ]
    q = [2.0 * cell * other / (cell + other) * lev.factor for other in across]
    diagonal = q[0] + q[1] + q[2] + q[3] + q[4] + q[5]
    inside = (lane < end) & (row < side)
    weight = jnp.where(inside, OMEGA / diagonal, 0.0)
    g = [weight * one for one in q]
    g[0] = jnp.where(depth == 0, 0.0, g[0])
    g[1] = jnp.where(depth == last, 0.0, g[1])
    masks = (row, lane, depth, inside, high_y)
    return q, g, weight, diagonal, masks


def both_totals(values):
    return jnp.sum(jnp.sum(values, axis=0, keepdims=True), axis=1, keepdims=True)


def spread_matrix():
    lane = iota((1, FINE.width), 1)
    y = over(lane, 24)
    group = 12 * (y >> 1) + ((lane - 24 * y) >> 1)
    group = jnp.where(lane < 576, group, -1)
    return (iota((COARSE.width, FINE.width), 0) == group).astype(F32).astype(jnp.bfloat16)


def split_three(values):
    high, rest = values.astype(jnp.bfloat16), values - values.astype(jnp.bfloat16).astype(F32)
    mid = rest.astype(jnp.bfloat16)
    return high, mid, (rest - mid.astype(F32)).astype(jnp.bfloat16)


def split_two(values):
    high = values.astype(jnp.bfloat16)
    return high, (values - high.astype(F32)).astype(jnp.bfloat16)


def coarsen_blocks(fine, spread, scratch):
    total = sum(
        lax.dot_general(part, spread, (((1,), (1,)), ((), ())), preferred_element_type=F32)
        for part in split_two(fine)
    )
    scratch[0] = total[:, :128]
    scratch[1] = total[:, 128:]


def coarse_rows(scratch, k):
    even, odd = pl.ds(24 * k, 12, stride=2), pl.ds(24 * k + 1, 12, stride=2)
    halves = [scratch[t, even, :] + scratch[t, odd, :] for t in range(2)]
    return 0.125 * jnp.concatenate(halves, axis=1)


def first_kernel(
    new_in, old_in, near_in, map_in, rhs_in, coef_in,
    y_out, x_out, info, rhs_ref, coef_ref, new_ref, old_ref, near_ref, map_ref, sems,
):
    pairs = (
        (new_in, new_ref), (old_in, old_ref), (near_in, near_ref), (map_in, map_ref),
        (rhs_in, rhs_ref), (coef_in, coef_ref),
    )
    copies = [pltpu.make_async_copy(a, b, sems.at[i]) for i, (a, b) in enumerate(pairs)]
    for copy in copies:
        copy.start()
    curve = lax.axis_index("curve")
    group = lax.axis_index("group")
    up = lax.rem(curve, 2) == 1
    for copy in copies[:4]:
        copy.wait()
    new, old = new_ref[...], old_ref[...]

    def count(mask):
        return jnp.sum(jnp.where(mask, 1.0, 0.0)).astype(I32)

    new_first, held = count(new < curve), count(new == curve)
    old_first, old_count = count(old < curve), count(old == curve)
    last = jnp.clip(old_count - 1, 0, CAP_OLD - 1)
    x_slot, y_slot = jnp.where(up, last, 0), jnp.where(up, 0, last)
    for copy in copies[4:]:
        copy.wait()
    x_out[0] = rhs_ref[x_slot]
    x_out[1] = coef_ref[x_slot]
    y_out[0] = rhs_ref[y_slot]
    y_out[1] = coef_ref[y_slot]
    info[HELD] = held
    final = jnp.maximum(held - REACH, 0)
    info[SEND_X], info[SEND_Y] = jnp.where(up, final, 0), jnp.where(up, 0, final)
    info[AT_X] = jnp.where(up, REACH + CAP_NEW, 0)
    info[AT_Y] = jnp.where(up, 0, REACH + CAP_NEW)
    for i in range(4 * REACH):
        info[FACING + i] = -1
    x_at = jnp.where(up, REACH + CAP_NEW, 0)
    from_next, from_previous = jnp.where(up, 0, CAP_OLD + 1), jnp.where(up, CAP_OLD + 1, 0)
    first_id = group * NBG + new_first
    finish = first_id + held
    for k in range(CAP_NEW):
        block = new_first + k
        pick = jnp.where(block >= old_first + old_count, from_next, 1 + block - old_first)
        pick = jnp.where(block < old_first, from_previous, pick)
        info[PICK + k] = jnp.clip(pick, 0, CAP_OLD + 1)
        occupied = k < held
        safe = jnp.clip(block, 0, NBG - 1)
        cell = map_ref[0, safe]
        info[CELL + k] = jnp.where(occupied, cell, -1)
        for f in range(4):
            near = near_ref[f, safe]
            present = occupied & (near >= 0)
            slot = jnp.where(near >= finish, REACH + CAP_NEW - finish, REACH - first_id) + near
            slot = jnp.clip(slot, 0, ABSENT - 1)
            info[TABLE + 4 * k + f] = jnp.where(present, slot, ABSENT)
            local = near - group * NBG
            inside = present & (local >= 0) & (local < NBG)
            other = map_ref[0, jnp.clip(local, 0, NBG - 1)]
            info[BAND + 4 * k + f] = jnp.where(inside, 8 * k + 3 + other - cell, -1)
            info[BESIDE + 4 * k + f] = jnp.where(inside, other, -1)
            outside = present & jnp.logical_not(inside)
            place = jnp.clip(slot - x_at, 0, REACH - 1)
            info[OTHER + 4 * k + f] = jnp.where(outside, place, REACH)
            info[jnp.where(outside, FACING + 4 * place + OPPOSITE[f], SPARE)] = cell


def place_kernel(info, rhs_ref, coef_ref, source, coef):
    source[...] = jnp.zeros(source.shape, F32)
    coef[...] = jnp.ones(coef.shape, F32)
    for k in range(CAP_NEW):
        slot = jnp.clip(info[PICK + k] - 1, 0, CAP_OLD - 1)
        occupied = k < info[HELD]
        source[k, :, 0:576] = jnp.where(occupied, rhs_ref[slot], 0.0)
        coef[k, :, 0:576] = jnp.where(occupied, coef_ref[slot], 1.0)


def patched(info, field, i, k, x_in, y_in):
    pick = info[PICK + k]
    occupied = k < info[HELD]
    block = jnp.where(occupied & (pick == 0), x_in[i], field[k, :, 0:576])
    return jnp.where(occupied & (pick == CAP_OLD + 1), y_in[i], block)


def collect_kernel(info, kept, y_in, x_in, coef, faces, x_out, y_out):
    coef[...] = kept[...]
    for k in range(CAP_NEW):
        coef[k, :, 0:576] = patched(info, kept, 1, k, x_in, y_in)
        pack_faces(FINE, coef[k], faces, k, 0)
    send_faces(info, faces, x_out, y_out)


def level_kernel(info, kept, y_in, x_in, coef, source, level, faces, spread, scratch):
    source[...] = kept[...]
    for k in range(CAP_NEW):
        source[k, :, 0:576] = patched(info, kept, 0, k, x_in, y_in)
    spread[...] = spread_matrix()
    coarsen_blocks(coef[...].reshape(CAP_NEW * 24, FINE.width), spread[...], scratch)
    row, lane = iota((16, 256), 0), iota((16, 256), 1)
    for k in range(CAP_NEW):
        level[k] = jnp.ones((16, 256), F32)
        level[k, 0:12, :] = coarse_rows(scratch, k)
        level[k] = jnp.where((row < 12) & (lane < 144), level[k], 1.0)
        pack_faces(COARSE, level[k], faces, k, 0)


def start_kernel(
    info, source, coef, faces_in, coarse_faces, x_in, y_in, u, faces, x_out, y_out, table
):
    fill_table(info, table, x_in, faces_in, y_in)
    for k in range(CAP_NEW):
        ghosts = ghosts_of(FINE, info, table, k, 0)
        _, _, weight, _, _ = conductances(FINE, coef[k], ghosts)
        start = weight * source[k]
        u[k] = start
        pack_faces(FINE, start, faces, k, 0)
    faces[:, FINE.face_rows : BOTH_ROWS, :] = coarse_faces[...]
    send_faces(info, faces, x_out, y_out)


def conduct_kernel(info, coef, faces_in, x_in, y_in, fine_g, fine_d, table):
    fill_table(info, table, x_in, faces_in, y_in)
    for k in range(CAP_NEW):
        ghosts = ghosts_of(FINE, info, table, k, 0)
        _, g, _, diagonal, _ = conductances(FINE, coef[k], ghosts)
        for i in range(6):
            fine_g[k, i] = g[i]
        fine_d[k] = (1.0 / OMEGA) * diagonal


def coarse_conduct_kernel(
    info, level, faces_in, x_in, y_in, coarse_g, coarse_w, coarse_d, alpha, g_faces, row_out, table
):
    fill_table(info, table, x_in, faces_in, y_in)
    lane_row = iota((1, 128), 1)
    band = jnp.zeros((1, 128), F32)
    for k in range(CAP_NEW):
        ghosts = ghosts_of(COARSE, info, table, k, FINE.face_rows)
        q, g, weight, diagonal, masks = conductances(COARSE, level[k], ghosts)
        row, lane, depth, inside, high_y = masks
        for i in range(6):
            coarse_g[k, i] = g[i]
        coarse_w[k] = weight
        one = g[0] + g[1]
        one += jnp.where(lane < 12, 0.0, g[2]) + jnp.where(high_y, 0.0, g[3])
        one += jnp.where(row == 0, 0.0, g[4]) + jnp.where(row == 11, 0.0, g[5])
        alpha[k] = jnp.where(inside, KEEP + one, 0.0)
        pack_fields(COARSE, g[2], g[4], g_faces, k, 0, g[3], g[5])
        low_y = jnp.where(lane < 12, g[2], 0.0)
        x_edge = jnp.where(lane >= 132, g[3], low_y)
        y_edge = jnp.where(row == 0, g[4], jnp.where(row == 11, g[5], 0.0))
        pack_fields(COARSE, y_edge, x_edge, g_faces, k, 16)
        coarse_d[k] = (1.0 / OMEGA) * diagonal
        face = [
            both_totals(jnp.where(inside & (row == 0), q[4], 0.0)),
            both_totals(jnp.where(inside & (row == 11), q[5], 0.0)),
            both_totals(jnp.where(inside & (lane < 12), q[2], 0.0)),
            both_totals(jnp.where(inside & high_y, q[3], 0.0)),
        ]
        ends = jnp.where(inside & (depth == 0), q[0], 0.0)
        ends += jnp.where(inside & (depth == 11), q[1], 0.0)
        surface = face[0] + face[1] + face[2] + face[3] + both_totals(ends)
        occupied = k < info[HELD]
        band += jnp.where((lane_row == 8 * k + 3) & occupied, surface, 0.0)
        for f in range(4):
            band -= jnp.where(lane_row == info[BAND + 4 * k + f], face[f], 0.0)
        band += jnp.where(lane_row == 64 + k, info[CELL + k].astype(F32), 0.0)
    row_out[...] = band


def sweep_kernel(info, u_in, g, start, faces_in, x_in, y_in, u, faces, x_out, y_out, table):
    fill_table(info, table, x_in, faces_in, y_in)
    for k in range(CAP_NEW):
        field = u_in[k]
        ghosts = ghosts_of(COARSE, info, table, k, 0)
        new = KEEP * field + (start[k] + neighbour_sum(COARSE, field, g.at[k], ghosts))
        u[k] = new
        pack_faces(COARSE, new, faces, k, 0)
    send_faces(info, faces, x_out, y_out)


def finish_kernel(info, part, g, faces_in, x_in, y_in, u, faces, x_out, y_out, table):
    fill_table(info, table, x_in, faces_in, y_in)
    for k in range(CAP_NEW):
        u[k] = part[k]
        add_ghosts(FINE, u.at[k], g.at[k], ghosts_of(FINE, info, table, k, 0))
        pack_faces(FINE, u[k], faces, k, 0)
    send_faces(info, faces, x_out, y_out)


def residual_kernel(
    info, u_in, part, g, diagonal, weight, spread, g_faces, faces_in, x_in, y_in,
    coarse_s, faces, x_out, y_out, table, rest, scratch,
):
    fill_table(info, table, x_in, faces_in, y_in)
    for k in range(CAP_NEW):
        rest[k] = part[k]
        add_ghosts(FINE, rest.at[k], g.at[k], ghosts_of(FINE, info, table, k, 0))
        rest[k] = diagonal[k] * (rest[k] - u_in[k])
    coarsen_blocks(rest[...].reshape(CAP_NEW * 24, FINE.width), spread[...], scratch)
    for k in range(CAP_NEW):
        coarse_s[k] = jnp.zeros((16, 256), F32)
        coarse_s[k, 0:12, :] = weight[k, 0:12, :] * coarse_rows(scratch, k)
        pack_faces(COARSE, coarse_s[k], faces, k, 0)
    x_first, y_first = info[SEND_X], info[SEND_Y]
    for j in range(REACH):
        x_out[j, 0:16] = faces[x_first + j]
        x_out[j, 16:48] = g_faces[x_first + j]
        y_out[j] = faces[y_first + j]


def total_kernel(
    info, u_in, g, start, diagonal, row_in, faces_in, x_in, y_in, rows_out, swept, table
):
    fill_table(info, table, x_in, faces_in, y_in)
    lane_row = iota((1, 128), 1)
    row, lane = iota((16, 256), 0), iota((16, 256), 1)
    inside = (row < 12) & (lane < 144)
    band = row_in[...]
    for k in range(CAP_NEW):
        field = u_in[k]
        ghosts = ghosts_of(COARSE, info, table, k, 0)
        inner = start[k] + neighbour_sum(COARSE, field, g.at[k], ghosts)
        swept[k] = KEEP * field + inner
        rest = jnp.where(inside, diagonal[k] * (inner - OMEGA * field), 0.0)
        occupied = k < info[HELD]
        band += jnp.where((lane_row == 8 * k + 7) & occupied, both_totals(rest), 0.0)
    rows_out[...] = jnp.broadcast_to(band, rows_out.shape)


def lifted(answer, cell):
    at = iota((NCOARSE, 128), 0)
    return jnp.sum(jnp.where(at == cell, answer, 0.0), axis=0, keepdims=True)


def wide(line):
    return jnp.concatenate([line, line], axis=1)


def surface_lift(g, lift):
    row, lane = iota((16, 256), 0), iota((16, 256), 1)
    total = jnp.where(row == 0, g[4] * lift[0], 0.0)
    total += jnp.where(row == 11, g[5] * lift[1], 0.0)
    total += jnp.where(lane < 12, g[2] * lift[2], 0.0)
    return total + jnp.where((lane >= 132) & (lane < 144), g[3] * lift[3], 0.0)


def solve_kernel(
    info, rows_in, swept, g, alpha, u, answer_out, faces, x_out
):
    rows = rows_in[...]
    shape = (NCOARSE, 128)
    row, lane = iota(shape, 0), iota(shape, 1)
    cells = iota((NCOARSE, NCOARSE), 1).astype(F32)
    member = jnp.concatenate(
        [(rows[:, 64 + k : 65 + k] == cells).astype(F32) for k in range(CAP_NEW)], axis=0
    ).astype(jnp.bfloat16)
    shifts = [rows] + [pltpu.roll(rows, 128 - 8 * k, 1) for k in range(1, CAP_NEW)]
    band = sum(
        lax.dot_general(member, part, (((0,), (0,)), ((), ())), preferred_element_type=F32)
        for part in split_three(jnp.concatenate(shifts, axis=0))
    )
    matrix = jnp.where(lane == 64, band[:, 7:8], 0.0)
    for o in range(7):
        matrix += jnp.where(lane == row + (o - REACH), band[:, o : o + 1], 0.0)

    lists = [[i for i in (t, 9 + t, 18 + t, 27 + t) if i < NCOARSE] for t in range(6)]
    lists += [[6 + t, 24 + t] for t in range(REACH)] + [[15 + t] for t in range(REACH)]
    for pivots in lists:
        drop = None
        for j in pivots:
            column = jnp.broadcast_to(matrix[:, j : j + 1], shape)
            scaled = matrix[j : j + 1, :] / column[j : j + 1, :]
            one = jnp.where(row == j, 0.0, column) * scaled
            drop = one if drop is None else drop + one
        matrix = matrix - drop
    pivots = jnp.sum(jnp.where(lane == row, matrix, 0.0), axis=1, keepdims=True)
    answer = jnp.broadcast_to(matrix[:, 64:65], shape) / jnp.broadcast_to(pivots, shape)
    answer_out[...] = answer
    for k in range(CAP_NEW):
        lift = lifted(answer, info[CELL + k])
        beside = [wide(lifted(answer, info[BESIDE + 4 * k + f])) for f in range(4)]
        new = swept[k] + wide(lift) * alpha[k] + surface_lift(g.at[k], beside)
        u[k] = new
        pack_faces(COARSE, new, faces, k, 0)
        faces[k, LIFT_ROW : LIFT_ROW + 1, 64:128] = lift[:, 64:128]
    for j in range(REACH):
        x_out[j] = faces[info[SEND_X] + j]


def across_kernel(
    info, u_in, g, answer_in, x_in, g_in, u, faces, ghosts, y_out, table
):
    table[0:REACH] = x_in[...]
    table[REACH] = jnp.zeros((16, 128), F32)
    answer = answer_in[...]
    upper = iota((1, 128), 1) >= 64
    for k in range(CAP_NEW):
        lift = [table[info[OTHER + 4 * k + f], pl.ds(LIFT_ROW, 1), :] for f in range(4)]
        lift = [wide(jnp.where(upper, line, pltpu.roll(line, 64, 1))) for line in lift]
        new = u_in[k] + surface_lift(g.at[k], lift)
        u[k] = new
        pack_faces(COARSE, new, faces, k, 0)
    row, lane = iota((16, 128), 0), iota((16, 128), 1)
    for j in range(REACH):
        lift = [lifted(answer, info[FACING + 4 * j + f]) for f in range(4)]
        face = jnp.where(lane < 64, lift[2], lift[3])
        face = jnp.where(row >= 14, lift[1], jnp.where(row >= 12, lift[0], face))
        edge = jnp.where(row == 0, lift[0], jnp.where(row == 11, lift[1], 0.0))
        edge = jnp.where((row == 12) | (row == 14), lift[2], edge)
        edge = jnp.where((row == 13) | (row == 15), lift[3], edge)
        ghosts[j] = x_in[j] + face * g_in[j, 16:32] + edge * g_in[j, 32:48]
        y_out[j] = faces[info[SEND_Y] + j]


def refine_kernel(
    info, e_in, g, start, faces_in, x_in, y_in, u_in, spread, u, faces, x_out, y_out, table, coarse, rest
):
    fill_table(info, table, x_in, faces_in, y_in)
    for k in range(CAP_NEW):
        field = e_in[k]
        ghosts = ghosts_of(COARSE, info, table, k, 0)
        coarse[k] = KEEP * field + (start[k] + neighbour_sum(COARSE, field, g.at[k], ghosts))
    total = sum(
        jnp.dot(part, spread[...], preferred_element_type=F32)
        for part in split_two(coarse[...].reshape(CAP_NEW * 16, 256))
    )
    for k in range(CAP_NEW):
        twelve = total[16 * k : 16 * k + 12, :]
        for t in range(FINE.tiles):
            part = slice(128 * t, 128 * t + 128)
            rest[t, pl.ds(0, 12, stride=2), :] = twelve[:, part]
            rest[t, pl.ds(1, 12, stride=2), :] = twelve[:, part]
        new = u_in[k] + jnp.concatenate([rest[t] for t in range(FINE.tiles)], axis=1)
        u[k] = new
        pack_faces(FINE, new, faces, k, 0)
    send_faces(info, faces, x_out, y_out)


def last_kernel(info, part, g, faces_in, x_in, y_in, out, table, u, block, sems):
    fill_table(info, table, x_in, faces_in, y_in)
    copies = [
        pltpu.make_async_copy(block.at[k], out.at[k], sems.at[k]) for k in range(CAP_NEW)
    ]
    for k in range(CAP_NEW):
        u[...] = part[k]
        add_ghosts(FINE, u, g.at[k], ghosts_of(FINE, info, table, k, 0))
        block[k] = jnp.where(k < info[HELD], u[:, 0:576], 0.0)
        copies[k].start()
    for copy in copies:
        copy.wait()


def sds(*shape):
    return jax.ShapeDtypeStruct(shape, F32)


SMEM = pl.BlockSpec(memory_space=pltpu.SMEM)
VMEM = pl.BlockSpec(memory_space=pltpu.VMEM)
HBM = pl.BlockSpec(memory_space=pltpu.HBM)


def call(kernel, name, outs, scratch, args, in_specs=None, out_specs=None):
    many = len(outs) > 1
    return pl.pallas_call(
        kernel,
        out_shape=outs if many else outs[0],
        in_specs=in_specs or [SMEM] + [VMEM] * (len(args) - 1),
        out_specs=out_specs or ([VMEM] * len(outs) if many else VMEM),
        scratch_shapes=[pltpu.VMEM(s, F32) if isinstance(s, tuple) else s for s in scratch],
        cost_estimate=pl.CostEstimate(flops=10_000_000, bytes_accessed=4_000_000, transcendentals=0),
        compiler_params=pltpu.CompilerParams(vmem_limit_bytes=24 * 1024 * 1024),
        name=name,
    )(*args)


def swap(block, axis, first):
    starts = range(first, lax.axis_size(axis) - 1, 2)
    return lax.ppermute(block, axis, [(i, i + 1) for i in starts] + [(i + 1, i) for i in starts])


def exchange(x_out, y_out):
    x_in = swap(x_out, AXES, 1)
    return x_in, swap(y_out, AXES, 0)


def face_outs(rows):
    return [sds(CAP_NEW, rows, 128), sds(REACH, rows, 128), sds(REACH, rows, 128)]


def body(rhs_old, coef_old, old_owner, new_owner, neighbours, coarse_map):
    near = jnp.transpose(neighbours[0])
    rhs_old, coef_old, new_owner, old_owner, near, coarse_map = (
        pltpu.with_memory_space_constraint(a, pltpu.HBM)
        for a in (rhs_old, coef_old, new_owner, old_owner, near, coarse_map)
    )
    pair, old = sds(2, 24, 576), sds(CAP_OLD, 24, 576)
    y_out, x_out, info, rhs_old, coef_old = call(
        first_kernel, "owners",
        [pair, pair, jax.ShapeDtypeStruct((128,), I32), old, old],
        [
            pltpu.VMEM((1, 128), I32), pltpu.VMEM((1, 128), I32),
            pltpu.SMEM((4, 128), I32), pltpu.SMEM((1, 128), I32),
            pltpu.SemaphoreType.DMA((6,)),
        ],
        (new_owner, old_owner, near, coarse_map, rhs_old, coef_old),
        [HBM] * 6, [VMEM, VMEM, SMEM, VMEM, VMEM],
    )
    y_in, x_in = swap(y_out, "curve", 0), swap(x_out, "curve", 1)

    fine = sds(CAP_NEW, 24, FINE.width)
    coarse = sds(CAP_NEW, 16, 256)
    fine_table = [(ABSENT + 1, FINE.face_rows, 128)]
    coarse_table = [(ABSENT + 1, COARSE.face_rows, 128)]
    fine_faces, coarse_faces = face_outs(FINE.face_rows), face_outs(COARSE.face_rows)
    sums = (2, CAP_NEW * 24, 128)

    source, coef = call(place_kernel, "place", [fine, fine], [], (info, rhs_old, coef_old))
    coef, faces, x_out, y_out = call(
        collect_kernel, "collect", [fine] + fine_faces, [], (info, coef, y_in, x_in)
    )
    source, level, coarse_own, spread = call(
        level_kernel, "level",
        [fine, coarse, coarse_faces[0], jax.ShapeDtypeStruct((256, FINE.width), jnp.bfloat16)],
        [sums],
        (info, source, y_in, x_in, coef),
    )
    x_in, y_in = exchange(x_out, y_out)
    u, new_faces, x_out, y_out = call(
        start_kernel, "start", [fine] + face_outs(BOTH_ROWS), fine_table,
        (info, source, coef, faces, coarse_own, x_in, y_in),
    )
    fine_s = u
    fine_g, fine_d = call(
        conduct_kernel, "conduct", [sds(CAP_NEW, 6, 24, FINE.width), fine], fine_table,
        (info, coef, faces, x_in, y_in),
    )
    faces = new_faces
    x_in, y_in = exchange(x_out, y_out)
    coarse_g, coarse_w, coarse_d, alpha, g_faces, row = call(
        coarse_conduct_kernel, "coarse_conduct",
        [sds(CAP_NEW, 6, 16, 256), coarse, coarse, coarse, sds(CAP_NEW, 32, 128), sds(1, 128)],
        [(ABSENT + 1, BOTH_ROWS, 128)],
        (info, level, faces, x_in, y_in),
    )

    def inner(u, name):
        return call(inner_kernel, name, [fine], [], (u, fine_g, fine_s), [VMEM] * 3)

    part = inner(u, "pre_inner")
    u0, faces, x_out, y_out = call(
        finish_kernel, "pre", [fine, *fine_faces], [(ABSENT + 1, BOTH_ROWS, 128)],
        (info, part, fine_g, faces, x_in, y_in),
    )
    x_in, y_in = exchange(x_out, y_out)
    part = inner(u0, "residual_inner")
    coarse_s, faces, x_out, y_out = call(
        residual_kernel, "residual",
        [coarse, coarse_faces[0], sds(REACH, 48, 128), coarse_faces[2]],
        fine_table + [(CAP_NEW, 24, FINE.width), sums],
        (info, u0, part, fine_g, fine_d, coarse_w, spread, g_faces, faces, x_in, y_in),
    )
    g_in, y_in = exchange(x_out, y_out)
    e, faces, x_out, y_out = call(
        sweep_kernel, "coarse_pre", [coarse, *coarse_faces],
        coarse_table, (info, coarse_s, coarse_g, coarse_s, faces, g_in, y_in),
    )
    x_in, y_in = exchange(x_out, y_out)
    rows, swept = call(
        total_kernel, "totals", [sds(NCOARSE, 128), coarse], coarse_table,
        (info, e, coarse_g, coarse_s, coarse_d, row, faces, x_in, y_in),
    )
    rows = lax.all_to_all(rows, "curve", 0, 0, tiled=True)
    e, answer, faces, x_out = call(
        solve_kernel, "solve", [coarse, sds(NCOARSE, 128), *coarse_faces[:2]], [],
        (info, rows, swept, coarse_g, alpha),
    )
    x_in = swap(x_out, AXES, 1)
    e, faces, x_in, y_out = call(
        across_kernel, "across", [coarse, *coarse_faces], [(REACH + 1, 16, 128)],
        (info, e, coarse_g, answer, x_in, g_in),
    )
    y_in = swap(y_out, AXES, 0)
    u, faces, x_out, y_out = call(
        refine_kernel, "refine", [fine, *fine_faces],
        coarse_table + [(CAP_NEW, 16, 256), (FINE.tiles, 24, 128)],
        (info, e, coarse_g, coarse_s, faces, x_in, y_in, u0, spread),
    )
    x_in, y_in = exchange(x_out, y_out)
    part = inner(u, "post_inner")
    u, faces, x_out, y_out = call(
        finish_kernel, "post", [fine, *fine_faces], fine_table,
        (info, part, fine_g, faces, x_in, y_in),
    )
    x_in, y_in = exchange(x_out, y_out)
    part = inner(u, "last_inner")
    return call(
        last_kernel, "last", [sds(CAP_NEW, 24, 576)],
        fine_table
        + [(24, FINE.width), (CAP_NEW, 24, 576), pltpu.SemaphoreType.DMA((CAP_NEW,))],
        (info, part, fine_g, faces, x_in, y_in), None, pl.BlockSpec(memory_space=pl.ANY),
    )


def solution(mesh):
    in_specs = (
        P(("group", "curve"), None, None),
        P(("group", "curve"), None, None),
        P("group", None),
        P("group", None),
        P("group", None, None),
        P("group", None),
    )
    out_specs = P(("group", "curve"), None, None)
    return jax.shard_map(body, mesh=mesh, in_specs=in_specs, out_specs=out_specs, check_vma=False)
```
